32 devices in a mesh: dp: 8 (over y, x, core), mp: 4 (over z).
Axes of the slice: x: 2, y: 2, z: 4, core: 2. Of those that a mesh axis runs over, the one named last changes fastest.
Arguments:
- users_list: int32 [32, 256], P(('dp', 'mp')), may hold values from 0 to 1023, as said below
- items_list: int32 [32, 256], P(('dp', 'mp')), may hold values from 0 to 1023, as said below
- days_list: int32 [32, 32], P(('dp', 'mp')), may hold values from 0 to 255, as said below
- status: int32 [32, 32, 256, 256], P(('dp', 'mp')), may hold values from 0 to 2
- user_factor: float32 [1024, 256], P('dp', 'mp'), may hold values from -2.4 to 2.4
- user_first: float32 [1024, 256], P('dp', 'mp'), may hold values from -6 to 6
- user_second: float32 [1024, 256], P('dp', 'mp'), may hold values from 0.05 to 2
- item_factor: float32 [1024, 256], P('dp', 'mp'), may hold values from -2.4 to 2.4
- item_first: float32 [1024, 256], P('dp', 'mp'), may hold values from -6 to 6
- item_second: float32 [1024, 256], P('dp', 'mp'), may hold values from 0.05 to 2
- day_factor: float32 [256, 256], P('dp', 'mp'), may hold values from -2.4 to 2.4
- day_first: float32 [256, 256], P('dp', 'mp'), may hold values from -6 to 6
- day_second: float32 [256, 256], P('dp', 'mp'), may hold values from 1 to 3000
Outputs:
- new_user_factor: float32 [1024, 256], P('dp', 'mp')
- new_user_first: float32 [1024, 256], P('dp', 'mp')
- new_user_second: float32 [1024, 256], P('dp', 'mp')
- new_item_factor: float32 [1024, 256], P('dp', 'mp')
- new_item_first: float32 [1024, 256], P('dp', 'mp')
- new_item_second: float32 [1024, 256], P('dp', 'mp')
- new_day_factor: float32 [256, 256], P('dp', 'mp')
- new_day_first: float32 [256, 256], P('dp', 'mp')
- new_day_second: float32 [256, 256], P('dp', 'mp')
The draws below stay inside these ranges and needn't reach their ends.
Inputs may be any that keep to these rules, and one draw needn't show every extreme that they name: `users_list`: the 256 users of a block are distinct; at most 48 of them lie in the rows n * 128 to (n + 1) * 128 - 1 of one index n of dp, and one such index holds exactly 48 users of every block. `items_list`: the 256 items of a block are distinct; at most 48 of them lie in the rows n * 128 to (n + 1) * 128 - 1 of one index n of dp, and one such index holds exactly 48 items of every block. `days_list`: the 32 days of a block are distinct; at most 8 of them lie in the rows n * 32 to (n + 1) * 32 - 1 of one index n of dp, and one such index holds exactly 8 days of every block.
All inputs are finite; a program needn't handle non-finite values.
Results may differ from the reference program's by a relative error of at most 0.0044.
Values may be sent and summed in bfloat16 or wider, within the bound.
No kernel may reach another device: no remote copies, remote signals or barrier semaphores. Data moves between devices by JAX's collectives and lax.ppermute only.
A program may use at most 64 MiB of HBM per device.

```python
import math
import jax
import jax.numpy as jnp
from jax import lax

R = 256
BU = 256
BI = 256
BD = 32
UO = 128
IO = 128
DAYS_OWN = 32
BLOCKS = 32
NU = 1024
NI = 1024
ND = 256
CAP_U = 48
CAP_I = 48
CAP_D = 8


def block_rows(base_key, blocks, row_count, locally_kept_lines, line_bundles, place_limit):
    subkeys = jax.random.split(base_key, 4)
    hot_owner = jax.random.randint(subkeys[0], (1, 1), 0, line_bundles)
    spare_slots = (line_bundles - 1) * place_limit
    ordering = jax.vmap(lambda subkey: jax.random.permutation(subkey, spare_slots))(jax.random.split(subkeys[1], blocks))
    chosen = ordering[:, :row_count - place_limit]
    owners = jnp.concatenate([jnp.broadcast_to(hot_owner, (blocks, place_limit)), (hot_owner + 1 + chosen // place_limit) % line_bundles], axis=1)
    slot_numbers = jnp.concatenate([jnp.broadcast_to(jnp.arange(place_limit)[None, :], (blocks, place_limit)), chosen % place_limit], axis=1)
    row_picks = jax.vmap(lambda subkey: jax.random.permutation(subkey, locally_kept_lines)[:place_limit])(jax.random.split(subkeys[2], blocks * line_bundles))
    row_picks = row_picks.reshape(blocks, line_bundles * place_limit)
    local_rows = jnp.take_along_axis(row_picks, owners * place_limit + slot_numbers, axis=1)
    global_rows = owners * locally_kept_lines + local_rows
    shuffle = jax.vmap(lambda subkey: jax.random.permutation(subkey, row_count))(jax.random.split(subkeys[3], blocks))
    return jnp.take_along_axis(global_rows, shuffle, axis=1).astype(jnp.int32)


def draw_users_list(key, part):
    return block_rows(jax.random.fold_in(key, 11), BLOCKS, BU, UO, NU // UO, CAP_U)


def draw_items_list(key, part):
    return block_rows(jax.random.fold_in(key, 22), BLOCKS, BI, IO, NI // IO, CAP_I)


def draw_days_list(key, part):
    return block_rows(jax.random.fold_in(key, 33), BLOCKS, BD, DAYS_OWN, ND // DAYS_OWN, CAP_D)


def place_ends(array, rng, low, high):
    index_at = [jax.random.randint(jax.random.fold_in(rng, axis), (), 0, length) for axis, length in enumerate(array.shape)]
    longest = array.shape.index(max(array.shape))
    next_to = index_at[:longest] + [(index_at[longest] + 1) % array.shape[longest]] + index_at[longest + 1:]
    return array.at[tuple(index_at)].set(low).at[tuple(next_to)].set(high)


def levels(key, extent, cuts, least, top_value):
    level = 1.0
    for dim, parts in cuts:
        steps = jax.random.uniform(jax.random.fold_in(jax.random.fold_in(key, 6), dim), (parts,), jnp.float32, least / len(cuts), top_value / len(cuts))
        level = level * jnp.repeat(jnp.exp(steps), extent[dim] // parts).reshape((-1,) + (1,) * (len(extent) - 1 - dim))
    return level


def normal_values(stream_key, dims, spread, limit, pieces=(), held_as=jnp.bfloat16):
    factor_of = levels(stream_key, dims, pieces, -0.22, 0.18) if pieces else 1.0
    result = jax.random.normal(stream_key, dims, jnp.float32) * spread * factor_of
    return jnp.minimum(jnp.maximum(result, -limit), limit).astype(held_as)


def setup_inputs(seed: int = 0) -> dict:
    splits = jax.random.split(jax.random.key(seed), 14)
    users_list = draw_users_list(jax.random.fold_in(splits[13], 71), 0)
    items_list = draw_items_list(jax.random.fold_in(splits[13], 71), 0)
    days_list = draw_days_list(jax.random.fold_in(splits[13], 71), 0)
    status = place_ends(jax.random.randint(splits[3], (BLOCKS, BD, BU, BI), 0, 3), jax.random.fold_in(splits[3], 1), 0, 2).astype(jnp.int32)
    user_factor = normal_values(splits[4], (NU, R), 0.4, 2.4, ((0, 8), (1, 4)), jnp.float32)
    user_first = normal_values(splits[5], (NU, R), 1.0, 6.0, ((0, 8), (1, 4)), jnp.float32)
    user_second = jnp.clip(jnp.exp(math.log(2.0) - 3.6888794 * jax.random.uniform(splits[6], (NU, R), jnp.float32) ** levels(splits[6], (NU, R), ((0, 8), (1, 4)), -0.2, 0.2)), 0.05, 2.0)
    item_factor = normal_values(splits[7], (NI, R), 0.4, 2.4, ((0, 8), (1, 4)), jnp.float32)
    item_first = normal_values(splits[8], (NI, R), 1.0, 6.0, ((0, 8), (1, 4)), jnp.float32)
    item_second = jnp.clip(jnp.exp(math.log(2.0) - 3.6888794 * jax.random.uniform(splits[9], (NI, R), jnp.float32) ** levels(splits[9], (NI, R), ((0, 8), (1, 4)), -0.2, 0.2)), 0.05, 2.0)
    day_factor = normal_values(splits[10], (ND, R), 0.4, 2.4, ((0, 8), (1, 4)), jnp.float32)
    day_first = normal_values(splits[11], (ND, R), 1.0, 6.0, ((0, 8), (1, 4)), jnp.float32)
    day_second = jnp.clip(jnp.exp(math.log(3000.0) - 8.006368 * jax.random.uniform(splits[12], (ND, R), jnp.float32) ** levels(splits[12], (ND, R), ((0, 8), (1, 4)), -0.2, 0.2)), 1.0, 3000.0)
    return {"users_list": users_list, "items_list": items_list, "days_list": days_list, "status": status, "user_factor": user_factor, "user_first": user_first, "user_second": user_second, "item_factor": item_factor, "item_first": item_first, "item_second": item_second, "day_factor": day_factor, "day_first": day_first, "day_second": day_second}


beta_one = 0.9
beta_two = 0.99
bias_one = 1.0 - 0.9 ** 10
bias_two = 1.0 - 0.99 ** 10
learn_rate = 0.01
epsilon = 1e-08
loss_scale = 0.0625
zero_weight = 2.0

def block_grads(user_row_values, item_row_values, day_row_values, block_status):
    day_count = day_row_values.shape[0]
    user_count = user_row_values.shape[0]
    scaled = day_row_values[:, None, :] * user_row_values[None, :, :]
    scaled_flat = scaled.reshape(day_count * user_count, -1)
    scaled_wide = scaled_flat.astype(jnp.float32)
    items_wide = item_row_values.astype(jnp.float32)
    logits = jnp.einsum('nr,ir->ni', scaled_wide, items_wide)
    chance = jax.nn.sigmoid(logits)
    status_flat = block_status.reshape(day_count * user_count, -1)
    residual = loss_scale * (jnp.where(status_flat == 1, chance - 1.0, 0.0) + jnp.where(status_flat == 2, zero_weight * chance, 0.0))
    residual = residual.astype(jnp.bfloat16)
    residual_wide = residual.astype(jnp.float32)
    projected = jnp.einsum('ni,ir->nr', residual_wide, items_wide).reshape(day_count, user_count, -1)
    user_gradient = lax.optimization_barrier(jnp.sum(projected * day_row_values[:, None, :].astype(jnp.float32), axis=0))
    day_gradient = lax.optimization_barrier(jnp.sum(projected * user_row_values[None, :, :].astype(jnp.float32), axis=1))
    item_gradient = jnp.einsum('ni,nr->ir', residual_wide, scaled_wide)
    return (user_gradient, item_gradient, day_gradient)

def adam_update(factor, first, second, gradient):
    first_new = beta_one * first + (1.0 - beta_one) * gradient
    second_new = beta_two * second + (1.0 - beta_two) * gradient * gradient
    change = learn_rate * (first_new / bias_one) / (jnp.sqrt(second_new / bias_two) + epsilon)
    return (factor - change, first_new, second_new)

def reference(users_list, items_list, days_list, status, user_factor, user_first, user_second, item_factor, item_first, item_second, day_factor, day_first, day_second):
    user_row_values = user_factor.astype(jnp.bfloat16)
    item_row_values = item_factor.astype(jnp.bfloat16)
    day_row_values = day_factor.astype(jnp.bfloat16)

    def one_block(carry, inputs):
        user_gradient_sum, item_gradient_sum, day_gradient_sum = carry
        user_index, item_index, day_index, block_status = inputs
        user_gradient, item_gradient, day_gradient = block_grads(user_row_values[user_index], item_row_values[item_index], day_row_values[day_index], block_status)
        return ((user_gradient_sum.at[user_index].add(user_gradient), item_gradient_sum.at[item_index].add(item_gradient), day_gradient_sum.at[day_index].add(day_gradient)), None)
    initial = (jnp.zeros(user_factor.shape, jnp.float32), jnp.zeros(item_factor.shape, jnp.float32), jnp.zeros(day_factor.shape, jnp.float32))
    totals, _ = lax.scan(one_block, initial, (users_list, items_list, days_list, status))
    user_gradient_sum, item_gradient_sum, day_gradient_sum = totals
    new_user_factor, new_user_first, new_user_second = adam_update(user_factor, user_first, user_second, user_gradient_sum)
    new_item_factor, new_item_first, new_item_second = adam_update(item_factor, item_first, item_second, item_gradient_sum)
    new_day_factor, new_day_first, new_day_second = adam_update(day_factor, day_first, day_second, day_gradient_sum)
    return (new_user_factor, new_user_first, new_user_second, new_item_factor, new_item_first, new_item_second, new_day_factor, new_day_first, new_day_second)
```

```python
import functools

import jax
import jax.numpy as jnp
from jax import lax
from jax.experimental import pallas as pl
from jax.experimental.pallas import tpu as pltpu
from jax.sharding import PartitionSpec as P

beta_one = 0.9
beta_two = 0.99
bias_one = 1.0 - 0.9**10
bias_two = 1.0 - 0.99**10
learn_rate = 0.01
epsilon = 1e-08
loss_scale = 0.0625

LANES = 128
DAYS_PER_STEP = 4

f32 = jnp.float32
bf16 = jnp.bfloat16


class Packing:
    def __init__(self, row_counts, columns):
        self.columns = columns
        self.parts = LANES // columns
        self.row_counts = row_counts
        self.packed = tuple(rows // self.parts for rows in row_counts)
        padded = [-(-rows // 16) * 16 for rows in self.packed]
        self.padded = tuple(padded)
        self.starts = tuple(sum(padded[:t]) for t in range(len(padded)))
        self.height = sum(padded)


def pack_kernel(packing, user_ref, item_ref, day_ref, out_ref):
    for t, ref in enumerate((user_ref, item_ref, day_ref)):
        rows = packing.packed[t]
        parts = [ref[p * rows : (p + 1) * rows, :] for p in range(packing.parts)]
        if packing.padded[t] != rows:
            blank = jnp.zeros((packing.padded[t] - rows, packing.columns), f32)
            parts = [jnp.concatenate([part, blank], axis=0) for part in parts]
        wide = jnp.concatenate(parts, axis=1).astype(bf16)
        out_ref[packing.starts[t] : packing.starts[t] + packing.padded[t], :] = wide


def lane_spread(packing, holders):
    wide = holders * LANES
    narrow = holders * packing.columns
    lane = lax.broadcasted_iota(jnp.int32, (wide, narrow), 0)
    column = lax.broadcasted_iota(jnp.int32, (wide, narrow), 1)
    target = (lane // LANES) * packing.columns + lane % packing.columns
    return jnp.where(target == column, 1.0, 0.0).astype(bf16)


def lane_part(packing, rows, holders):
    lane = lax.broadcasted_iota(jnp.int32, (rows, holders * LANES), 1)
    return (lane % LANES) // packing.columns


def split_rows(packing, t, numbers):
    owner = numbers // packing.row_counts[t]
    local = numbers % packing.row_counts[t]
    return owner * packing.padded[t] + local % packing.packed[t], local // packing.packed[t]


def block_kernel(
    packing,
    owners,
    holders,
    days_per_step,
    user_row_ref,
    item_row_ref,
    day_row_ref,
    user_col_ref,
    item_col_ref,
    day_col_ref,
    table_ref,
    status_ref,
    out_ref,
    users,
    items,
    items_half_t,
    days,
    user_gradient,
    item_gradient,
    day_gradient,
):
    step = pl.program_id(0)
    user_count = users.shape[0]

    def pick(t, numbers):
        slots, part = split_rows(packing, t, numbers)
        rows = numbers.shape[0]
        depth = owners * packing.padded[t]
        selector = jnp.where(
            slots == lax.broadcasted_iota(jnp.int32, (rows, depth), 1), 1.0, 0.0
        ).astype(bf16)
        start = packing.starts[t]
        wide = jnp.concatenate(
            [
                jnp.dot(
                    selector,
                    table_ref[:, m, start : start + packing.padded[t], :].reshape(depth, LANES),
                    preferred_element_type=f32,
                )
                for m in range(holders)
            ],
            axis=1,
        )
        wide = jnp.where(lane_part(packing, rows, holders) == part, wide, 0.0).astype(bf16)
        return jnp.dot(wide, lane_spread(packing, holders), preferred_element_type=f32)

    @pl.when(step == 0)
    def _():
        users[...] = pick(0, user_col_ref[...])
        item_values = pick(1, item_col_ref[...])
        items[...] = item_values.astype(bf16)
        items_half_t[...] = (0.5 * item_values).T.astype(bf16)
        days[...] = pick(2, day_col_ref[...])
        user_gradient[...] = jnp.zeros_like(user_gradient)
        item_gradient[...] = jnp.zeros_like(item_gradient)

    for j in range(days_per_step):
        k = step * days_per_step + j
        day = days[pl.ds(k, 1), :]
        user_values = users[...]
        scaled = (day * user_values).astype(bf16)
        half_logits = jnp.dot(scaled, items_half_t[...], preferred_element_type=f32)
        state = status_ref[0, j]
        residual = (
            (0.5 * loss_scale)
            * state.astype(f32)
            * (jnp.tanh(half_logits) + jnp.where(state == 1, -1.0, 1.0))
        ).astype(bf16)
        projected = jnp.dot(residual, items[...], preferred_element_type=f32)
        user_gradient[...] += projected * day
        day_gradient[pl.ds(k, 1), :] = jnp.sum(projected * user_values, axis=0, keepdims=True)
        item_gradient[...] += lax.dot_general(
            residual, scaled, (((0,), (0,)), ((), ())), preferred_element_type=f32
        )

    def place(t, numbers, gradient):
        slots, part = split_rows(packing, t, numbers[1])
        _, part_col = split_rows(packing, t, numbers[0])
        count = gradient.shape[0]
        depth = owners * packing.padded[t]
        placer = jnp.where(
            lax.broadcasted_iota(jnp.int32, (depth, count), 0) == slots, 1.0, 0.0
        ).astype(bf16)
        wide = lax.dot_general(
            gradient.astype(bf16),
            lane_spread(packing, holders),
            (((1,), (1,)), ((), ())),
            preferred_element_type=f32,
        )
        wide = jnp.where(lane_part(packing, count, holders) == part_col, wide, 0.0).astype(bf16)
        placed = jnp.dot(placer, wide, preferred_element_type=f32)
        start = packing.starts[t]
        for m in range(holders):
            out_ref[:, m, start : start + packing.padded[t], :] = placed[
                :, m * LANES : (m + 1) * LANES
            ].reshape(owners, packing.padded[t], LANES)

    @pl.when(step == pl.num_programs(0) - 1)
    def _():
        place(0, (user_col_ref[...], user_row_ref[...]), user_gradient[...])
        place(1, (item_col_ref[...], item_row_ref[...]), item_gradient[...])
        place(2, (day_col_ref[...], day_row_ref[...]), day_gradient[...])


def adam_kernel(packing, gradient_ref, *refs):
    for t in range(3):
        factor, first, second = refs[3 * t : 3 * t + 3]
        new_factor, new_first, new_second = refs[9 + 3 * t : 12 + 3 * t]
        rows, columns = packing.packed[t], packing.columns
        start = packing.starts[t]
        wide = gradient_ref[start : start + packing.padded[t], :]
        gradient = jnp.concatenate(
            [wide[:rows, p * columns : (p + 1) * columns] for p in range(packing.parts)], axis=0
        )
        first_value = beta_one * first[...] + (1.0 - beta_one) * gradient
        second_value = beta_two * second[...] + (1.0 - beta_two) * gradient * gradient
        change = (
            learn_rate
            * (first_value / bias_one)
            / (jnp.sqrt(second_value / bias_two) + epsilon)
        )
        new_factor[...] = factor[...] - change
        new_first[...] = first_value
        new_second[...] = second_value


def local(
    users_list,
    items_list,
    days_list,
    status,
    user_factor,
    user_first,
    user_second,
    item_factor,
    item_first,
    item_second,
    day_factor,
    day_first,
    day_second,
):
    owners = lax.axis_size("dp")
    holders = lax.axis_size("mp")
    columns = user_factor.shape[1]
    rank = columns * holders
    packing = Packing((user_factor.shape[0], item_factor.shape[0], day_factor.shape[0]), columns)
    user_count, item_count, day_count = (
        users_list.shape[1],
        items_list.shape[1],
        days_list.shape[1],
    )
    packed = pl.pallas_call(
        functools.partial(pack_kernel, packing),
        out_shape=jax.ShapeDtypeStruct((packing.height, LANES), bf16),
        name="pack",
    )(user_factor, item_factor, day_factor)
    table = lax.all_gather(packed, ("dp", "mp"), axis=0).reshape(
        owners, holders, packing.height, LANES
    )
    whole = lambda shape: pl.BlockSpec(shape, lambda s: (0,) * len(shape))
    dense = pl.pallas_call(
        functools.partial(block_kernel, packing, owners, holders, DAYS_PER_STEP),
        out_shape=jax.ShapeDtypeStruct(table.shape, f32),
        grid=(day_count // DAYS_PER_STEP,),
        in_specs=[
            whole((1, user_count)),
            whole((1, item_count)),
            whole((1, day_count)),
            whole((user_count, 1)),
            whole((item_count, 1)),
            whole((day_count, 1)),
            whole(table.shape),
            pl.BlockSpec(
                (1, DAYS_PER_STEP, user_count, item_count), lambda s: (0, s, 0, 0)
            ),
        ],
        out_specs=whole(table.shape),
        scratch_shapes=[
            pltpu.VMEM((user_count, rank), f32),
            pltpu.VMEM((item_count, rank), bf16),
            pltpu.VMEM((rank, item_count), bf16),
            pltpu.VMEM((day_count, rank), f32),
            pltpu.VMEM((user_count, rank), f32),
            pltpu.VMEM((item_count, rank), f32),
            pltpu.VMEM((day_count, rank), f32),
        ],
        compiler_params=pltpu.CompilerParams(vmem_limit_bytes=48 * 1024 * 1024),
        name="block_gradients",
    )(
        users_list,
        items_list,
        days_list,
        users_list.reshape(user_count, 1),
        items_list.reshape(item_count, 1),
        days_list.reshape(day_count, 1),
        table,
        status,
    )
    gradient = lax.psum_scatter(
        dense.reshape(owners * holders, packing.height, LANES),
        ("dp", "mp"),
        scatter_dimension=0,
        tiled=False,
    )
    states = (
        user_factor,
        user_first,
        user_second,
        item_factor,
        item_first,
        item_second,
        day_factor,
        day_first,
        day_second,
    )
    return pl.pallas_call(
        functools.partial(adam_kernel, packing),
        out_shape=tuple(jax.ShapeDtypeStruct(a.shape, a.dtype) for a in states),
        name="adam",
    )(gradient, *states)


def solution(mesh):
    block = P(("dp", "mp"), None)
    piece = P("dp", "mp")
    return jax.shard_map(
        local,
        mesh=mesh,
        in_specs=(block, block, block, P(("dp", "mp"), None, None, None)) + (piece,) * 9,
        out_specs=(piece,) * 9,
        check_vma=False,
    )
```

```python
import functools

import jax
import jax.numpy as jnp
from jax import lax
from jax.experimental import pallas as pl
from jax.experimental.pallas import tpu as pltpu
from jax.sharding import PartitionSpec as P

beta_one = 0.9
beta_two = 0.99
bias_one = 1.0 - 0.9**10
bias_two = 1.0 - 0.99**10
learn_rate = 0.01
epsilon = 1e-08
loss_scale = 0.0625

LANES = 128
DAYS_PER_STEP = 4
VMEM_LIMIT = 56 * 1024 * 1024

f32 = jnp.float32
bf16 = jnp.bfloat16


class Sizes:
    def __init__(self, owners, holders, columns, row_counts, list_counts):
        self.owners = owners
        self.holders = holders
        self.columns = columns
        self.rank = columns * holders
        self.row_counts = row_counts
        self.list_counts = list_counts
        limits = (
            max(2, 3 * list_counts[0] // (2 * owners)),
            max(2, 3 * list_counts[1] // (2 * owners)),
            max(2, 2 * list_counts[2] // owners),
        )
        self.slots = tuple(-(-limit // 16) * 16 for limit in limits)
        self.slot_starts = (0, self.slots[0], self.slots[0] + self.slots[1])
        self.slot_rows = sum(self.slots)
        self.list_starts = (0, list_counts[0], list_counts[0] + list_counts[1])
        self.day_parts = LANES // columns
        self.day_packed = -(-(row_counts[2] // self.day_parts) // 16) * 16
        self.piece_rows = 2 * columns + self.day_packed


def iota(shape, dimension):
    return lax.broadcasted_iota(jnp.int32, shape, dimension)


def onehot(condition):
    return jnp.where(condition, 1.0, 0.0).astype(bf16)


def dot_nt(a, b):
    return lax.dot_general(a, b, (((1,), (1,)), ((), ())), preferred_element_type=f32)


def pack_days(sizes, days):
    rows = sizes.row_counts[2] // sizes.day_parts
    parts = [days[p * rows : (p + 1) * rows] for p in range(sizes.day_parts)]
    if rows != sizes.day_packed:
        blank = jnp.zeros((sizes.day_packed - rows, days.shape[1]), days.dtype)
        parts = [jnp.concatenate([part, blank], axis=0) for part in parts]
    return jnp.concatenate(parts, axis=1)


def unpack_days(sizes, packed):
    rows = sizes.row_counts[2] // sizes.day_parts
    return jnp.concatenate(
        [
            packed[:rows, p * sizes.columns : (p + 1) * sizes.columns]
            for p in range(sizes.day_parts)
        ],
        axis=0,
    )


def pack_kernel(sizes, user_ref, item_ref, day_ref, out_ref):
    columns = sizes.columns
    out_ref[:columns, :] = user_ref[...].astype(bf16)
    out_ref[columns : 2 * columns, :] = item_ref[...].astype(bf16)
    out_ref[2 * columns :, :] = pack_days(sizes, day_ref[...]).astype(bf16)


def slot_kernel(sizes, me_ref, *refs):
    owners = sizes.owners
    lists = refs[:owners]
    outs = refs[owners:]
    me = me_ref[0]
    for t in range(3):
        serve_ref, sum_ref, pick_ref, place_ref = outs[4 * t : 4 * t + 4]
        count, rows, slots = sizes.list_counts[t], sizes.row_counts[t], sizes.slots[t]
        start = sizes.list_starts[t]
        numbers = jnp.concatenate([ref[:, start : start + count] for ref in lists], axis=0)
        owner = numbers // rows
        row = numbers % rows
        earlier = onehot(iota((count, count), 0) < iota((count, count), 1))
        mine = owner == me
        position = jnp.dot(onehot(mine), earlier, preferred_element_type=f32).astype(jnp.int32)
        position = jnp.where(mine, position, -1)
        for s in range(owners):
            slot_hot = onehot(iota((slots, count), 0) == position[s : s + 1])
            row_hot = onehot(iota((rows, count), 0) == row[s : s + 1])
            serve_ref[s * slots : (s + 1) * slots, :] = dot_nt(slot_hot, row_hot).astype(bf16)
        sum_ref[...] = serve_ref[...].astype(f32).T.astype(bf16)
        own = owner[0:1]
        owner_hot = iota((owners, count), 0) == own
        before = jnp.dot(onehot(owner_hot), earlier, preferred_element_type=f32)
        position = jnp.sum(jnp.where(owner_hot, before, 0.0), axis=0, keepdims=True)
        target = lax.bitwise_xor(own, jnp.full_like(own, me)) * slots + position.astype(jnp.int32)
        place = jnp.where(iota((owners * slots, count), 0) == target, 1.0, 0.0)
        place_ref[...] = place.astype(bf16)
        pick_ref[...] = place.T.astype(bf16)


def serve_kernel(sizes, *refs):
    holders, owners, columns = sizes.holders, sizes.owners, sizes.columns
    pieces = refs[:holders]
    selectors = refs[holders : holders + 3]
    outs = refs[holders + 3 :]
    for t in range(3):
        if t < 2:
            table = jnp.concatenate(
                [ref[t * columns : (t + 1) * columns, :] for ref in pieces], axis=0
            )
            rows = dot_nt(selectors[t][...], table)
        else:
            table = jnp.concatenate(
                [unpack_days(sizes, ref[2 * columns :, :].astype(f32)) for ref in pieces], axis=1
            ).astype(bf16)
            rows = jnp.dot(selectors[t][...], table, preferred_element_type=f32)
        rows = rows.astype(bf16)
        start, slots = sizes.slot_starts[t], sizes.slots[t]
        for s in range(owners):
            outs[s][start : start + slots, :] = rows[s * slots : (s + 1) * slots]


def block_kernel(sizes, days_per_step, *refs):
    owners = sizes.owners
    arrived = refs[:owners]
    picks = refs[owners : owners + 3]
    places = refs[owners + 3 : owners + 6]
    status_ref = refs[owners + 6]
    outs = refs[owners + 7 : 2 * owners + 7]
    users, items, items_half_t, days, user_gradient, item_gradient, day_gradient = refs[
        2 * owners + 7 :
    ]
    step = pl.program_id(0)

    def pick(t):
        start, slots = sizes.slot_starts[t], sizes.slots[t]
        rows = jnp.concatenate([ref[start : start + slots, :] for ref in arrived], axis=0)
        return jnp.dot(picks[t][...], rows, preferred_element_type=f32)

    @pl.when(step == 0)
    def _():
        users[...] = pick(0)
        item_values = pick(1)
        items[...] = item_values.astype(bf16)
        items_half_t[...] = (0.5 * item_values).T.astype(bf16)
        days[...] = pick(2)
        user_gradient[...] = jnp.zeros_like(user_gradient)
        item_gradient[...] = jnp.zeros_like(item_gradient)

    for j in range(days_per_step):
        k = step * days_per_step + j
        day = days[pl.ds(k, 1), :]
        user_values = users[...]
        scaled = (day * user_values).astype(bf16)
        half_logits = jnp.dot(scaled, items_half_t[...], preferred_element_type=f32)
        state = status_ref[0, j]
        residual = (
            (0.5 * loss_scale)
            * state.astype(f32)
            * (jnp.tanh(half_logits) + jnp.where(state == 1, -1.0, 1.0))
        ).astype(bf16)
        projected = jnp.dot(residual, items[...], preferred_element_type=f32)
        user_gradient[...] += projected * day
        day_gradient[pl.ds(k, 1), :] = jnp.sum(projected * user_values, axis=0, keepdims=True)
        item_gradient[...] += lax.dot_general(
            residual, scaled, (((0,), (0,)), ((), ())), preferred_element_type=f32
        )

    @pl.when(step == pl.num_programs(0) - 1)
    def _():
        for t, gradient in enumerate((user_gradient, item_gradient, day_gradient)):
            start, slots = sizes.slot_starts[t], sizes.slots[t]
            placed = jnp.dot(
                places[t][...], gradient[...].astype(bf16), preferred_element_type=f32
            ).astype(bf16)
            for s in range(owners):
                outs[s][start : start + slots, :] = placed[s * slots : (s + 1) * slots]


def sum_kernel(sizes, *refs):
    holders, owners, columns = sizes.holders, sizes.owners, sizes.columns
    arrived = refs[:owners]
    selectors = refs[owners : owners + 3]
    outs = refs[owners + 3 :]
    for t in range(3):
        start, slots = sizes.slot_starts[t], sizes.slots[t]
        rows = jnp.concatenate([ref[start : start + slots, :] for ref in arrived], axis=0)
        total = jnp.dot(selectors[t][...], rows, preferred_element_type=f32)
        if t < 2:
            turned = total.T.astype(bf16)
            for j in range(holders):
                outs[j][t * columns : (t + 1) * columns, :] = turned[
                    j * columns : (j + 1) * columns
                ]
        else:
            for j in range(holders):
                outs[j][2 * columns :, :] = pack_days(
                    sizes, total[:, j * columns : (j + 1) * columns]
                ).astype(bf16)


def adam_kernel(sizes, *refs):
    holders, columns = sizes.holders, sizes.columns
    pieces = refs[:holders]
    states = refs[holders : holders + 9]
    outs = refs[holders + 9 :]
    total = pieces[0][...].astype(f32)
    for ref in pieces[1:]:
        total = total + ref[...].astype(f32)
    for t in range(3):
        if t < 2:
            gradient = total[t * columns : (t + 1) * columns]
        else:
            gradient = unpack_days(sizes, total[2 * columns :])
        factor, first, second = states[3 * t : 3 * t + 3]
        new_factor, new_first, new_second = outs[3 * t : 3 * t + 3]
        first_value = beta_one * first[...] + (1.0 - beta_one) * gradient
        second_value = beta_two * second[...] + (1.0 - beta_two) * gradient * gradient
        change = (
            learn_rate
            * (first_value / bias_one)
            / (jnp.sqrt(second_value / bias_two) + epsilon)
        )
        new_factor[...] = factor[...] - change
        new_first[...] = first_value
        new_second[...] = second_value


def swap_all(arrays, axis, size):
    return [arrays[0]] + [
        lax.ppermute(arrays[s], axis, [(i, i ^ s) for i in range(size)]) for s in range(1, size)
    ]


def local(
    users_list,
    items_list,
    days_list,
    status,
    user_factor,
    user_first,
    user_second,
    item_factor,
    item_first,
    item_second,
    day_factor,
    day_first,
    day_second,
):
    owners = lax.axis_size("dp")
    holders = lax.axis_size("mp")
    row_counts = (user_factor.shape[0], item_factor.shape[0], day_factor.shape[0])
    list_counts = (users_list.shape[1], items_list.shape[1], days_list.shape[1])
    sizes = Sizes(owners, holders, user_factor.shape[1], row_counts, list_counts)
    params = pltpu.CompilerParams(vmem_limit_bytes=VMEM_LIMIT)
    shape = jax.ShapeDtypeStruct

    numbers = jnp.concatenate([users_list, items_list, days_list], axis=1)
    lists = swap_all([numbers] * owners, "dp", owners)
    piece = pl.pallas_call(
        functools.partial(pack_kernel, sizes),
        out_shape=shape((sizes.piece_rows, LANES), bf16),
        compiler_params=params,
        name="pack",
    )(user_factor.T, item_factor.T, day_factor)
    pieces = swap_all([piece] * holders, "mp", holders)

    selector_shapes = []
    for t in range(3):
        flat = owners * sizes.slots[t]
        selector_shapes += [
            shape((flat, row_counts[t]), bf16),
            shape((row_counts[t], flat), bf16),
            shape((list_counts[t], flat), bf16),
            shape((flat, list_counts[t]), bf16),
        ]
    selectors = pl.pallas_call(
        functools.partial(slot_kernel, sizes),
        out_shape=tuple(selector_shapes),
        in_specs=[pl.BlockSpec(memory_space=pltpu.SMEM)]
        + [pl.BlockSpec(memory_space=pltpu.VMEM)] * owners,
        compiler_params=params,
        name="slots",
    )(lax.axis_index("dp").astype(jnp.int32).reshape(1), *lists)
    serves, sums, picks, places = (selectors[n::4] for n in range(4))

    served = pl.pallas_call(
        functools.partial(serve_kernel, sizes),
        out_shape=tuple([shape((sizes.slot_rows, sizes.rank), bf16)] * owners),
        compiler_params=params,
        name="serve",
    )(*pieces, *serves)
    arrived = swap_all(served, "dp", owners)

    whole = lambda a: pl.BlockSpec(a.shape, lambda s: (0,) * len(a.shape))
    inputs = [*arrived, *picks, *places]
    users, items, days = list_counts
    gradients = pl.pallas_call(
        functools.partial(block_kernel, sizes, DAYS_PER_STEP),
        out_shape=tuple(shape(a.shape, bf16) for a in arrived),
        grid=(days // DAYS_PER_STEP,),
        in_specs=[whole(a) for a in inputs]
        + [pl.BlockSpec((1, DAYS_PER_STEP, users, items), lambda s: (0, s, 0, 0))],
        out_specs=tuple(whole(a) for a in arrived),
        scratch_shapes=[
            pltpu.VMEM((users, sizes.rank), f32),
            pltpu.VMEM((items, sizes.rank), bf16),
            pltpu.VMEM((sizes.rank, items), bf16),
            pltpu.VMEM((days, sizes.rank), f32),
            pltpu.VMEM((users, sizes.rank), f32),
            pltpu.VMEM((items, sizes.rank), f32),
            pltpu.VMEM((days, sizes.rank), f32),
        ],
        compiler_params=params,
        name="block_gradients",
    )(*inputs, status)
    returned = swap_all(gradients, "dp", owners)

    totals = pl.pallas_call(
        functools.partial(sum_kernel, sizes),
        out_shape=tuple([shape(piece.shape, bf16)] * holders),
        compiler_params=params,
        name="row_sums",
    )(*returned, *sums)
    column_totals = swap_all(totals, "mp", holders)

    states = (
        user_factor.T,
        user_first.T,
        user_second.T,
        item_factor.T,
        item_first.T,
        item_second.T,
        day_factor,
        day_first,
        day_second,
    )
    updated = pl.pallas_call(
        functools.partial(adam_kernel, sizes),
        out_shape=tuple(shape(a.shape, a.dtype) for a in states),
        compiler_params=params,
        name="adam",
    )(*column_totals, *states)
    return tuple(a.T for a in updated[:6]) + tuple(updated[6:])


def solution(mesh):
    block = P(("dp", "mp"), None)
    piece = P("dp", "mp")
    return jax.shard_map(
        local,
        mesh=mesh,
        in_specs=(block, block, block, P(("dp", "mp"), None, None, None)) + (piece,) * 9,
        out_specs=(piece,) * 9,
        check_vma=False,
    )
```

```python
import functools

import jax
import jax.numpy as jnp
from jax import lax
from jax.experimental import pallas as pl
from jax.experimental.pallas import tpu as pltpu
from jax.sharding import PartitionSpec as P

beta_one = 0.9
beta_two = 0.99
bias_one = 1.0 - 0.9**10
bias_two = 1.0 - 0.99**10
learn_rate = 0.01
epsilon = 1e-08
loss_scale = 0.0625

LANES = 128
DAYS_PER_STEP = 4
SMALL_VMEM = 16 * 1024 * 1024
BLOCK_VMEM = 32 * 1024 * 1024

f32 = jnp.float32
bf16 = jnp.bfloat16


class Sizes:
    def __init__(self, owners, holders, columns, row_counts, list_counts):
        self.owners = owners
        self.holders = holders
        self.columns = columns
        self.rank = columns * holders
        self.row_counts = row_counts
        self.list_counts = list_counts
        limits = (
            max(2, 3 * list_counts[0] // (2 * owners)),
            max(2, 3 * list_counts[1] // (2 * owners)),
            max(2, 2 * list_counts[2] // owners),
        )
        self.slots = tuple(-(-(limit + t // 2) // 16) * 16 for t, limit in enumerate(limits))
        self.note_row = limits[2]
        self.slot_starts = (0, self.slots[0], self.slots[0] + self.slots[1])
        self.slot_rows = sum(self.slots)
        self.day_parts = LANES // columns
        self.day_packed = -(-(row_counts[2] // self.day_parts) // 16) * 16
        self.piece_rows = 2 * columns + self.day_packed
        self.day_chunks = self.rank // LANES
        self.table_rows = 2 * self.rank + self.day_chunks * row_counts[2]


def iota(shape, dimension):
    return lax.broadcasted_iota(jnp.int32, shape, dimension)


def onehot(condition):
    return jnp.where(condition, 1.0, 0.0).astype(bf16)


def dot_nt(a, b):
    return lax.dot_general(a, b, (((1,), (1,)), ((), ())), preferred_element_type=f32)


def pack_days(sizes, days):
    rows = sizes.row_counts[2] // sizes.day_parts
    parts = [days[p * rows : (p + 1) * rows] for p in range(sizes.day_parts)]
    if rows != sizes.day_packed:
        blank = jnp.zeros((sizes.day_packed - rows, days.shape[1]), days.dtype)
        parts = [jnp.concatenate([part, blank], axis=0) for part in parts]
    return jnp.concatenate(parts, axis=1)


def unpack_days(sizes, packed):
    rows = sizes.row_counts[2] // sizes.day_parts
    return jnp.concatenate(
        [
            packed[:rows, p * sizes.columns : (p + 1) * sizes.columns]
            for p in range(sizes.day_parts)
        ],
        axis=0,
    )


def pack_kernel(sizes, user_ref, item_ref, day_ref, out_ref):
    columns = sizes.columns
    out_ref[:columns, :] = user_ref[...].astype(bf16)
    out_ref[columns : 2 * columns, :] = item_ref[...].astype(bf16)
    out_ref[2 * columns :, :] = pack_days(sizes, day_ref[...]).astype(bf16)


def slot_kernel(sizes, me_ref, *refs):
    owners = sizes.owners
    lists, picks, places, note_ref = refs[:3], refs[3:6], refs[6:9], refs[9]
    me = me_ref[0]
    notes = [[] for _ in range(owners)]
    for t in range(3):
        count, rows, slots = sizes.list_counts[t], sizes.row_counts[t], sizes.slots[t]
        number = lists[t][...]
        owner = number // rows
        row = number % rows
        partner = lax.bitwise_xor(owner, jnp.full_like(owner, me))
        picks[t][...] = onehot(iota((owners * rows, count), 0) == partner * rows + row)
        earlier = onehot(iota((count, count), 0) < iota((count, count), 1))
        owner_hot = iota((owners, count), 0) == owner
        before = jnp.dot(onehot(owner_hot), earlier, preferred_element_type=f32)
        position = jnp.sum(jnp.where(owner_hot, before, 0.0), axis=0, keepdims=True)
        target = partner * slots + position.astype(jnp.int32)
        place = onehot(iota((owners * slots, count), 0) == target)
        places[t][...] = place
        following = (row + 1).astype(bf16)
        for s in range(owners):
            notes[s].append(dot_nt(following, place[s * slots : (s + 1) * slots]) - 1.0)
    blank = jnp.full((1, sizes.rank - sizes.slot_rows), -1.0, f32)
    note_ref[...] = jnp.concatenate(
        [jnp.concatenate(note + [blank], axis=1) for note in notes], axis=0
    )


def table_kernel(sizes, *refs):
    pieces, out_ref = refs[:-1], refs[-1]
    columns, rank, day_rows = sizes.columns, sizes.rank, sizes.row_counts[2]
    for j, ref in enumerate(pieces):
        for t in range(2):
            out_ref[t * rank + j * columns : t * rank + (j + 1) * columns, :] = ref[
                t * columns : (t + 1) * columns, :
            ]
    days = jnp.concatenate(
        [unpack_days(sizes, ref[2 * columns :, :].astype(f32)) for ref in pieces], axis=1
    ).astype(bf16)
    for chunk in range(sizes.day_chunks):
        start = 2 * rank + chunk * day_rows
        out_ref[start : start + day_rows, :] = days[:, chunk * LANES : (chunk + 1) * LANES]


def block_kernel(sizes, days_per_step, *refs):
    owners, rank, day_rows = sizes.owners, sizes.rank, sizes.row_counts[2]
    tables = refs[:owners]
    picks = refs[owners : owners + 3]
    places = refs[owners + 3 : owners + 6]
    note_ref, status_ref = refs[owners + 6 : owners + 8]
    outs = refs[owners + 8 : 2 * owners + 8]
    users, items, items_half_t, days, user_gradient, item_gradient, day_gradient = refs[
        2 * owners + 8 :
    ]
    step = pl.program_id(0)

    def pick(t):
        table = jnp.concatenate([ref[t * rank : (t + 1) * rank, :] for ref in tables], axis=1)
        return jnp.dot(table, picks[t][...], preferred_element_type=f32)

    @pl.when(step == 0)
    def _():
        users[...] = pick(0).T
        items_t = pick(1)
        items[...] = items_t.T.astype(bf16)
        items_half_t[...] = (0.5 * items_t).astype(bf16)
        starts = [2 * rank + chunk * day_rows for chunk in range(sizes.day_chunks)]
        day_table = jnp.concatenate(
            [
                jnp.concatenate([ref[start : start + day_rows, :] for start in starts], axis=1)
                for ref in tables
            ],
            axis=0,
        )
        days[...] = lax.dot_general(
            picks[2][...], day_table, (((0,), (0,)), ((), ())), preferred_element_type=f32
        )
        user_gradient[...] = jnp.zeros_like(user_gradient)
        item_gradient[...] = jnp.zeros_like(item_gradient)

    for j in range(days_per_step):
        k = step * days_per_step + j
        day = days[pl.ds(k, 1), :]
        user_values = users[...]
        scaled = (day * user_values).astype(bf16)
        half_logits = jnp.dot(scaled, items_half_t[...], preferred_element_type=f32)
        state = status_ref[0, j]
        residual = (
            (0.5 * loss_scale)
            * state.astype(f32)
            * (jnp.tanh(half_logits) + jnp.where(state == 1, -1.0, 1.0))
        ).astype(bf16)
        projected = jnp.dot(residual, items[...], preferred_element_type=f32)
        user_gradient[...] += projected * day
        day_gradient[pl.ds(k, 1), :] = jnp.sum(projected * user_values, axis=0, keepdims=True)
        item_gradient[...] += lax.dot_general(
            residual, scaled, (((0,), (0,)), ((), ())), preferred_element_type=f32
        )

    @pl.when(step == pl.num_programs(0) - 1)
    def _():
        for t, gradient in enumerate((user_gradient, item_gradient, day_gradient)):
            start, slots = sizes.slot_starts[t], sizes.slots[t]
            placed = jnp.dot(
                places[t][...], gradient[...].astype(bf16), preferred_element_type=f32
            )
            for s in range(owners):
                rows = placed[s * slots : (s + 1) * slots]
                if t == 2:
                    note = iota(rows.shape, 0) == sizes.note_row
                    rows = jnp.where(note, note_ref[s : s + 1, :], rows)
                outs[s][start : start + slots, :] = rows.astype(bf16)


def sum_kernel(sizes, *refs):
    holders, owners, columns = sizes.holders, sizes.owners, sizes.columns
    arrived, outs = refs[:owners], refs[owners:]
    day_start = sizes.slot_starts[2]
    totals = [0.0, 0.0, 0.0]
    for ref in arrived:
        notes = ref[day_start : day_start + sizes.slots[2], :].astype(f32)
        rows = notes[sizes.note_row : sizes.note_row + 1, : sizes.slot_rows].astype(jnp.int32)
        for t in range(3):
            start, slots = sizes.slot_starts[t], sizes.slots[t]
            shape = (sizes.row_counts[t], sizes.slot_rows)
            slot = iota(shape, 1)
            mine = (slot >= start) & (slot < start + slots)
            selector = onehot((iota(shape, 0) == rows) & mine)
            totals[t] = totals[t] + jnp.dot(selector, ref[...], preferred_element_type=f32)
    for t in range(3):
        if t < 2:
            turned = totals[t].T.astype(bf16)
            for j in range(holders):
                outs[j][t * columns : (t + 1) * columns, :] = turned[
                    j * columns : (j + 1) * columns
                ]
        else:
            for j in range(holders):
                outs[j][2 * columns :, :] = pack_days(
                    sizes, totals[t][:, j * columns : (j + 1) * columns]
                ).astype(bf16)


def adam_kernel(sizes, *refs):
    holders, columns = sizes.holders, sizes.columns
    pieces = refs[:holders]
    states = refs[holders : holders + 9]
    outs = refs[holders + 9 :]
    total = pieces[0][...].astype(f32)
    for ref in pieces[1:]:
        total = total + ref[...].astype(f32)
    for t in range(3):
        if t < 2:
            gradient = total[t * columns : (t + 1) * columns]
        else:
            gradient = unpack_days(sizes, total[2 * columns :])
        factor, first, second = states[3 * t : 3 * t + 3]
        new_factor, new_first, new_second = outs[3 * t : 3 * t + 3]
        first_value = beta_one * first[...] + (1.0 - beta_one) * gradient
        second_value = beta_two * second[...] + (1.0 - beta_two) * gradient * gradient
        change = (
            learn_rate
            * (first_value / bias_one)
            / (jnp.sqrt(second_value / bias_two) + epsilon)
        )
        new_factor[...] = factor[...] - change
        new_first[...] = first_value
        new_second[...] = second_value


def swap(array, axis, size, bits):
    return lax.ppermute(array, axis, [(i, i ^ bits) for i in range(size)])


def local(
    users_list,
    items_list,
    days_list,
    status,
    user_factor,
    user_first,
    user_second,
    item_factor,
    item_first,
    item_second,
    day_factor,
    day_first,
    day_second,
):
    owners = lax.axis_size("dp")
    holders = lax.axis_size("mp")
    row_counts = (user_factor.shape[0], item_factor.shape[0], day_factor.shape[0])
    list_counts = (users_list.shape[1], items_list.shape[1], days_list.shape[1])
    sizes = Sizes(owners, holders, user_factor.shape[1], row_counts, list_counts)
    shape = jax.ShapeDtypeStruct
    small = pltpu.CompilerParams(vmem_limit_bytes=SMALL_VMEM)

    piece = pl.pallas_call(
        functools.partial(pack_kernel, sizes),
        out_shape=shape((sizes.piece_rows, LANES), bf16),
        compiler_params=small,
        name="pack",
    )(user_factor.T, item_factor.T, day_factor)
    pieces = [piece] + [swap(piece, "mp", holders, bits) for bits in range(1, holders)]

    picks_places_notes = pl.pallas_call(
        functools.partial(slot_kernel, sizes),
        out_shape=tuple(
            [shape((owners * row_counts[t], list_counts[t]), bf16) for t in range(3)]
            + [shape((owners * sizes.slots[t], list_counts[t]), bf16) for t in range(3)]
            + [shape((owners, sizes.rank), f32)]
        ),
        in_specs=[pl.BlockSpec(memory_space=pltpu.SMEM)]
        + [pl.BlockSpec(memory_space=pltpu.VMEM)] * 3,
        compiler_params=small,
        name="slots",
    )(lax.axis_index("dp").astype(jnp.int32).reshape(1), users_list, items_list, days_list)

    table = pl.pallas_call(
        functools.partial(table_kernel, sizes),
        out_shape=shape((sizes.table_rows, LANES), bf16),
        compiler_params=small,
        name="table",
    )(*pieces)
    tables = {0: table}
    for bits in range(2, owners, 2):
        tables[bits] = swap(table, "dp", owners, bits)
    for bits in range(0, owners, 2):
        tables[bits + 1] = swap(tables[bits], "dp", owners, 1)

    whole = lambda a: pl.BlockSpec(a.shape, lambda s: (0,) * len(a.shape))
    inputs = [*[tables[bits] for bits in range(owners)], *picks_places_notes]
    users, items, days = list_counts
    message = shape((sizes.slot_rows, sizes.rank), bf16)
    gradients = pl.pallas_call(
        functools.partial(block_kernel, sizes, DAYS_PER_STEP),
        out_shape=tuple([message] * owners),
        grid=(days // DAYS_PER_STEP,),
        in_specs=[whole(a) for a in inputs]
        + [pl.BlockSpec((1, DAYS_PER_STEP, users, items), lambda s: (0, s, 0, 0))],
        out_specs=tuple([whole(message)] * owners),
        scratch_shapes=[
            pltpu.VMEM((users, sizes.rank), f32),
            pltpu.VMEM((items, sizes.rank), bf16),
            pltpu.VMEM((sizes.rank, items), bf16),
            pltpu.VMEM((days, sizes.rank), f32),
            pltpu.VMEM((users, sizes.rank), f32),
            pltpu.VMEM((items, sizes.rank), f32),
            pltpu.VMEM((days, sizes.rank), f32),
        ],
        compiler_params=pltpu.CompilerParams(vmem_limit_bytes=BLOCK_VMEM),
        name="block_gradients",
    )(*inputs, status)
    crossed = [swap(gradients[bits + 1], "dp", owners, 1) for bits in range(0, owners, 2)]
    returned = [gradients[0], crossed[0]]
    for bits in range(2, owners, 2):
        returned.append(swap(gradients[bits], "dp", owners, bits))
        returned.append(swap(crossed[bits // 2], "dp", owners, bits))

    totals = pl.pallas_call(
        functools.partial(sum_kernel, sizes),
        out_shape=tuple([shape(piece.shape, bf16)] * holders),
        compiler_params=small,
        name="row_sums",
    )(*returned)
    column_totals = [totals[0]] + [
        swap(totals[bits], "mp", holders, bits) for bits in range(1, holders)
    ]

    states = (
        user_factor.T,
        user_first.T,
        user_second.T,
        item_factor.T,
        item_first.T,
        item_second.T,
        day_factor,
        day_first,
        day_second,
    )
    updated = pl.pallas_call(
        functools.partial(adam_kernel, sizes),
        out_shape=tuple(shape(a.shape, a.dtype) for a in states),
        compiler_params=small,
        name="adam",
    )(*column_totals, *states)
    return tuple(a.T for a in updated[:6]) + tuple(updated[6:])


def solution(mesh):
    block = P(("dp", "mp"), None)
    piece = P("dp", "mp")
    return jax.shard_map(
        local,
        mesh=mesh,
        in_specs=(block, block, block, P(("dp", "mp"), None, None, None)) + (piece,) * 9,
        out_specs=(piece,) * 9,
        check_vma=False,
    )
```

```python
import functools

import jax
import jax.numpy as jnp
from jax import lax
from jax.experimental import pallas as pl
from jax.experimental.pallas import tpu as pltpu
from jax.sharding import PartitionSpec as P

beta_one = 0.9
beta_two = 0.99
bias_one = 1.0 - 0.9**10
bias_two = 1.0 - 0.99**10
learn_rate = 0.01
epsilon = 1e-08
loss_scale = 0.0625

LANES = 128
DAYS_PER_STEP = 4
SMALL_VMEM = 16 * 1024 * 1024
BLOCK_VMEM = 48 * 1024 * 1024
PACK_VMEM = 56 * 1024 * 1024

f32 = jnp.float32
bf16 = jnp.bfloat16


class Sizes:
    def __init__(self, owners, holders, columns, row_counts, list_counts):
        self.owners = owners
        self.holders = holders
        self.columns = columns
        self.rank = columns * holders
        self.row_counts = row_counts
        self.list_counts = list_counts
        limits = (
            max(2, 3 * list_counts[0] // (2 * owners)),
            max(2, 3 * list_counts[1] // (2 * owners)),
            max(2, 2 * list_counts[2] // owners),
        )
        self.slots = tuple(-(-(limit + t // 2) // 16) * 16 for t, limit in enumerate(limits))
        self.note_row = limits[2]
        self.slot_starts = (0, self.slots[0], self.slots[0] + self.slots[1])
        self.slot_rows = sum(self.slots)
        self.day_parts = LANES // columns
        self.day_packed = -(-(row_counts[2] // self.day_parts) // 16) * 16
        self.piece_rows = 2 * columns + self.day_packed
        self.day_chunks = self.rank // LANES
        self.table_rows = 2 * self.rank + self.day_chunks * row_counts[2]


def iota(shape, dimension):
    return lax.broadcasted_iota(jnp.int32, shape, dimension)


def onehot(condition):
    return jnp.where(condition, 1.0, 0.0).astype(bf16)


def dot_nt(a, b):
    return lax.dot_general(a, b, (((1,), (1,)), ((), ())), preferred_element_type=f32)


def pack_days(sizes, days):
    rows = sizes.row_counts[2] // sizes.day_parts
    parts = [days[p * rows : (p + 1) * rows] for p in range(sizes.day_parts)]
    if rows != sizes.day_packed:
        blank = jnp.zeros((sizes.day_packed - rows, days.shape[1]), days.dtype)
        parts = [jnp.concatenate([part, blank], axis=0) for part in parts]
    return jnp.concatenate(parts, axis=1)


def unpack_days(sizes, packed):
    rows = sizes.row_counts[2] // sizes.day_parts
    return jnp.concatenate(
        [
            packed[:rows, p * sizes.columns : (p + 1) * sizes.columns]
            for p in range(sizes.day_parts)
        ],
        axis=0,
    )


def fetch(sources, targets, semaphores):
    copies = [
        pltpu.make_async_copy(source, target, semaphores.at[n])
        for n, (source, target) in enumerate(zip(sources, targets))
    ]
    for copy in copies:
        copy.start()
    for copy in copies:
        copy.wait()


def pack_kernel(sizes, user_hbm, item_hbm, day_hbm, out_ref, user, item, day, semaphores):
    columns = sizes.columns
    fetch((user_hbm, item_hbm, day_hbm), (user, item, day), semaphores)
    out_ref[:columns, :] = user[...].astype(bf16)
    out_ref[columns : 2 * columns, :] = item[...].astype(bf16)
    out_ref[2 * columns :, :] = pack_days(sizes, day[...]).astype(bf16)


def slot_kernel(sizes, me_ref, *refs):
    owners = sizes.owners
    picks, places, note_ref, lists = refs[3:6], refs[6:9], refs[9], refs[10:13]
    fetch(refs[:3], lists, refs[13])
    me = me_ref[0]
    notes = [[] for _ in range(owners)]
    for t in range(3):
        count, rows, slots = sizes.list_counts[t], sizes.row_counts[t], sizes.slots[t]
        number = lists[t][...]
        owner = number // rows
        row = number % rows
        partner = lax.bitwise_xor(owner, jnp.full_like(owner, me))
        picks[t][...] = onehot(iota((owners * rows, count), 0) == partner * rows + row)
        earlier = onehot(iota((count, count), 0) < iota((count, count), 1))
        owner_hot = iota((owners, count), 0) == owner
        before = jnp.dot(onehot(owner_hot), earlier, preferred_element_type=f32)
        position = jnp.sum(jnp.where(owner_hot, before, 0.0), axis=0, keepdims=True)
        target = partner * slots + position.astype(jnp.int32)
        place = onehot(iota((owners * slots, count), 0) == target)
        places[t][...] = place
        following = (row + 1).astype(bf16)
        for s in range(owners):
            notes[s].append(dot_nt(following, place[s * slots : (s + 1) * slots]) - 1.0)
    blank = jnp.full((1, sizes.rank - sizes.slot_rows), -1.0, f32)
    note_ref[...] = jnp.concatenate(
        [jnp.concatenate(note + [blank], axis=1) for note in notes], axis=0
    )


def table_kernel(sizes, *refs):
    pieces, out_ref = refs[:-2], refs[-1]
    columns, rank, day_rows = sizes.columns, sizes.rank, sizes.row_counts[2]
    for j, ref in enumerate(pieces):
        for t in range(2):
            out_ref[t * rank + j * columns : t * rank + (j + 1) * columns, :] = ref[
                t * columns : (t + 1) * columns, :
            ]
    days = jnp.concatenate(
        [unpack_days(sizes, ref[2 * columns :, :].astype(f32)) for ref in pieces], axis=1
    ).astype(bf16)
    for chunk in range(sizes.day_chunks):
        start = 2 * rank + chunk * day_rows
        out_ref[start : start + day_rows, :] = days[:, chunk * LANES : (chunk + 1) * LANES]


def block_kernel(sizes, days_per_step, *refs):
    owners, rank, day_rows = sizes.owners, sizes.rank, sizes.row_counts[2]
    tables = refs[:owners]
    picks = refs[owners : owners + 3]
    places = refs[owners + 3 : owners + 6]
    note_ref, status_hbm, own_ref, other_ref = refs[owners + 6 : owners + 10]
    (
        users,
        items,
        items_half_t,
        days,
        user_gradient,
        item_gradient,
        day_gradient,
        status,
        semaphores,
    ) = refs[owners + 10 :]
    steps = status.shape[0] // days_per_step

    def status_copy(step):
        chunk = pl.ds(step * days_per_step, days_per_step)
        return pltpu.make_async_copy(
            status_hbm.at[0, chunk], status.at[chunk], semaphores.at[step]
        )

    for step in range(steps):
        status_copy(step).start()

    def pick(t):
        table = jnp.concatenate([ref[t * rank : (t + 1) * rank, :] for ref in tables], axis=1)
        return jnp.dot(table, picks[t][...], preferred_element_type=f32)

    users[...] = pick(0).T
    items_t = pick(1)
    items[...] = items_t.T.astype(bf16)
    items_half_t[...] = (0.5 * items_t).astype(bf16)
    starts = [2 * rank + chunk * day_rows for chunk in range(sizes.day_chunks)]
    day_table = jnp.concatenate(
        [
            jnp.concatenate([ref[start : start + day_rows, :] for start in starts], axis=1)
            for ref in tables
        ],
        axis=0,
    )
    days[...] = lax.dot_general(
        picks[2][...], day_table, (((0,), (0,)), ((), ())), preferred_element_type=f32
    )
    user_gradient[...] = jnp.zeros_like(user_gradient)
    item_gradient[...] = jnp.zeros_like(item_gradient)

    @pl.loop(0, steps)
    def _(step):
        status_copy(step).wait()
        for j in range(days_per_step):
            k = step * days_per_step + j
            day = days[pl.ds(k, 1), :]
            user_values = users[...]
            scaled = (day * user_values).astype(bf16)
            half_logits = jnp.dot(scaled, items_half_t[...], preferred_element_type=f32)
            state = status[k]
            residual = (
                (0.5 * loss_scale)
                * state.astype(f32)
                * (jnp.tanh(half_logits) + jnp.where(state == 1, -1.0, 1.0))
            ).astype(bf16)
            projected = jnp.dot(residual, items[...], preferred_element_type=f32)
            user_gradient[...] += projected * day
            day_gradient[pl.ds(k, 1), :] = jnp.sum(projected * user_values, axis=0, keepdims=True)
            item_gradient[...] += lax.dot_general(
                residual, scaled, (((0,), (0,)), ((), ())), preferred_element_type=f32
            )

    for t, gradient in enumerate((user_gradient, item_gradient, day_gradient)):
        start, slots = sizes.slot_starts[t], sizes.slots[t]
        placed = jnp.dot(places[t][...], gradient[...].astype(bf16), preferred_element_type=f32)
        for s in range(owners):
            rows = placed[s * slots : (s + 1) * slots]
            if t == 2:
                note = iota(rows.shape, 0) == sizes.note_row
                rows = jnp.where(note, note_ref[s : s + 1, :], rows)
            out = (own_ref, other_ref)[s % 2]
            first = (s // 2) * sizes.slot_rows + start
            out[first : first + slots, :] = rows.astype(bf16)


def merge_kernel(sizes, own_ref, crossed_ref, *outs):
    rows = sizes.slot_rows
    for n, out in enumerate(outs):
        start = (n + 1) * rows
        out[:rows, :] = own_ref[start : start + rows, :]
        out[rows:, :] = crossed_ref[start : start + rows, :]


def sum_kernel(sizes, *refs):
    holders, columns = sizes.holders, sizes.columns
    inputs = sizes.owners // 2 + 1
    arrived, outs = refs[:inputs], refs[inputs:]
    day_start = sizes.slot_starts[2]
    totals = [0.0, 0.0, 0.0]
    messages = [ref.at[: sizes.slot_rows] for ref in arrived]
    messages += [ref.at[sizes.slot_rows :] for ref in arrived[2:]]
    for ref in messages:
        notes = ref[day_start : day_start + sizes.slots[2], :].astype(f32)
        rows = notes[sizes.note_row : sizes.note_row + 1, : sizes.slot_rows].astype(jnp.int32)
        for t in range(3):
            start, slots = sizes.slot_starts[t], sizes.slots[t]
            shape = (sizes.row_counts[t], sizes.slot_rows)
            slot = iota(shape, 1)
            mine = (slot >= start) & (slot < start + slots)
            selector = onehot((iota(shape, 0) == rows) & mine)
            totals[t] = totals[t] + jnp.dot(selector, ref[...], preferred_element_type=f32)
    for t in range(3):
        if t < 2:
            turned = totals[t].T.astype(bf16)
            for j in range(holders):
                outs[j][t * columns : (t + 1) * columns, :] = turned[
                    j * columns : (j + 1) * columns
                ]
        else:
            for j in range(holders):
                outs[j][2 * columns :, :] = pack_days(
                    sizes, totals[t][:, j * columns : (j + 1) * columns]
                ).astype(bf16)


def adam_kernel(sizes, *refs):
    holders, columns = sizes.holders, sizes.columns
    pieces = refs[:holders]
    states = refs[holders : holders + 9]
    outs = refs[holders + 9 :]
    total = pieces[0][...].astype(f32)
    for ref in pieces[1:]:
        total = total + ref[...].astype(f32)
    for t in range(3):
        if t < 2:
            gradient = total[t * columns : (t + 1) * columns]
        else:
            gradient = unpack_days(sizes, total[2 * columns :])
        factor, first, second = states[3 * t : 3 * t + 3]
        new_factor, new_first, new_second = outs[3 * t : 3 * t + 3]
        first_value = beta_one * first[...] + (1.0 - beta_one) * gradient
        second_value = beta_two * second[...] + (1.0 - beta_two) * gradient * gradient
        change = (
            learn_rate
            * (first_value / bias_one)
            / (jnp.sqrt(second_value / bias_two) + epsilon)
        )
        new_factor[...] = factor[...] - change
        new_first[...] = first_value
        new_second[...] = second_value


def swap(array, axis, size, bits):
    return lax.ppermute(array, axis, [(i, i ^ bits) for i in range(size)])


def local(
    users_list,
    items_list,
    days_list,
    status,
    user_factor,
    user_first,
    user_second,
    item_factor,
    item_first,
    item_second,
    day_factor,
    day_first,
    day_second,
):
    owners = lax.axis_size("dp")
    holders = lax.axis_size("mp")
    row_counts = (user_factor.shape[0], item_factor.shape[0], day_factor.shape[0])
    list_counts = (users_list.shape[1], items_list.shape[1], days_list.shape[1])
    sizes = Sizes(owners, holders, user_factor.shape[1], row_counts, list_counts)
    shape = jax.ShapeDtypeStruct
    small = pltpu.CompilerParams(vmem_limit_bytes=SMALL_VMEM)

    hbm = pl.BlockSpec(memory_space=pltpu.HBM)
    tables_in = (user_factor.T, item_factor.T, day_factor)
    piece = pl.pallas_call(
        functools.partial(pack_kernel, sizes),
        out_shape=shape((sizes.piece_rows, LANES), bf16),
        in_specs=[hbm] * 3,
        scratch_shapes=[pltpu.VMEM(a.shape, f32) for a in tables_in]
        + [pltpu.SemaphoreType.DMA((3,))],
        compiler_params=pltpu.CompilerParams(vmem_limit_bytes=PACK_VMEM),
        name="pack",
    )(*tables_in)
    pieces = [piece] + [swap(piece, "mp", holders, bits) for bits in range(1, holders)]

    picks_places_notes = pl.pallas_call(
        functools.partial(slot_kernel, sizes),
        out_shape=tuple(
            [shape((owners * row_counts[t], list_counts[t]), bf16) for t in range(3)]
            + [shape((owners * sizes.slots[t], list_counts[t]), bf16) for t in range(3)]
            + [shape((owners, sizes.rank), f32)]
        ),
        in_specs=[pl.BlockSpec(memory_space=pltpu.SMEM)] + [hbm] * 3,
        scratch_shapes=[pltpu.VMEM((1, count), jnp.int32) for count in list_counts]
        + [pltpu.SemaphoreType.DMA((3,))],
        compiler_params=small,
        name="slots",
    )(lax.axis_index("dp").astype(jnp.int32).reshape(1), users_list, items_list, days_list)

    table = pl.pallas_call(
        functools.partial(table_kernel, sizes),
        out_shape=shape((sizes.table_rows, LANES), bf16),
        compiler_params=small,
        name="table",
    )(*pieces, picks_places_notes[6])
    tables = {0: table}
    for bits in range(2, owners, 2):
        tables[bits] = swap(table, "dp", owners, bits)
    for bits in range(0, owners, 2):
        tables[bits + 1] = swap(tables[bits], "dp", owners, 1)

    inputs = [*[tables[bits] for bits in range(owners)], *picks_places_notes]
    users, items, days = list_counts
    steps = days // DAYS_PER_STEP
    half = shape((owners // 2 * sizes.slot_rows, sizes.rank), bf16)
    own, other = pl.pallas_call(
        functools.partial(block_kernel, sizes, DAYS_PER_STEP),
        out_shape=(half, half),
        in_specs=[pl.BlockSpec(memory_space=pltpu.VMEM)] * len(inputs) + [hbm],
        scratch_shapes=[
            pltpu.VMEM((users, sizes.rank), f32),
            pltpu.VMEM((items, sizes.rank), bf16),
            pltpu.VMEM((sizes.rank, items), bf16),
            pltpu.VMEM((days, sizes.rank), f32),
            pltpu.VMEM((users, sizes.rank), f32),
            pltpu.VMEM((items, sizes.rank), f32),
            pltpu.VMEM((days, sizes.rank), f32),
            pltpu.VMEM((days, users, items), jnp.int32),
            pltpu.SemaphoreType.DMA((steps,)),
        ],
        compiler_params=pltpu.CompilerParams(vmem_limit_bytes=BLOCK_VMEM),
        name="block_gradients",
    )(*inputs, status)
    crossed = swap(other, "dp", owners, 1)
    message = shape((2 * sizes.slot_rows, sizes.rank), bf16)
    merged = pl.pallas_call(
        functools.partial(merge_kernel, sizes),
        out_shape=tuple([message] * (owners // 2 - 1)),
        compiler_params=small,
        name="merge",
    )(own, crossed)
    returned = [own, crossed]
    returned += [swap(merged[bits // 2 - 1], "dp", owners, bits) for bits in range(2, owners, 2)]

    totals = pl.pallas_call(
        functools.partial(sum_kernel, sizes),
        out_shape=tuple([shape(piece.shape, bf16)] * holders),
        compiler_params=small,
        name="row_sums",
    )(*returned)
    column_totals = [totals[0]] + [
        swap(totals[bits], "mp", holders, bits) for bits in range(1, holders)
    ]

    states = (
        user_factor.T,
        user_first.T,
        user_second.T,
        item_factor.T,
        item_first.T,
        item_second.T,
        day_factor,
        day_first,
        day_second,
    )
    updated = pl.pallas_call(
        functools.partial(adam_kernel, sizes),
        out_shape=tuple(shape(a.shape, a.dtype) for a in states),
        compiler_params=small,
        name="adam",
    )(*column_totals, *states)
    return tuple(a.T for a in updated[:6]) + tuple(updated[6:])


def solution(mesh):
    block = P(("dp", "mp"), None)
    piece = P("dp", "mp")
    return jax.shard_map(
        local,
        mesh=mesh,
        in_specs=(block, block, block, P(("dp", "mp"), None, None, None)) + (piece,) * 9,
        out_specs=(piece,) * 9,
        check_vma=False,
    )
```

```python
import functools

import jax
import jax.numpy as jnp
from jax import lax
from jax.experimental import pallas as pl
from jax.experimental.pallas import tpu as pltpu
from jax.sharding import PartitionSpec as P

beta_one = 0.9
beta_two = 0.99
bias_one = 1.0 - 0.9**10
bias_two = 1.0 - 0.99**10
learn_rate = 0.01
epsilon = 1e-08
loss_scale = 0.0625

LANES = 128
SMALL_VMEM = 16 * 1024 * 1024
BLOCK_VMEM = 48 * 1024 * 1024
PACK_VMEM = 56 * 1024 * 1024

f32 = jnp.float32
bf16 = jnp.bfloat16


class Sizes:
    def __init__(self, owners, holders, columns, row_counts, list_counts):
        self.owners = owners
        self.holders = holders
        self.columns = columns
        self.rank = columns * holders
        self.row_counts = row_counts
        self.list_counts = list_counts
        limits = (
            max(2, 3 * list_counts[0] // (2 * owners)),
            max(2, 3 * list_counts[1] // (2 * owners)),
            max(2, 2 * list_counts[2] // owners),
        )
        self.slots = tuple(-(-(limit + t // 2) // 16) * 16 for t, limit in enumerate(limits))
        self.note_row = limits[2]
        self.slot_starts = (0, self.slots[0], self.slots[0] + self.slots[1])
        self.slot_rows = sum(self.slots)
        self.day_parts = LANES // columns
        self.day_packed = -(-(row_counts[2] // self.day_parts) // 16) * 16
        self.piece_rows = 2 * columns + self.day_packed
        self.day_chunks = self.rank // LANES
        self.table_rows = 2 * self.rank + self.day_chunks * row_counts[2]


def iota(shape, dimension):
    return lax.broadcasted_iota(jnp.int32, shape, dimension)


def onehot(condition):
    return jnp.where(condition, 1.0, 0.0).astype(bf16)


def dot_nt(a, b):
    return lax.dot_general(a, b, (((1,), (1,)), ((), ())), preferred_element_type=f32)


def pack_days(sizes, days):
    rows = sizes.row_counts[2] // sizes.day_parts
    parts = [days[p * rows : (p + 1) * rows] for p in range(sizes.day_parts)]
    if rows != sizes.day_packed:
        blank = jnp.zeros((sizes.day_packed - rows, days.shape[1]), days.dtype)
        parts = [jnp.concatenate([part, blank], axis=0) for part in parts]
    return jnp.concatenate(parts, axis=1)


def unpack_days(sizes, packed):
    rows = sizes.row_counts[2] // sizes.day_parts
    return jnp.concatenate(
        [
            packed[:rows, p * sizes.columns : (p + 1) * sizes.columns]
            for p in range(sizes.day_parts)
        ],
        axis=0,
    )


def fetch(sources, targets, semaphores):
    copies = [
        pltpu.make_async_copy(source, target, semaphores.at[n])
        for n, (source, target) in enumerate(zip(sources, targets))
    ]
    for copy in copies:
        copy.start()
    for copy in copies:
        copy.wait()


def pack_kernel(sizes, user_hbm, item_hbm, day_hbm, out_ref, user, item, day, semaphores):
    columns = sizes.columns
    fetch((user_hbm, item_hbm, day_hbm), (user, item, day), semaphores)
    out_ref[:columns, :] = user[...].astype(bf16)
    out_ref[columns : 2 * columns, :] = item[...].astype(bf16)
    out_ref[2 * columns :, :] = pack_days(sizes, day[...]).astype(bf16)


def slot_kernel(sizes, me_ref, *refs):
    owners = sizes.owners
    picks, places, note_ref, lists = refs[4:7], refs[7:10], refs[10], refs[11:14]
    fetch(refs[:3], lists, refs[14])
    me = me_ref[0]
    notes = [[] for _ in range(owners)]
    for t in range(3):
        count, rows, slots = sizes.list_counts[t], sizes.row_counts[t], sizes.slots[t]
        number = lists[t][...]
        owner = number // rows
        row = number % rows
        partner = lax.bitwise_xor(owner, jnp.full_like(owner, me))
        picks[t][...] = onehot(iota((owners * rows, count), 0) == partner * rows + row)
        earlier = onehot(iota((count, count), 0) < iota((count, count), 1))
        owner_hot = iota((owners, count), 0) == owner
        before = jnp.dot(onehot(owner_hot), earlier, preferred_element_type=f32)
        position = jnp.sum(jnp.where(owner_hot, before, 0.0), axis=0, keepdims=True)
        target = partner * slots + position.astype(jnp.int32)
        place = onehot(iota((owners * slots, count), 0) == target)
        places[t][...] = place
        following = (row + 1).astype(bf16)
        for s in range(owners):
            notes[s].append(dot_nt(following, place[s * slots : (s + 1) * slots]) - 1.0)
    blank = jnp.full((1, sizes.rank - sizes.slot_rows), -1.0, f32)
    note_ref[...] = jnp.concatenate(
        [jnp.concatenate(note + [blank], axis=1) for note in notes], axis=0
    )


def table_kernel(sizes, *refs):
    pieces, out_ref = refs[:-1], refs[-1]
    columns, rank, day_rows = sizes.columns, sizes.rank, sizes.row_counts[2]
    for j, ref in enumerate(pieces):
        for t in range(2):
            out_ref[t * rank + j * columns : t * rank + (j + 1) * columns, :] = ref[
                t * columns : (t + 1) * columns, :
            ]
    days = jnp.concatenate(
        [unpack_days(sizes, ref[2 * columns :, :].astype(f32)) for ref in pieces], axis=1
    ).astype(bf16)
    for chunk in range(sizes.day_chunks):
        start = 2 * rank + chunk * day_rows
        out_ref[start : start + day_rows, :] = days[:, chunk * LANES : (chunk + 1) * LANES]


def block_kernel(sizes, *refs):
    owners, rank, day_rows = sizes.owners, sizes.rank, sizes.row_counts[2]
    own_table, own_crossed, tables_ref, tables_crossed = refs[:4]
    picks, places = refs[4:7], refs[7:10]
    note_ref, status_hbm, own_ref, other_ref = refs[10:14]
    (
        users,
        users_low,
        items,
        items_half_t,
        days,
        user_gradient,
        item_gradient,
        day_gradient,
        scaled_even,
        scaled_odd,
        residual_even,
        residual_odd,
        status,
        semaphores,
    ) = refs[14:]
    pair = 2
    pairs = status.shape[0] // pair
    chunks = [(0, pair)]
    chunks += [((2 * n - 1) * pair, 2 * pair) for n in range(1, pairs // 2)]
    chunks += [((pairs - 1) * pair, pair)]

    def status_copy(start, size, semaphore):
        part = pl.ds(start, size)
        return pltpu.make_async_copy(
            status_hbm.at[0, part], status.at[part], semaphores.at[semaphore]
        )

    for n, (start, size) in enumerate(chunks):
        status_copy(start, size, n).start()

    height = sizes.table_rows
    tables = []
    for n in range(owners // 2):
        if n == 0:
            tables += [own_table, own_crossed]
        else:
            part = slice((n - 1) * height, n * height)
            tables += [tables_ref.at[part], tables_crossed.at[part]]

    def pick(t):
        table = jnp.concatenate([ref[t * rank : (t + 1) * rank, :] for ref in tables], axis=1)
        return jnp.dot(table, picks[t][...], preferred_element_type=f32)

    user_values = pick(0).T
    users[...] = user_values
    users_low[...] = user_values.astype(bf16)
    items_t = pick(1)
    items[...] = items_t.T.astype(bf16)
    items_half_t[...] = (0.5 * items_t).astype(bf16)
    starts = [2 * rank + chunk * day_rows for chunk in range(sizes.day_chunks)]
    day_table = jnp.concatenate(
        [
            jnp.concatenate([ref[start : start + day_rows, :] for start in starts], axis=1)
            for ref in tables
        ],
        axis=0,
    )
    days[...] = lax.dot_general(
        picks[2][...], day_table, (((0,), (0,)), ((), ())), preferred_element_type=f32
    )
    user_gradient[...] = jnp.zeros_like(user_gradient)
    item_gradient[...] = jnp.zeros_like(item_gradient)
    count = users.shape[0]

    def residuals(first, scaled, residual):
        for j in range(pair):
            rows = slice(j * count, (j + 1) * count)
            day = days[pl.ds(first + j, 1), :].astype(bf16)
            scaled_values = day * users_low[...]
            scaled[rows, :] = scaled_values
            half_logits = jnp.dot(scaled_values, items_half_t[...], preferred_element_type=f32)
            state = status[first + j]
            residual[rows, :] = (
                state.astype(f32) * (jnp.tanh(half_logits) + jnp.where(state == 1, -1.0, 1.0))
            ).astype(bf16)

    def gradients(first, scaled, residual):
        total = 0.0
        for j in range(pair):
            rows = slice(j * count, (j + 1) * count)
            day = days[pl.ds(first + j, 1), :]
            projected = jnp.dot(residual[rows, :], items[...], preferred_element_type=f32)
            total = total + projected * day
            day_gradient[pl.ds(first + j, 1), :] = jnp.sum(
                projected * users[...], axis=0, keepdims=True
            )
        user_gradient[...] += total
        item_gradient[...] += lax.dot_general(
            residual[...], scaled[...], (((0,), (0,)), ((), ())), preferred_element_type=f32
        )

    even, odd = (scaled_even, residual_even), (scaled_odd, residual_odd)
    status_copy(*chunks[0], 0).wait()
    residuals(0, *even)

    @pl.loop(0, pairs // 2 - 1)
    def _(n):
        first = 2 * n * pair
        status_copy(first + pair, 2 * pair, n + 1).wait()
        residuals(first + pair, *odd)
        gradients(first, *even)
        residuals(first + 2 * pair, *even)
        gradients(first + pair, *odd)

    last = (pairs - 1) * pair
    status_copy(*chunks[-1], len(chunks) - 1).wait()
    residuals(last, *odd)
    gradients(last - pair, *even)
    gradients(last, *odd)

    for t, gradient in enumerate((user_gradient, item_gradient, day_gradient)):
        start, slots = sizes.slot_starts[t], sizes.slots[t]
        values = (0.5 * loss_scale * gradient[...]).astype(bf16)
        placed = jnp.dot(places[t][...], values, preferred_element_type=f32)
        for s in range(owners):
            rows = placed[s * slots : (s + 1) * slots]
            if t == 2:
                note = iota(rows.shape, 0) == sizes.note_row
                rows = jnp.where(note, note_ref[s : s + 1, :], rows)
            out = (own_ref, other_ref)[s % 2]
            first = (s // 2) * sizes.slot_rows + start
            out[first : first + slots, :] = rows.astype(bf16)


def join_kernel(sizes, *refs):
    arrived, out_ref = refs[:-2], refs[-1]
    for n, ref in enumerate(arrived):
        out_ref[n * sizes.table_rows : (n + 1) * sizes.table_rows, :] = ref[...]


def merge_kernel(sizes, own_ref, crossed_ref, *outs):
    rows = sizes.slot_rows
    for n, out in enumerate(outs):
        start = (n + 1) * rows
        out[:rows, :] = own_ref[start : start + rows, :]
        out[rows:, :] = crossed_ref[start : start + rows, :]


def sum_kernel(sizes, *refs):
    holders, columns = sizes.holders, sizes.columns
    inputs = sizes.owners // 2 + 1
    arrived, outs = refs[:inputs], refs[inputs:]
    day_start = sizes.slot_starts[2]
    totals = [0.0, 0.0, 0.0]
    messages = [ref.at[: sizes.slot_rows] for ref in arrived]
    messages += [ref.at[sizes.slot_rows :] for ref in arrived[2:]]
    for ref in messages:
        notes = ref[day_start : day_start + sizes.slots[2], :].astype(f32)
        rows = notes[sizes.note_row : sizes.note_row + 1, : sizes.slot_rows].astype(jnp.int32)
        for t in range(3):
            start, slots = sizes.slot_starts[t], sizes.slots[t]
            shape = (sizes.row_counts[t], sizes.slot_rows)
            slot = iota(shape, 1)
            mine = (slot >= start) & (slot < start + slots)
            selector = onehot((iota(shape, 0) == rows) & mine)
            totals[t] = totals[t] + jnp.dot(selector, ref[...], preferred_element_type=f32)
    for t in range(3):
        if t < 2:
            turned = totals[t].T.astype(bf16)
            for j in range(holders):
                outs[j][t * columns : (t + 1) * columns, :] = turned[
                    j * columns : (j + 1) * columns
                ]
        else:
            for j in range(holders):
                outs[j][2 * columns :, :] = pack_days(
                    sizes, totals[t][:, j * columns : (j + 1) * columns]
                ).astype(bf16)


def adam_kernel(sizes, *refs):
    holders, columns = sizes.holders, sizes.columns
    pieces = refs[:holders]
    states = refs[holders : holders + 9]
    outs = refs[holders + 9 :]
    total = pieces[0][...].astype(f32)
    for ref in pieces[1:]:
        total = total + ref[...].astype(f32)
    for t in range(3):
        if t < 2:
            gradient = total[t * columns : (t + 1) * columns]
        else:
            gradient = unpack_days(sizes, total[2 * columns :])
        factor, first, second = states[3 * t : 3 * t + 3]
        new_factor, new_first, new_second = outs[3 * t : 3 * t + 3]
        first_value = beta_one * first[...] + (1.0 - beta_one) * gradient
        second_value = beta_two * second[...] + (1.0 - beta_two) * gradient * gradient
        change = (
            learn_rate
            * (first_value / bias_one)
            / (jnp.sqrt(second_value / bias_two) + epsilon)
        )
        new_factor[...] = factor[...] - change
        new_first[...] = first_value
        new_second[...] = second_value


def swap(array, axis, size, bits):
    return lax.ppermute(array, axis, [(i, i ^ bits) for i in range(size)])


def local(
    users_list,
    items_list,
    days_list,
    status,
    user_factor,
    user_first,
    user_second,
    item_factor,
    item_first,
    item_second,
    day_factor,
    day_first,
    day_second,
):
    owners = lax.axis_size("dp")
    holders = lax.axis_size("mp")
    row_counts = (user_factor.shape[0], item_factor.shape[0], day_factor.shape[0])
    list_counts = (users_list.shape[1], items_list.shape[1], days_list.shape[1])
    sizes = Sizes(owners, holders, user_factor.shape[1], row_counts, list_counts)
    shape = jax.ShapeDtypeStruct
    small = pltpu.CompilerParams(vmem_limit_bytes=SMALL_VMEM)

    hbm = pl.BlockSpec(memory_space=pltpu.HBM)
    tables_in = (user_factor.T, item_factor.T, day_factor)
    piece = pl.pallas_call(
        functools.partial(pack_kernel, sizes),
        out_shape=shape((sizes.piece_rows, LANES), bf16),
        in_specs=[hbm] * 3,
        scratch_shapes=[pltpu.VMEM(a.shape, f32) for a in tables_in]
        + [pltpu.SemaphoreType.DMA((3,))],
        compiler_params=pltpu.CompilerParams(vmem_limit_bytes=PACK_VMEM),
        name="pack",
    )(*tables_in)
    pieces = [piece] + [swap(piece, "mp", holders, bits) for bits in range(1, holders)]

    table = pl.pallas_call(
        functools.partial(table_kernel, sizes),
        out_shape=shape((sizes.table_rows, LANES), bf16),
        compiler_params=small,
        name="table",
    )(*pieces)
    arrived = [swap(table, "dp", owners, bits) for bits in range(2, owners, 2)]
    own_crossed = swap(table, "dp", owners, 1)
    picks_places_notes = pl.pallas_call(
        functools.partial(slot_kernel, sizes),
        out_shape=tuple(
            [shape((owners * row_counts[t], list_counts[t]), bf16) for t in range(3)]
            + [shape((owners * sizes.slots[t], list_counts[t]), bf16) for t in range(3)]
            + [shape((owners, sizes.rank), f32)]
        ),
        in_specs=[pl.BlockSpec(memory_space=pltpu.SMEM)] + [hbm] * 4,
        scratch_shapes=[pltpu.VMEM((1, count), jnp.int32) for count in list_counts]
        + [pltpu.SemaphoreType.DMA((3,))],
        compiler_params=small,
        name="slots",
    )(lax.axis_index("dp").astype(jnp.int32).reshape(1), users_list, items_list, days_list, table)

    joined = pl.pallas_call(
        functools.partial(join_kernel, sizes),
        out_shape=shape((len(arrived) * sizes.table_rows, LANES), bf16),
        compiler_params=small,
        name="join",
    )(*arrived, picks_places_notes[6])
    joined_crossed = swap(joined, "dp", owners, 1)

    inputs = [table, own_crossed, joined, joined_crossed, *picks_places_notes]
    users, items, days = list_counts
    half = shape((owners // 2 * sizes.slot_rows, sizes.rank), bf16)
    own, other = pl.pallas_call(
        functools.partial(block_kernel, sizes),
        out_shape=(half, half),
        in_specs=[pl.BlockSpec(memory_space=pltpu.VMEM)] * len(inputs) + [hbm],
        scratch_shapes=[
            pltpu.VMEM((users, sizes.rank), f32),
            pltpu.VMEM((users, sizes.rank), bf16),
            pltpu.VMEM((items, sizes.rank), bf16),
            pltpu.VMEM((sizes.rank, items), bf16),
            pltpu.VMEM((days, sizes.rank), f32),
            pltpu.VMEM((users, sizes.rank), f32),
            pltpu.VMEM((items, sizes.rank), f32),
            pltpu.VMEM((days, sizes.rank), f32),
            pltpu.VMEM((2 * users, sizes.rank), bf16),
            pltpu.VMEM((2 * users, sizes.rank), bf16),
            pltpu.VMEM((2 * users, items), bf16),
            pltpu.VMEM((2 * users, items), bf16),
            pltpu.VMEM((days, users, items), jnp.int32),
            pltpu.SemaphoreType.DMA((days // 4 + 1,)),
        ],
        compiler_params=pltpu.CompilerParams(vmem_limit_bytes=BLOCK_VMEM),
        name="block_gradients",
    )(*inputs, status)
    crossed = swap(other, "dp", owners, 1)
    message = shape((2 * sizes.slot_rows, sizes.rank), bf16)
    merged = pl.pallas_call(
        functools.partial(merge_kernel, sizes),
        out_shape=tuple([message] * (owners // 2 - 1)),
        compiler_params=small,
        name="merge",
    )(own, crossed)
    returned = [own, crossed]
    returned += [swap(merged[bits // 2 - 1], "dp", owners, bits) for bits in range(2, owners, 2)]

    totals = pl.pallas_call(
        functools.partial(sum_kernel, sizes),
        out_shape=tuple([shape(piece.shape, bf16)] * holders),
        compiler_params=small,
        name="row_sums",
    )(*returned)
    column_totals = [totals[0]] + [
        swap(totals[bits], "mp", holders, bits) for bits in range(1, holders)
    ]

    states = (
        user_factor.T,
        user_first.T,
        user_second.T,
        item_factor.T,
        item_first.T,
        item_second.T,
        day_factor,
        day_first,
        day_second,
    )
    updated = pl.pallas_call(
        functools.partial(adam_kernel, sizes),
        out_shape=tuple(shape(a.shape, a.dtype) for a in states),
        compiler_params=small,
        name="adam",
    )(*column_totals, *states)
    return tuple(a.T for a in updated[:6]) + tuple(updated[6:])


def solution(mesh):
    block = P(("dp", "mp"), None)
    piece = P("dp", "mp")
    return jax.shard_map(
        local,
        mesh=mesh,
        in_specs=(block, block, block, P(("dp", "mp"), None, None, None)) + (piece,) * 9,
        out_specs=(piece,) * 9,
        check_vma=False,
    )
```

```python
import functools

import jax
import jax.numpy as jnp
from jax import lax
from jax.experimental import pallas as pl
from jax.experimental.pallas import tpu as pltpu
from jax.sharding import PartitionSpec as P

beta_one = 0.9
beta_two = 0.99
bias_one = 1.0 - 0.9**10
bias_two = 1.0 - 0.99**10
learn_rate = 0.01
epsilon = 1e-08
loss_scale = 0.0625

LANES = 128
SMALL_VMEM = 16 * 1024 * 1024
BLOCK_VMEM = 48 * 1024 * 1024

f32 = jnp.float32
bf16 = jnp.bfloat16


class Sizes:
    def __init__(self, owners, holders, columns, row_counts, list_counts):
        self.owners = owners
        self.holders = holders
        self.columns = columns
        self.rank = columns * holders
        self.row_counts = row_counts
        self.list_counts = list_counts
        limits = (
            max(2, 3 * list_counts[0] // (2 * owners)),
            max(2, 3 * list_counts[1] // (2 * owners)),
            max(2, 2 * list_counts[2] // owners),
        )
        self.slots = tuple(-(-(limit + t // 2) // 16) * 16 for t, limit in enumerate(limits))
        self.note_row = limits[2]
        self.slot_starts = (0, self.slots[0], self.slots[0] + self.slots[1])
        self.slot_rows = sum(self.slots)
        self.day_parts = LANES // columns
        self.day_packed = -(-(row_counts[2] // self.day_parts) // 16) * 16
        self.piece_rows = 2 * columns + self.day_packed
        self.day_chunks = self.rank // LANES
        self.table_rows = 2 * self.rank + self.day_chunks * row_counts[2]


def iota(shape, dimension):
    return lax.broadcasted_iota(jnp.int32, shape, dimension)


def onehot(condition):
    return jnp.where(condition, 1.0, 0.0).astype(bf16)


def dot_nt(a, b):
    return lax.dot_general(a, b, (((1,), (1,)), ((), ())), preferred_element_type=f32)


def pack_days(sizes, days):
    rows = sizes.row_counts[2] // sizes.day_parts
    parts = [days[p * rows : (p + 1) * rows] for p in range(sizes.day_parts)]
    if rows != sizes.day_packed:
        blank = jnp.zeros((sizes.day_packed - rows, days.shape[1]), days.dtype)
        parts = [jnp.concatenate([part, blank], axis=0) for part in parts]
    return jnp.concatenate(parts, axis=1)


def unpack_days(sizes, packed):
    rows = sizes.row_counts[2] // sizes.day_parts
    return jnp.concatenate(
        [
            packed[:rows, p * sizes.columns : (p + 1) * sizes.columns]
            for p in range(sizes.day_parts)
        ],
        axis=0,
    )


def fetch(sources, targets, semaphores):
    copies = [
        pltpu.make_async_copy(source, target, semaphores.at[n])
        for n, (source, target) in enumerate(zip(sources, targets))
    ]
    for copy in copies:
        copy.start()
    for copy in copies:
        copy.wait()


def pack_kernel(sizes, user_hbm, item_hbm, day_hbm, out_ref, user, item, day, semaphores):
    columns = sizes.columns
    fetch((user_hbm, item_hbm, day_hbm), (user, item, day), semaphores)
    out_ref[:columns, :] = user[...].astype(bf16)
    out_ref[columns : 2 * columns, :] = item[...].astype(bf16)
    out_ref[2 * columns :, :] = pack_days(sizes, day[...]).astype(bf16)


def slot_kernel(sizes, me_ref, *refs):
    owners = sizes.owners
    picks, places, note_ref, lists = refs[4:7], refs[7:10], refs[10], refs[11:14]
    fetch(refs[:3], lists, refs[14])
    me = me_ref[0]
    notes = [[] for _ in range(owners)]
    for t in range(3):
        count, rows, slots = sizes.list_counts[t], sizes.row_counts[t], sizes.slots[t]
        number = lists[t][...]
        owner = number // rows
        row = number % rows
        partner = lax.bitwise_xor(owner, jnp.full_like(owner, me))
        picks[t][...] = onehot(iota((owners * rows, count), 0) == partner * rows + row)
        earlier = onehot(iota((count, count), 0) < iota((count, count), 1))
        owner_hot = iota((owners, count), 0) == owner
        before = jnp.dot(onehot(owner_hot), earlier, preferred_element_type=f32)
        position = jnp.sum(jnp.where(owner_hot, before, 0.0), axis=0, keepdims=True)
        target = partner * slots + position.astype(jnp.int32)
        place = onehot(iota((owners * slots, count), 0) == target)
        places[t][...] = place
        following = (row + 1).astype(bf16)
        for s in range(owners):
            notes[s].append(dot_nt(following, place[s * slots : (s + 1) * slots]) - 1.0)
    blank = jnp.full((1, sizes.rank - sizes.slot_rows), -1.0, f32)
    note_ref[...] = jnp.concatenate(
        [jnp.concatenate(note + [blank], axis=1) for note in notes], axis=0
    )


def table_kernel(sizes, *refs):
    pieces, out_ref = refs[-2::-1], refs[-1]
    columns, rank, day_rows = sizes.columns, sizes.rank, sizes.row_counts[2]
    for j, ref in enumerate(pieces):
        for t in range(2):
            out_ref[t * rank + j * columns : t * rank + (j + 1) * columns, :] = ref[
                t * columns : (t + 1) * columns, :
            ]
    days = jnp.concatenate(
        [unpack_days(sizes, ref[2 * columns :, :].astype(f32)) for ref in pieces], axis=1
    ).astype(bf16)
    for chunk in range(sizes.day_chunks):
        start = 2 * rank + chunk * day_rows
        out_ref[start : start + day_rows, :] = days[:, chunk * LANES : (chunk + 1) * LANES]


def block_kernel(sizes, *refs):
    owners, rank, day_rows = sizes.owners, sizes.rank, sizes.row_counts[2]
    own_table, own_crossed, tables_ref, tables_crossed = refs[:4]
    picks, places = refs[4:7], refs[7:10]
    note_ref, status_hbm, own_ref, other_ref = refs[10:14]
    (
        users,
        users_low,
        items,
        items_half_t,
        days,
        user_gradient,
        item_gradient,
        day_gradient,
        scaled_even,
        scaled_odd,
        residual_even,
        residual_odd,
        status,
        semaphores,
    ) = refs[14:]
    pair = 2
    pairs = status.shape[0] // pair
    chunks = [(0, pair)]
    chunks += [((2 * n - 1) * pair, 2 * pair) for n in range(1, pairs // 2)]
    chunks += [((pairs - 1) * pair, pair)]

    def status_copy(start, size, semaphore):
        part = pl.ds(start, size)
        return pltpu.make_async_copy(
            status_hbm.at[0, part], status.at[part], semaphores.at[semaphore]
        )

    for n, (start, size) in enumerate(chunks):
        status_copy(start, size, n).start()

    height = sizes.table_rows
    tables = []
    for n in range(owners // 2):
        if n == 0:
            tables += [own_table, own_crossed]
        else:
            part = slice((n - 1) * height, n * height)
            tables += [tables_ref.at[part], tables_crossed.at[part]]

    def pick(t):
        table = jnp.concatenate([ref[t * rank : (t + 1) * rank, :] for ref in tables], axis=1)
        return jnp.dot(table, picks[t][...], preferred_element_type=f32)

    user_values = pick(0).T
    users[...] = user_values
    users_low[...] = user_values.astype(bf16)
    items_t = pick(1)
    items[...] = items_t.T.astype(bf16)
    items_half_t[...] = (0.5 * items_t).astype(bf16)
    starts = [2 * rank + chunk * day_rows for chunk in range(sizes.day_chunks)]
    day_table = jnp.concatenate(
        [
            jnp.concatenate([ref[start : start + day_rows, :] for start in starts], axis=1)
            for ref in tables
        ],
        axis=0,
    )
    days[...] = lax.dot_general(
        picks[2][...], day_table, (((0,), (0,)), ((), ())), preferred_element_type=f32
    )
    user_gradient[...] = jnp.zeros_like(user_gradient)
    item_gradient[...] = jnp.zeros_like(item_gradient)
    count = users.shape[0]

    def residuals(first, scaled, residual):
        for j in range(pair):
            rows = slice(j * count, (j + 1) * count)
            day = days[pl.ds(first + j, 1), :].astype(bf16)
            scaled_values = day * users_low[...]
            scaled[rows, :] = scaled_values
            half_logits = jnp.dot(scaled_values, items_half_t[...], preferred_element_type=f32)
            state = status[first + j]
            residual[rows, :] = (
                state.astype(f32) * (jnp.tanh(half_logits) + jnp.where(state == 1, -1.0, 1.0))
            ).astype(bf16)

    def gradients(first, scaled, residual):
        total = 0.0
        for j in range(pair):
            rows = slice(j * count, (j + 1) * count)
            day = days[pl.ds(first + j, 1), :]
            projected = jnp.dot(residual[rows, :], items[...], preferred_element_type=f32)
            total = total + projected * day
            day_gradient[pl.ds(first + j, 1), :] = jnp.sum(
                projected * users[...], axis=0, keepdims=True
            )
        user_gradient[...] += total
        item_gradient[...] += lax.dot_general(
            residual[...], scaled[...], (((0,), (0,)), ((), ())), preferred_element_type=f32
        )

    even, odd = (scaled_even, residual_even), (scaled_odd, residual_odd)
    status_copy(*chunks[0], 0).wait()
    residuals(0, *even)

    @pl.loop(0, pairs // 2 - 1)
    def _(n):
        first = 2 * n * pair
        status_copy(first + pair, 2 * pair, n + 1).wait()
        residuals(first + pair, *odd)
        gradients(first, *even)
        residuals(first + 2 * pair, *even)
        gradients(first + pair, *odd)

    last = (pairs - 1) * pair
    status_copy(*chunks[-1], len(chunks) - 1).wait()
    residuals(last, *odd)
    gradients(last - pair, *even)
    gradients(last, *odd)

    for t, gradient in enumerate((user_gradient, item_gradient, day_gradient)):
        start, slots = sizes.slot_starts[t], sizes.slots[t]
        values = (0.5 * loss_scale * gradient[...]).astype(bf16)
        placed = jnp.dot(places[t][...], values, preferred_element_type=f32)
        for s in range(owners):
            rows = placed[s * slots : (s + 1) * slots]
            if t == 2:
                note = iota(rows.shape, 0) == sizes.note_row
                rows = jnp.where(note, note_ref[s : s + 1, :], rows)
            out = (own_ref, other_ref)[s % 2]
            first = (s // 2) * sizes.slot_rows + start
            out[first : first + slots, :] = rows.astype(bf16)


def join_kernel(sizes, *refs):
    arrived, out_ref = refs[:-2], refs[-1]
    for n, ref in enumerate(arrived[::-1]):
        out_ref[n * sizes.table_rows : (n + 1) * sizes.table_rows, :] = ref[...]


def merge_kernel(sizes, own_ref, crossed_ref, *outs):
    rows = sizes.slot_rows
    for n, out in enumerate(outs):
        start = (n + 1) * rows
        out[:rows, :] = own_ref[start : start + rows, :]
        out[rows:, :] = crossed_ref[start : start + rows, :]


def sum_kernel(sizes, *refs):
    holders, columns = sizes.holders, sizes.columns
    inputs = sizes.owners // 2 + 1
    arrived, outs = refs[:inputs], refs[inputs:]
    day_start = sizes.slot_starts[2]
    totals = [0.0, 0.0, 0.0]
    messages = [ref.at[: sizes.slot_rows] for ref in arrived]
    messages += [ref.at[sizes.slot_rows :] for ref in arrived[2:]]
    for ref in messages:
        notes = ref[day_start : day_start + sizes.slots[2], :].astype(f32)
        rows = notes[sizes.note_row : sizes.note_row + 1, : sizes.slot_rows].astype(jnp.int32)
        for t in range(3):
            start, slots = sizes.slot_starts[t], sizes.slots[t]
            shape = (sizes.row_counts[t], sizes.slot_rows)
            slot = iota(shape, 1)
            mine = (slot >= start) & (slot < start + slots)
            selector = onehot((iota(shape, 0) == rows) & mine)
            totals[t] = totals[t] + jnp.dot(selector, ref[...], preferred_element_type=f32)
    for t in range(3):
        if t < 2:
            turned = totals[t].T.astype(bf16)
            for j in range(holders):
                outs[j][t * columns : (t + 1) * columns, :] = turned[
                    j * columns : (j + 1) * columns
                ]
        else:
            for j in range(holders):
                outs[j][2 * columns :, :] = pack_days(
                    sizes, totals[t][:, j * columns : (j + 1) * columns]
                ).astype(bf16)


def adam_kernel(sizes, *refs):
    holders, columns = sizes.holders, sizes.columns
    pieces = refs[:holders]
    states = refs[holders : holders + 9]
    outs = refs[holders + 9 :]
    total = pieces[0][...].astype(f32)
    for ref in pieces[1:]:
        total = total + ref[...].astype(f32)
    for t in range(3):
        if t < 2:
            gradient = total[t * columns : (t + 1) * columns]
        else:
            gradient = unpack_days(sizes, total[2 * columns :])
        factor, first, second = states[3 * t : 3 * t + 3]
        new_factor, new_first, new_second = outs[3 * t : 3 * t + 3]
        first_value = beta_one * first[...] + (1.0 - beta_one) * gradient
        second_value = beta_two * second[...] + (1.0 - beta_two) * gradient * gradient
        change = (
            learn_rate
            * (first_value / bias_one)
            / (jnp.sqrt(second_value / bias_two) + epsilon)
        )
        new_factor[...] = factor[...] - change
        new_first[...] = first_value
        new_second[...] = second_value


def swap(array, axis, size, bits):
    return lax.ppermute(array, axis, [(i, i ^ bits) for i in range(size)])


def local(
    users_list,
    items_list,
    days_list,
    status,
    user_factor,
    user_first,
    user_second,
    item_factor,
    item_first,
    item_second,
    day_factor,
    day_first,
    day_second,
):
    owners = lax.axis_size("dp")
    holders = lax.axis_size("mp")
    row_counts = (user_factor.shape[0], item_factor.shape[0], day_factor.shape[0])
    list_counts = (users_list.shape[1], items_list.shape[1], days_list.shape[1])
    sizes = Sizes(owners, holders, user_factor.shape[1], row_counts, list_counts)
    shape = jax.ShapeDtypeStruct
    small = pltpu.CompilerParams(vmem_limit_bytes=SMALL_VMEM)

    hbm = pl.BlockSpec(memory_space=pltpu.HBM)
    in_hbm = lambda a: pltpu.with_memory_space_constraint(a, pltpu.HBM)
    tables_in = (user_factor.T, item_factor.T, day_factor)
    piece = pl.pallas_call(
        functools.partial(pack_kernel, sizes),
        out_shape=shape((sizes.piece_rows, LANES), bf16),
        in_specs=[hbm] * 3,
        scratch_shapes=[pltpu.VMEM(a.shape, f32) for a in tables_in]
        + [pltpu.SemaphoreType.DMA((3,))],
        compiler_params=small,
        name="pack",
    )(*[in_hbm(a) for a in tables_in])
    pieces = [swap(piece, "mp", holders, bits) for bits in range(holders - 1, 0, -1)] + [piece]

    table = pl.pallas_call(
        functools.partial(table_kernel, sizes),
        out_shape=shape((sizes.table_rows, LANES), bf16),
        compiler_params=small,
        name="table",
    )(*pieces)
    arrived = [swap(table, "dp", owners, bits) for bits in range(owners - 2, 0, -2)]
    own_crossed = swap(table, "dp", owners, 1)
    picks_places_notes = pl.pallas_call(
        functools.partial(slot_kernel, sizes),
        out_shape=tuple(
            [shape((owners * row_counts[t], list_counts[t]), bf16) for t in range(3)]
            + [shape((owners * sizes.slots[t], list_counts[t]), bf16) for t in range(3)]
            + [shape((owners, sizes.rank), f32)]
        ),
        in_specs=[pl.BlockSpec(memory_space=pltpu.SMEM)]
        + [hbm] * 3
        + [pl.BlockSpec(memory_space=pl.ANY)],
        scratch_shapes=[pltpu.VMEM((1, count), jnp.int32) for count in list_counts]
        + [pltpu.SemaphoreType.DMA((3,))],
        compiler_params=small,
        name="slots",
    )(
        lax.axis_index("dp").astype(jnp.int32).reshape(1),
        *[in_hbm(a) for a in (users_list, items_list, days_list)],
        table,
    )

    joined = pl.pallas_call(
        functools.partial(join_kernel, sizes),
        out_shape=shape((len(arrived) * sizes.table_rows, LANES), bf16),
        compiler_params=small,
        name="join",
    )(*arrived, picks_places_notes[6])
    joined_crossed = swap(joined, "dp", owners, 1)

    inputs = [table, own_crossed, joined, joined_crossed, *picks_places_notes]
    users, items, days = list_counts
    half = shape((owners // 2 * sizes.slot_rows, sizes.rank), bf16)
    own, other = pl.pallas_call(
        functools.partial(block_kernel, sizes),
        out_shape=(half, half),
        in_specs=[pl.BlockSpec(memory_space=pltpu.VMEM)] * len(inputs) + [hbm],
        scratch_shapes=[
            pltpu.VMEM((users, sizes.rank), f32),
            pltpu.VMEM((users, sizes.rank), bf16),
            pltpu.VMEM((items, sizes.rank), bf16),
            pltpu.VMEM((sizes.rank, items), bf16),
            pltpu.VMEM((days, sizes.rank), f32),
            pltpu.VMEM((users, sizes.rank), f32),
            pltpu.VMEM((items, sizes.rank), f32),
            pltpu.VMEM((days, sizes.rank), f32),
            pltpu.VMEM((2 * users, sizes.rank), bf16),
            pltpu.VMEM((2 * users, sizes.rank), bf16),
            pltpu.VMEM((2 * users, items), bf16),
            pltpu.VMEM((2 * users, items), bf16),
            pltpu.VMEM((days, users, items), jnp.int32),
            pltpu.SemaphoreType.DMA((days // 4 + 1,)),
        ],
        compiler_params=pltpu.CompilerParams(vmem_limit_bytes=BLOCK_VMEM),
        name="block_gradients",
    )(*inputs, in_hbm(status))
    crossed = swap(other, "dp", owners, 1)
    message = shape((2 * sizes.slot_rows, sizes.rank), bf16)
    merged = pl.pallas_call(
        functools.partial(merge_kernel, sizes),
        out_shape=tuple([message] * (owners // 2 - 1)),
        compiler_params=small,
        name="merge",
    )(own, crossed)
    returned = [own, crossed]
    returned += [swap(merged[bits // 2 - 1], "dp", owners, bits) for bits in range(2, owners, 2)]

    totals = pl.pallas_call(
        functools.partial(sum_kernel, sizes),
        out_shape=tuple([shape(piece.shape, bf16)] * holders),
        compiler_params=small,
        name="row_sums",
    )(*returned)
    column_totals = [totals[0]] + [
        swap(totals[bits], "mp", holders, bits) for bits in range(1, holders)
    ]

    states = (
        user_factor.T,
        user_first.T,
        user_second.T,
        item_factor.T,
        item_first.T,
        item_second.T,
        day_factor,
        day_first,
        day_second,
    )
    updated = pl.pallas_call(
        functools.partial(adam_kernel, sizes),
        out_shape=tuple(shape(a.shape, a.dtype) for a in states),
        compiler_params=small,
        name="adam",
    )(*column_totals, *states)
    return tuple(a.T for a in updated[:6]) + tuple(updated[6:])


def solution(mesh):
    block = P(("dp", "mp"), None)
    piece = P("dp", "mp")
    return jax.shard_map(
        local,
        mesh=mesh,
        in_specs=(block, block, block, P(("dp", "mp"), None, None, None)) + (piece,) * 9,
        out_specs=(piece,) * 9,
        check_vma=False,
    )
```

```python
import functools

import jax
import jax.numpy as jnp
from jax import lax
from jax.experimental import pallas as pl
from jax.experimental.pallas import tpu as pltpu
from jax.sharding import PartitionSpec as P

beta_one = 0.9
beta_two = 0.99
bias_one = 1.0 - 0.9**10
bias_two = 1.0 - 0.99**10
learn_rate = 0.01
epsilon = 1e-08
loss_scale = 0.0625

LANES = 128
SMALL_VMEM = 16 * 1024 * 1024
BLOCK_VMEM = 48 * 1024 * 1024

f32 = jnp.float32
bf16 = jnp.bfloat16


class Sizes:
    def __init__(self, owners, holders, columns, row_counts, list_counts):
        self.owners = owners
        self.folded = owners == 8
        self.holders = holders
        self.columns = columns
        self.rank = columns * holders
        self.row_counts = row_counts
        self.list_counts = list_counts
        limits = (
            max(2, 3 * list_counts[0] // (2 * owners)),
            max(2, 3 * list_counts[1] // (2 * owners)),
            max(2, 2 * list_counts[2] // owners),
        )
        self.slots = tuple(-(-(limit + t // 2) // 16) * 16 for t, limit in enumerate(limits))
        self.note_row = limits[2]
        self.slot_starts = (0, self.slots[0], self.slots[0] + self.slots[1])
        self.slot_rows = sum(self.slots)
        self.day_parts = LANES // columns
        self.day_packed = -(-(row_counts[2] // self.day_parts) // 16) * 16
        self.piece_rows = 2 * columns + self.day_packed
        self.day_chunks = self.rank // LANES
        self.table_rows = 2 * self.rank + self.day_chunks * row_counts[2]


def iota(shape, dimension):
    return lax.broadcasted_iota(jnp.int32, shape, dimension)


def onehot(condition):
    return jnp.where(condition, 1.0, 0.0).astype(bf16)


def dot_nt(a, b):
    return lax.dot_general(a, b, (((1,), (1,)), ((), ())), preferred_element_type=f32)


def pack_days(sizes, days):
    rows = sizes.row_counts[2] // sizes.day_parts
    parts = [days[p * rows : (p + 1) * rows] for p in range(sizes.day_parts)]
    if rows != sizes.day_packed:
        blank = jnp.zeros((sizes.day_packed - rows, days.shape[1]), days.dtype)
        parts = [jnp.concatenate([part, blank], axis=0) for part in parts]
    return jnp.concatenate(parts, axis=1)


def unpack_days(sizes, packed):
    rows = sizes.row_counts[2] // sizes.day_parts
    return jnp.concatenate(
        [
            packed[:rows, p * sizes.columns : (p + 1) * sizes.columns]
            for p in range(sizes.day_parts)
        ],
        axis=0,
    )


def fetch(sources, targets, semaphores):
    copies = [
        pltpu.make_async_copy(source, target, semaphores.at[n])
        for n, (source, target) in enumerate(zip(sources, targets))
    ]
    for copy in copies:
        copy.start()
    for copy in copies:
        copy.wait()


def pack_kernel(sizes, user_hbm, item_hbm, day_hbm, out_ref, user, item, day, semaphores):
    columns = sizes.columns
    fetch((user_hbm, item_hbm, day_hbm), (user, item, day), semaphores)
    out_ref[:columns, :] = user[...].astype(bf16)
    out_ref[columns : 2 * columns, :] = item[...].astype(bf16)
    out_ref[2 * columns :, :] = pack_days(sizes, day[...]).astype(bf16)


def place_of(sizes, owner, me):
    apart = lax.bitwise_xor(owner, jnp.full_like(owner, me))
    other_core = apart % 2
    chip = apart // 2
    if sizes.folded:
        core = (other_core + me) % 2
        along_x = jnp.where(core == 0, 2, 1)
        chip = jnp.where(chip == 1, along_x, jnp.where(chip == 2, 3 - along_x, chip))
    return other_core * (sizes.owners // 2) + chip


def slot_kernel(sizes, me_ref, *refs):
    owners = sizes.owners
    picks, places, note_ref, lists = refs[4:7], refs[7:10], refs[10], refs[11:14]
    fetch(refs[:3], lists, refs[14])
    me = me_ref[0]
    notes = [[] for _ in range(owners)]
    for t in range(3):
        count, rows, slots = sizes.list_counts[t], sizes.row_counts[t], sizes.slots[t]
        number = lists[t][...]
        owner = number // rows
        row = number % rows
        partner = place_of(sizes, owner, me)
        picks[t][...] = onehot(iota((owners * rows, count), 0) == partner * rows + row)
        earlier = onehot(iota((count, count), 0) < iota((count, count), 1))
        owner_hot = iota((owners, count), 0) == owner
        before = jnp.dot(onehot(owner_hot), earlier, preferred_element_type=f32)
        position = jnp.sum(jnp.where(owner_hot, before, 0.0), axis=0, keepdims=True)
        target = partner * slots + position.astype(jnp.int32)
        place = onehot(iota((owners * slots, count), 0) == target)
        places[t][...] = place
        following = (row + 1).astype(bf16)
        for s in range(owners):
            notes[s].append(dot_nt(following, place[s * slots : (s + 1) * slots]) - 1.0)
    blank = jnp.full((1, sizes.rank - sizes.slot_rows), -1.0, f32)
    note_ref[...] = jnp.concatenate(
        [jnp.concatenate(note + [blank], axis=1) for note in notes], axis=0
    )


def table_kernel(sizes, *refs):
    pieces, out_ref = refs[-2::-1], refs[-1]
    columns, rank, day_rows = sizes.columns, sizes.rank, sizes.row_counts[2]
    for j, ref in enumerate(pieces):
        for t in range(2):
            out_ref[t * rank + j * columns : t * rank + (j + 1) * columns, :] = ref[
                t * columns : (t + 1) * columns, :
            ]
    days = jnp.concatenate(
        [unpack_days(sizes, ref[2 * columns :, :].astype(f32)) for ref in pieces], axis=1
    ).astype(bf16)
    for chunk in range(sizes.day_chunks):
        start = 2 * rank + chunk * day_rows
        out_ref[start : start + day_rows, :] = days[:, chunk * LANES : (chunk + 1) * LANES]


def block_kernel(sizes, *refs):
    owners, rank, day_rows = sizes.owners, sizes.rank, sizes.row_counts[2]
    tables, refs = refs[:owners], refs[owners:]
    picks, places = refs[:3], refs[3:6]
    note_ref, status_hbm, own_ref, other_ref = refs[6:10]
    (
        users,
        users_low,
        items,
        items_half_t,
        days,
        user_gradient,
        item_gradient,
        day_gradient,
        scaled_even,
        scaled_odd,
        residual_even,
        residual_odd,
        status,
        semaphores,
    ) = refs[10:]
    pair = 2
    pairs = status.shape[0] // pair
    chunks = [(0, pair)]
    chunks += [((2 * n - 1) * pair, 2 * pair) for n in range(1, pairs // 2)]
    chunks += [((pairs - 1) * pair, pair)]

    def status_copy(start, size, semaphore):
        part = pl.ds(start, size)
        return pltpu.make_async_copy(
            status_hbm.at[0, part], status.at[part], semaphores.at[semaphore]
        )

    for n, (start, size) in enumerate(chunks):
        status_copy(start, size, n).start()

    def pick(t):
        table = jnp.concatenate([ref[t * rank : (t + 1) * rank, :] for ref in tables], axis=1)
        return jnp.dot(table, picks[t][...], preferred_element_type=f32)

    user_values = pick(0).T
    users[...] = user_values
    users_low[...] = user_values.astype(bf16)
    items_t = pick(1)
    items[...] = items_t.T.astype(bf16)
    items_half_t[...] = (0.5 * items_t).astype(bf16)
    starts = [2 * rank + chunk * day_rows for chunk in range(sizes.day_chunks)]
    day_table = jnp.concatenate(
        [
            jnp.concatenate([ref[start : start + day_rows, :] for start in starts], axis=1)
            for ref in tables
        ],
        axis=0,
    )
    days[...] = lax.dot_general(
        picks[2][...], day_table, (((0,), (0,)), ((), ())), preferred_element_type=f32
    )
    user_gradient[...] = jnp.zeros_like(user_gradient)
    item_gradient[...] = jnp.zeros_like(item_gradient)
    count = users.shape[0]

    def residuals(first, scaled, residual):
        for j in range(pair):
            rows = slice(j * count, (j + 1) * count)
            day = days[pl.ds(first + j, 1), :].astype(bf16)
            scaled_values = day * users_low[...]
            scaled[rows, :] = scaled_values
            half_logits = jnp.dot(scaled_values, items_half_t[...], preferred_element_type=f32)
            state = status[first + j]
            residual[rows, :] = (
                state.astype(f32) * (jnp.tanh(half_logits) + jnp.where(state == 1, -1.0, 1.0))
            ).astype(bf16)

    def gradients(first, scaled, residual):
        total = 0.0
        for j in range(pair):
            rows = slice(j * count, (j + 1) * count)
            day = days[pl.ds(first + j, 1), :]
            projected = jnp.dot(residual[rows, :], items[...], preferred_element_type=f32)
            total = total + projected * day
            day_gradient[pl.ds(first + j, 1), :] = jnp.sum(
                projected * users[...], axis=0, keepdims=True
            )
        user_gradient[...] += total
        item_gradient[...] += lax.dot_general(
            residual[...], scaled[...], (((0,), (0,)), ((), ())), preferred_element_type=f32
        )

    even, odd = (scaled_even, residual_even), (scaled_odd, residual_odd)
    status_copy(*chunks[0], 0).wait()
    residuals(0, *even)

    @pl.loop(0, pairs // 2 - 1)
    def _(n):
        first = 2 * n * pair
        status_copy(first + pair, 2 * pair, n + 1).wait()
        residuals(first + pair, *odd)
        gradients(first, *even)
        residuals(first + 2 * pair, *even)
        gradients(first + pair, *odd)

    last = (pairs - 1) * pair
    status_copy(*chunks[-1], len(chunks) - 1).wait()
    residuals(last, *odd)
    gradients(last - pair, *even)
    gradients(last, *odd)

    for t, gradient in enumerate((user_gradient, item_gradient, day_gradient)):
        start, slots = sizes.slot_starts[t], sizes.slots[t]
        values = (0.5 * loss_scale * gradient[...]).astype(bf16)
        placed = jnp.dot(places[t][...], values, preferred_element_type=f32)
        for s in range(owners):
            rows = placed[s * slots : (s + 1) * slots]
            if t == 2:
                note = iota(rows.shape, 0) == sizes.note_row
                rows = jnp.where(note, note_ref[s : s + 1, :], rows)
            out = (own_ref, other_ref)[2 * s // owners]
            first = (s % (owners // 2)) * sizes.slot_rows + start
            out[first : first + slots, :] = rows.astype(bf16)


def hold_kernel(arrived_ref, note_ref, out_ref):
    out_ref[...] = arrived_ref[...]


def merge_kernel(sizes, parts, own_ref, crossed_ref, *outs):
    rows = sizes.slot_rows
    for part, out in zip(parts, outs):
        start = part * rows
        out[:rows, :] = own_ref[start : start + rows, :]
        out[rows:, :] = crossed_ref[start : start + rows, :]


def sum_messages(sizes, messages):
    day_start = sizes.slot_starts[2]
    totals = [0.0, 0.0, 0.0]
    for ref in messages:
        notes = ref[day_start : day_start + sizes.slots[2], :].astype(f32)
        rows = notes[sizes.note_row : sizes.note_row + 1, : sizes.slot_rows].astype(jnp.int32)
        for t in range(3):
            start, slots = sizes.slot_starts[t], sizes.slots[t]
            shape = (sizes.row_counts[t], sizes.slot_rows)
            slot = iota(shape, 1)
            mine = (slot >= start) & (slot < start + slots)
            selector = onehot((iota(shape, 0) == rows) & mine)
            totals[t] = totals[t] + jnp.dot(selector, ref[...], preferred_element_type=f32)
    columns = sizes.columns
    users, items = totals[0].T, totals[1].T
    pieces = []
    for j in range(sizes.holders):
        part = slice(j * columns, (j + 1) * columns)
        pieces.append((users[part], items[part], pack_days(sizes, totals[2][:, part])))
    return pieces


def fold_kernel(sizes, start, own_ref, crossed_ref, arrived_ref, *outs):
    rows, columns = sizes.slot_rows, sizes.columns
    messages = [own_ref.at[start : start + rows], crossed_ref.at[start : start + rows]]
    messages += [arrived_ref.at[:rows], arrived_ref.at[rows:]]
    for j, (users, items, days) in enumerate(sum_messages(sizes, messages)):
        out_ref = outs[j * len(outs) // sizes.holders]
        first = j % (sizes.holders // len(outs)) * sizes.piece_rows
        out_ref[first : first + columns, :] = users.astype(bf16)
        out_ref[first + columns : first + 2 * columns, :] = items.astype(bf16)
        out_ref[first + 2 * columns : first + sizes.piece_rows, :] = days.astype(bf16)


def sum_kernel(sizes, inputs, *refs):
    rows, columns = sizes.slot_rows, sizes.columns
    arrived, outs = refs[:inputs], refs[inputs:]
    folded = ()
    if sizes.folded:
        arrived, folded = arrived[:-2], arrived[-2:]
    messages = [ref.at[:rows] for ref in arrived]
    messages += [ref.at[rows:] for ref in arrived[2:]]
    for j, piece in enumerate(sum_messages(sizes, messages)):
        starts = (0, columns, 2 * columns, sizes.piece_rows)
        for t in range(3):
            total = piece[t]
            if folded:
                ref = folded[j * len(folded) // sizes.holders]
                first = j % (sizes.holders // len(folded)) * sizes.piece_rows
                total = total + ref[first + starts[t] : first + starts[t + 1], :].astype(f32)
            outs[j][starts[t] : starts[t + 1], :] = total.astype(bf16)


def adam_kernel(sizes, *refs):
    holders, columns = sizes.holders, sizes.columns
    pieces = refs[:holders]
    states = refs[holders : holders + 9]
    outs = refs[holders + 9 :]
    total = pieces[0][...].astype(f32)
    for ref in pieces[1:]:
        total = total + ref[...].astype(f32)
    for t in range(3):
        if t < 2:
            gradient = total[t * columns : (t + 1) * columns]
        else:
            gradient = unpack_days(sizes, total[2 * columns :])
        factor, first, second = states[3 * t : 3 * t + 3]
        new_factor, new_first, new_second = outs[3 * t : 3 * t + 3]
        first_value = beta_one * first[...] + (1.0 - beta_one) * gradient
        second_value = beta_two * second[...] + (1.0 - beta_two) * gradient * gradient
        change = (
            learn_rate
            * (first_value / bias_one)
            / (jnp.sqrt(second_value / bias_two) + epsilon)
        )
        new_factor[...] = factor[...] - change
        new_first[...] = first_value
        new_second[...] = second_value


def swap(array, axis, size, *bits):
    return lax.ppermute(array, axis, [(i, i ^ bits[i % len(bits)]) for i in range(size)])


def local(
    users_list,
    items_list,
    days_list,
    status,
    user_factor,
    user_first,
    user_second,
    item_factor,
    item_first,
    item_second,
    day_factor,
    day_first,
    day_second,
):
    owners = lax.axis_size("dp")
    holders = lax.axis_size("mp")
    row_counts = (user_factor.shape[0], item_factor.shape[0], day_factor.shape[0])
    list_counts = (users_list.shape[1], items_list.shape[1], days_list.shape[1])
    sizes = Sizes(owners, holders, user_factor.shape[1], row_counts, list_counts)
    shape = jax.ShapeDtypeStruct
    small = pltpu.CompilerParams(vmem_limit_bytes=SMALL_VMEM)

    hbm = pl.BlockSpec(memory_space=pltpu.HBM)
    in_hbm = lambda a: pltpu.with_memory_space_constraint(a, pltpu.HBM)
    tables_in = (user_factor.T, item_factor.T, day_factor)
    piece = pl.pallas_call(
        functools.partial(pack_kernel, sizes),
        out_shape=shape((sizes.piece_rows, LANES), bf16),
        in_specs=[hbm] * 3,
        scratch_shapes=[pltpu.VMEM(a.shape, f32) for a in tables_in]
        + [pltpu.SemaphoreType.DMA((3,))],
        compiler_params=small,
        name="pack",
    )(*[in_hbm(a) for a in tables_in])
    pieces = [swap(piece, "mp", holders, bits) for bits in range(holders - 1, 0, -1)] + [piece]

    table = pl.pallas_call(
        functools.partial(table_kernel, sizes),
        out_shape=shape((sizes.table_rows, LANES), bf16),
        compiler_params=small,
        name="table",
    )(*pieces)
    if sizes.folded:
        across = swap(table, "dp", owners, 2, 4)
        along = swap(table, "dp", owners, 4, 2)
        arrived = [along, across]
    else:
        arrived = [swap(table, "dp", owners, bits) for bits in range(2, owners, 2)]
    own_crossed = swap(table, "dp", owners, 1)
    picks_places_notes = pl.pallas_call(
        functools.partial(slot_kernel, sizes),
        out_shape=tuple(
            [shape((owners * row_counts[t], list_counts[t]), bf16) for t in range(3)]
            + [shape((owners * sizes.slots[t], list_counts[t]), bf16) for t in range(3)]
            + [shape((owners, sizes.rank), f32)]
        ),
        in_specs=[pl.BlockSpec(memory_space=pltpu.SMEM)]
        + [hbm] * 3
        + [pl.BlockSpec(memory_space=pl.ANY)],
        scratch_shapes=[pltpu.VMEM((1, count), jnp.int32) for count in list_counts]
        + [pltpu.SemaphoreType.DMA((3,))],
        compiler_params=small,
        name="slots",
    )(
        lax.axis_index("dp").astype(jnp.int32).reshape(1),
        *[in_hbm(a) for a in (users_list, items_list, days_list)],
        table,
    )

    held = pl.pallas_call(
        hold_kernel,
        out_shape=shape(table.shape, bf16),
        compiler_params=small,
        name="hold",
    )(arrived[0], picks_places_notes[6])
    arrived[0] = held
    if sizes.folded:
        arrived.append(swap(held, "dp", owners, 2, 4))
    crossed = [own_crossed] + [swap(a, "dp", owners, 1) for a in arrived]
    inputs = [table, *arrived, *crossed, *picks_places_notes]
    users, items, days = list_counts
    half = shape((owners // 2 * sizes.slot_rows, sizes.rank), bf16)
    own, other = pl.pallas_call(
        functools.partial(block_kernel, sizes),
        out_shape=(half, half),
        in_specs=[pl.BlockSpec(memory_space=pltpu.VMEM)] * len(inputs) + [hbm],
        scratch_shapes=[
            pltpu.VMEM((users, sizes.rank), f32),
            pltpu.VMEM((users, sizes.rank), bf16),
            pltpu.VMEM((items, sizes.rank), bf16),
            pltpu.VMEM((sizes.rank, items), bf16),
            pltpu.VMEM((days, sizes.rank), f32),
            pltpu.VMEM((users, sizes.rank), f32),
            pltpu.VMEM((items, sizes.rank), f32),
            pltpu.VMEM((days, sizes.rank), f32),
            pltpu.VMEM((2 * users, sizes.rank), bf16),
            pltpu.VMEM((2 * users, sizes.rank), bf16),
            pltpu.VMEM((2 * users, items), bf16),
            pltpu.VMEM((2 * users, items), bf16),
            pltpu.VMEM((days, users, items), jnp.int32),
            pltpu.SemaphoreType.DMA((days // 4 + 1,)),
        ],
        compiler_params=pltpu.CompilerParams(vmem_limit_bytes=BLOCK_VMEM),
        name="block_gradients",
    )(*inputs, in_hbm(status))
    crossed = swap(other, "dp", owners, 1)
    message = shape((2 * sizes.slot_rows, sizes.rank), bf16)
    if sizes.folded:
        merges = (1, 3)
    else:
        merges = tuple(range(1, owners // 2))
    merged = pl.pallas_call(
        functools.partial(merge_kernel, sizes, merges),
        out_shape=tuple([message] * len(merges)),
        compiler_params=small,
        name="merge",
    )(own, crossed)
    returned = [own, crossed]
    if sizes.folded:
        diagonal = swap(merged[1], "dp", owners, 4, 2)
        returned.append(swap(merged[0], "dp", owners, 4, 2))
        folded = pl.pallas_call(
            functools.partial(fold_kernel, sizes, 2 * sizes.slot_rows),
            out_shape=(shape((holders // 2 * sizes.piece_rows, LANES), bf16),) * 2,
            compiler_params=small,
            cost_estimate=pl.CostEstimate(
                flops=4 * 10**9, bytes_accessed=4 * 10**6, transcendentals=0
            ),
            name="fold",
        )(own, crossed, diagonal)
        returned += [swap(a, "dp", owners, 2, 4) for a in folded]
    else:
        returned += [
            swap(merged[bits // 2 - 1], "dp", owners, bits) for bits in range(2, owners, 2)
        ]

    totals = pl.pallas_call(
        functools.partial(sum_kernel, sizes, len(returned)),
        out_shape=tuple([shape(piece.shape, bf16)] * holders),
        compiler_params=small,
        name="row_sums",
    )(*returned)
    column_totals = [totals[0]] + [
        swap(totals[bits], "mp", holders, bits) for bits in range(1, holders)
    ]

    states = (
        user_factor.T,
        user_first.T,
        user_second.T,
        item_factor.T,
        item_first.T,
        item_second.T,
        day_factor,
        day_first,
        day_second,
    )
    updated = pl.pallas_call(
        functools.partial(adam_kernel, sizes),
        out_shape=tuple(shape(a.shape, a.dtype) for a in states),
        compiler_params=small,
        name="adam",
    )(*column_totals, *states)
    return tuple(a.T for a in updated[:6]) + tuple(updated[6:])


def solution(mesh):
    block = P(("dp", "mp"), None)
    piece = P("dp", "mp")
    return jax.shard_map(
        local,
        mesh=mesh,
        in_specs=(block, block, block, P(("dp", "mp"), None, None, None)) + (piece,) * 9,
        out_specs=(piece,) * 9,
        check_vma=False,
    )
```

```python
import functools

import jax
import jax.numpy as jnp
from jax import lax
from jax.experimental import pallas as pl
from jax.experimental.pallas import tpu as pltpu
from jax.sharding import PartitionSpec as P

beta_one = 0.9
beta_two = 0.99
bias_one = 1.0 - 0.9**10
bias_two = 1.0 - 0.99**10
learn_rate = 0.01
epsilon = 1e-08
loss_scale = 0.0625

LANES = 128
SMALL_VMEM = 16 * 1024 * 1024
BLOCK_VMEM = 48 * 1024 * 1024

f32 = jnp.float32
bf16 = jnp.bfloat16


class Sizes:
    def __init__(self, owners, holders, columns, row_counts, list_counts):
        self.owners = owners
        self.holders = holders
        self.columns = columns
        self.rank = columns * holders
        self.row_counts = row_counts
        self.list_counts = list_counts
        limits = (
            max(2, 3 * list_counts[0] // (2 * owners)),
            max(2, 3 * list_counts[1] // (2 * owners)),
            max(2, 2 * list_counts[2] // owners),
        )
        self.slots = tuple(-(-(limit + t // 2) // 16) * 16 for t, limit in enumerate(limits))
        self.note_row = limits[2]
        self.slot_starts = (0, 0, self.slots[1])
        self.message_rows = (self.slots[1] + self.slots[2], self.slots[0])
        self.note_lanes = (0, LANES)
        self.day_parts = LANES // columns
        self.day_packed = -(-(row_counts[2] // self.day_parts) // 16) * 16
        self.piece_rows = 2 * columns + self.day_packed
        self.day_chunks = self.rank // LANES
        self.table_rows = 2 * self.rank + self.day_chunks * row_counts[2]


def iota(shape, dimension):
    return lax.broadcasted_iota(jnp.int32, shape, dimension)


def onehot(condition):
    return jnp.where(condition, 1.0, 0.0).astype(bf16)


def dot_nt(a, b):
    return lax.dot_general(a, b, (((1,), (1,)), ((), ())), preferred_element_type=f32)


def pack_days(sizes, days):
    rows = sizes.row_counts[2] // sizes.day_parts
    parts = [days[p * rows : (p + 1) * rows] for p in range(sizes.day_parts)]
    if rows != sizes.day_packed:
        blank = jnp.zeros((sizes.day_packed - rows, days.shape[1]), days.dtype)
        parts = [jnp.concatenate([part, blank], axis=0) for part in parts]
    return jnp.concatenate(parts, axis=1)


def unpack_days(sizes, packed):
    rows = sizes.row_counts[2] // sizes.day_parts
    return jnp.concatenate(
        [
            packed[:rows, p * sizes.columns : (p + 1) * sizes.columns]
            for p in range(sizes.day_parts)
        ],
        axis=0,
    )


def fetch(sources, targets, semaphores):
    copies = [
        pltpu.make_async_copy(source, target, semaphores.at[n])
        for n, (source, target) in enumerate(zip(sources, targets))
    ]
    for copy in copies:
        copy.start()
    for copy in copies:
        copy.wait()


def pack_kernel(sizes, user_hbm, item_hbm, day_hbm, out_ref, user, item, day, semaphores):
    columns = sizes.columns
    fetch((user_hbm, item_hbm, day_hbm), (user, item, day), semaphores)
    out_ref[:columns, :] = user[...].astype(bf16)
    out_ref[columns : 2 * columns, :] = item[...].astype(bf16)
    out_ref[2 * columns :, :] = pack_days(sizes, day[...]).astype(bf16)


def slot_kernel(sizes, me_ref, *refs):
    owners = sizes.owners
    picks, places, note_ref, lists = refs[4:7], refs[7:10], refs[10], refs[11:14]
    fetch(refs[:3], lists, refs[14])
    me = me_ref[0]
    notes = [[] for _ in range(owners)]
    for t in range(3):
        count, rows, slots = sizes.list_counts[t], sizes.row_counts[t], sizes.slots[t]
        number = lists[t][...]
        owner = number // rows
        row = number % rows
        partner = lax.bitwise_xor(owner, jnp.full_like(owner, me))
        picks[t][...] = onehot(iota((owners * rows, count), 0) == partner * rows + row)
        earlier = onehot(iota((count, count), 0) < iota((count, count), 1))
        owner_hot = iota((owners, count), 0) == owner
        before = jnp.dot(onehot(owner_hot), earlier, preferred_element_type=f32)
        position = jnp.sum(jnp.where(owner_hot, before, 0.0), axis=0, keepdims=True)
        target = partner * slots + position.astype(jnp.int32)
        place = onehot(iota((owners * slots, count), 0) == target)
        places[t][...] = place
        following = (row + 1).astype(bf16)
        for s in range(owners):
            notes[s].append(dot_nt(following, place[s * slots : (s + 1) * slots]) - 1.0)
    blanks = [jnp.full((1, LANES - rows), -1.0, f32) for rows in sizes.message_rows]
    note_ref[...] = jnp.concatenate(
        [
            jnp.concatenate([items, days, blanks[0], users, blanks[1]], axis=1)
            for users, items, days in notes
        ],
        axis=0,
    )


def table_kernel(sizes, *refs):
    pieces, out_ref = refs[-2::-1], refs[-1]
    columns, rank, day_rows = sizes.columns, sizes.rank, sizes.row_counts[2]
    for j, ref in enumerate(pieces):
        for t in range(2):
            out_ref[t * rank + j * columns : t * rank + (j + 1) * columns, :] = ref[
                t * columns : (t + 1) * columns, :
            ]
    days = jnp.concatenate(
        [unpack_days(sizes, ref[2 * columns :, :].astype(f32)) for ref in pieces], axis=1
    ).astype(bf16)
    for chunk in range(sizes.day_chunks):
        start = 2 * rank + chunk * day_rows
        out_ref[start : start + day_rows, :] = days[:, chunk * LANES : (chunk + 1) * LANES]


def block_kernel(sizes, *refs):
    owners, rank, day_rows = sizes.owners, sizes.rank, sizes.row_counts[2]
    tables, refs = refs[:owners], refs[owners:]
    picks, places = refs[:3], refs[3:6]
    note_ref, status_hbm = refs[6:8]
    own_refs, other_refs = refs[8:10], refs[10:12]
    (
        users,
        users_low,
        items,
        items_half_t,
        days,
        user_gradient,
        item_gradient,
        day_gradient,
        scaled_even,
        scaled_odd,
        residual_even,
        residual_odd,
        status,
        semaphores,
    ) = refs[12:]
    pair = 2
    pairs = status.shape[0] // pair
    chunks = [(0, pair)]
    chunks += [((2 * n - 1) * pair, 2 * pair) for n in range(1, pairs // 2)]
    chunks += [((pairs - 1) * pair, pair)]

    def status_copy(start, size, semaphore):
        part = pl.ds(start, size)
        return pltpu.make_async_copy(
            status_hbm.at[0, part], status.at[part], semaphores.at[semaphore]
        )

    for n, (start, size) in enumerate(chunks):
        status_copy(start, size, n).start()

    def pick(t):
        table = jnp.concatenate([ref[t * rank : (t + 1) * rank, :] for ref in tables], axis=1)
        return jnp.dot(table, picks[t][...], preferred_element_type=f32)

    user_values = pick(0).T
    users[...] = user_values
    users_low[...] = user_values.astype(bf16)
    items_t = pick(1)
    items[...] = items_t.T.astype(bf16)
    items_half_t[...] = (0.5 * items_t).astype(bf16)
    starts = [2 * rank + chunk * day_rows for chunk in range(sizes.day_chunks)]
    day_table = jnp.concatenate(
        [
            jnp.concatenate([ref[start : start + day_rows, :] for start in starts], axis=1)
            for ref in tables
        ],
        axis=0,
    )
    days[...] = lax.dot_general(
        picks[2][...], day_table, (((0,), (0,)), ((), ())), preferred_element_type=f32
    )
    user_gradient[...] = jnp.zeros_like(user_gradient)
    item_gradient[...] = jnp.zeros_like(item_gradient)
    count = users.shape[0]

    def residuals(first, scaled, residual):
        for j in range(pair):
            rows = slice(j * count, (j + 1) * count)
            day = days[pl.ds(first + j, 1), :].astype(bf16)
            scaled_values = day * users_low[...]
            scaled[rows, :] = scaled_values
            half_logits = jnp.dot(scaled_values, items_half_t[...], preferred_element_type=f32)
            state = status[first + j]
            residual[rows, :] = (
                state.astype(f32) * (jnp.tanh(half_logits) + jnp.where(state == 1, -1.0, 1.0))
            ).astype(bf16)

    def gradients(first, scaled, residual):
        total = 0.0
        for j in range(pair):
            rows = slice(j * count, (j + 1) * count)
            day = days[pl.ds(first + j, 1), :]
            projected = jnp.dot(residual[rows, :], items[...], preferred_element_type=f32)
            total = total + projected * day
            day_gradient[pl.ds(first + j, 1), :] = jnp.sum(
                projected * users[...], axis=0, keepdims=True
            )
        user_gradient[...] += total
        item_gradient[...] += lax.dot_general(
            residual[...], scaled[...], (((0,), (0,)), ((), ())), preferred_element_type=f32
        )

    even, odd = (scaled_even, residual_even), (scaled_odd, residual_odd)
    status_copy(*chunks[0], 0).wait()
    residuals(0, *even)

    @pl.loop(0, pairs // 2 - 1)
    def _(n):
        first = 2 * n * pair
        status_copy(first + pair, 2 * pair, n + 1).wait()
        residuals(first + pair, *odd)
        gradients(first, *even)
        residuals(first + 2 * pair, *even)
        gradients(first + pair, *odd)

    last = (pairs - 1) * pair
    status_copy(*chunks[-1], len(chunks) - 1).wait()
    residuals(last, *odd)
    gradients(last - pair, *even)
    gradients(last, *odd)

    for t, gradient in enumerate((user_gradient, item_gradient, day_gradient)):
        start, slots = sizes.slot_starts[t], sizes.slots[t]
        values = (0.5 * loss_scale * gradient[...]).astype(bf16)
        placed = jnp.dot(places[t][...], values, preferred_element_type=f32)
        for s in range(owners):
            rows = placed[s * slots : (s + 1) * slots]
            if t == 2:
                note = iota(rows.shape, 0) == sizes.note_row
                rows = jnp.where(note, note_ref[s : s + 1, :], rows)
            part = int(t == 0)
            out = (own_refs, other_refs)[s % 2][part]
            first = (s // 2) * sizes.message_rows[part] + start
            out[first : first + slots, :] = rows.astype(bf16)


def hold_kernel(arrived_ref, note_ref, out_ref):
    out_ref[...] = arrived_ref[...]


def merge_kernel(rows, own_ref, crossed_ref, *outs):
    for n, out in enumerate(outs):
        start = (n + 1) * rows
        out[:rows, :] = own_ref[start : start + rows, :]
        out[rows:, :] = crossed_ref[start : start + rows, :]


def split_messages(rows, refs):
    messages = [ref.at[:rows] for ref in refs]
    return messages + [ref.at[rows:] for ref in refs[2:]]


def sum_kernel(sizes, part, *refs):
    holders, columns = sizes.holders, sizes.columns
    count = sizes.owners // 2 + 1
    outs = refs[-holders:]
    firsts = split_messages(sizes.message_rows[0], refs[:count])
    messages = split_messages(sizes.message_rows[part], refs[part * count : (part + 1) * count])
    tables = ((1, 2), (0,))[part]
    totals = [0.0] * len(tables)
    day_start = sizes.slot_starts[2]
    width = sizes.message_rows[part]
    for first, ref in zip(firsts, messages):
        notes = first[day_start : day_start + sizes.slots[2], :].astype(f32)
        lane = sizes.note_lanes[part]
        rows = notes[sizes.note_row : sizes.note_row + 1, lane : lane + width].astype(jnp.int32)
        for n, t in enumerate(tables):
            start, slots = sizes.slot_starts[t], sizes.slots[t]
            shape = (sizes.row_counts[t], width)
            slot = iota(shape, 1)
            mine = (slot >= start) & (slot < start + slots)
            selector = onehot((iota(shape, 0) == rows) & mine)
            totals[n] = totals[n] + jnp.dot(selector, ref[...], preferred_element_type=f32)
    turned = totals[0].T.astype(bf16)
    for j in range(holders):
        outs[j][:columns, :] = turned[j * columns : (j + 1) * columns]
        if part == 0:
            days = totals[1][:, j * columns : (j + 1) * columns]
            outs[j][columns:, :] = pack_days(sizes, days).astype(bf16)


def adam_kernel(sizes, tables, *refs):
    holders, columns = sizes.holders, sizes.columns
    count = 3 * len(tables)
    pieces = refs[:holders]
    states = refs[holders : holders + count]
    outs = refs[-count:]
    total = pieces[0][...].astype(f32)
    for ref in pieces[1:]:
        total = total + ref[...].astype(f32)
    for t, table in enumerate(tables):
        if table < 2:
            gradient = total[:columns]
        else:
            gradient = unpack_days(sizes, total[columns:])
        factor, first, second = states[3 * t : 3 * t + 3]
        new_factor, new_first, new_second = outs[3 * t : 3 * t + 3]
        first_value = beta_one * first[...] + (1.0 - beta_one) * gradient
        second_value = beta_two * second[...] + (1.0 - beta_two) * gradient * gradient
        change = (
            learn_rate
            * (first_value / bias_one)
            / (jnp.sqrt(second_value / bias_two) + epsilon)
        )
        new_factor[...] = factor[...] - change
        new_first[...] = first_value
        new_second[...] = second_value


def swap(array, axis, size, bits):
    return lax.ppermute(array, axis, [(i, i ^ bits) for i in range(size)])


def local(
    users_list,
    items_list,
    days_list,
    status,
    user_factor,
    user_first,
    user_second,
    item_factor,
    item_first,
    item_second,
    day_factor,
    day_first,
    day_second,
):
    owners = lax.axis_size("dp")
    holders = lax.axis_size("mp")
    row_counts = (user_factor.shape[0], item_factor.shape[0], day_factor.shape[0])
    list_counts = (users_list.shape[1], items_list.shape[1], days_list.shape[1])
    sizes = Sizes(owners, holders, user_factor.shape[1], row_counts, list_counts)
    shape = jax.ShapeDtypeStruct
    small = pltpu.CompilerParams(vmem_limit_bytes=SMALL_VMEM)

    hbm = pl.BlockSpec(memory_space=pltpu.HBM)
    vmem = pl.BlockSpec(memory_space=pltpu.VMEM)
    anywhere = pl.BlockSpec(memory_space=pl.ANY)
    in_hbm = lambda a: pltpu.with_memory_space_constraint(a, pltpu.HBM)
    tables_in = (user_factor.T, item_factor.T, day_factor)
    piece = pl.pallas_call(
        functools.partial(pack_kernel, sizes),
        out_shape=shape((sizes.piece_rows, LANES), bf16),
        in_specs=[hbm] * 3,
        scratch_shapes=[pltpu.VMEM(a.shape, f32) for a in tables_in]
        + [pltpu.SemaphoreType.DMA((3,))],
        compiler_params=small,
        name="pack",
    )(*[in_hbm(a) for a in tables_in])
    pieces = [swap(piece, "mp", holders, bits) for bits in range(holders - 1, 0, -1)] + [piece]

    table = pl.pallas_call(
        functools.partial(table_kernel, sizes),
        out_shape=shape((sizes.table_rows, LANES), bf16),
        compiler_params=small,
        name="table",
    )(*pieces)
    arrived = [swap(table, "dp", owners, bits) for bits in range(owners - 2, 0, -2)]
    own_crossed = swap(table, "dp", owners, 1)
    picks_places_notes = pl.pallas_call(
        functools.partial(slot_kernel, sizes),
        out_shape=tuple(
            [shape((owners * row_counts[t], list_counts[t]), bf16) for t in range(3)]
            + [shape((owners * sizes.slots[t], list_counts[t]), bf16) for t in range(3)]
            + [shape((owners, 2 * LANES), f32)]
        ),
        in_specs=[pl.BlockSpec(memory_space=pltpu.SMEM)]
        + [hbm] * 3
        + [anywhere],
        scratch_shapes=[pltpu.VMEM((1, count), jnp.int32) for count in list_counts]
        + [pltpu.SemaphoreType.DMA((3,))],
        compiler_params=small,
        name="slots",
    )(
        lax.axis_index("dp").astype(jnp.int32).reshape(1),
        *[in_hbm(a) for a in (users_list, items_list, days_list)],
        table,
    )

    arrived[0] = pl.pallas_call(
        hold_kernel,
        out_shape=shape(table.shape, bf16),
        compiler_params=small,
        name="hold",
    )(arrived[0], picks_places_notes[6])
    tables = [table, own_crossed]
    for a in arrived[::-1]:
        tables += [a, swap(a, "dp", owners, 1)]
    inputs = [*tables, *picks_places_notes]
    users, items, days = list_counts
    halves = tuple(
        shape((owners // 2 * rows, sizes.rank), bf16) for rows in sizes.message_rows
    )
    gradients = pl.pallas_call(
        functools.partial(block_kernel, sizes),
        out_shape=halves + halves,
        in_specs=[vmem] * len(inputs) + [hbm],
        scratch_shapes=[
            pltpu.VMEM((users, sizes.rank), f32),
            pltpu.VMEM((users, sizes.rank), bf16),
            pltpu.VMEM((items, sizes.rank), bf16),
            pltpu.VMEM((sizes.rank, items), bf16),
            pltpu.VMEM((days, sizes.rank), f32),
            pltpu.VMEM((users, sizes.rank), f32),
            pltpu.VMEM((items, sizes.rank), f32),
            pltpu.VMEM((days, sizes.rank), f32),
            pltpu.VMEM((2 * users, sizes.rank), bf16),
            pltpu.VMEM((2 * users, sizes.rank), bf16),
            pltpu.VMEM((2 * users, items), bf16),
            pltpu.VMEM((2 * users, items), bf16),
            pltpu.VMEM((days, users, items), jnp.int32),
            pltpu.SemaphoreType.DMA((days // 4 + 1,)),
        ],
        compiler_params=pltpu.CompilerParams(vmem_limit_bytes=BLOCK_VMEM),
        name="block_gradients",
    )(*inputs, in_hbm(status))
    returned, updated = [], {}
    for part, rows in enumerate(sizes.message_rows):
        own, other = gradients[part], gradients[2 + part]
        crossed = swap(other, "dp", owners, 1)
        message = shape((2 * rows, sizes.rank), bf16)
        merged = pl.pallas_call(
            functools.partial(merge_kernel, rows),
            out_shape=tuple([message] * (owners // 2 - 1)),
            compiler_params=small,
            name="merge",
        )(own, crossed)
        returned += [own, crossed]
        returned += [
            swap(merged[bits // 2 - 1], "dp", owners, bits) for bits in range(2, owners, 2)
        ]
    states = (
        user_factor.T,
        user_first.T,
        user_second.T,
        item_factor.T,
        item_first.T,
        item_second.T,
        day_factor,
        day_first,
        day_second,
    )
    behind_sums, behind_adam = [], []
    for part, members in enumerate(((1, 2), (0,))):
        rows = sizes.columns + (sizes.day_packed if part == 0 else 0)
        totals = pl.pallas_call(
            functools.partial(sum_kernel, sizes, part),
            out_shape=tuple([shape((rows, LANES), bf16)] * holders),
            in_specs=[vmem] * ((part + 1) * (owners // 2 + 1)) + [anywhere] * part,
            compiler_params=small,
            name="row_sums",
        )(*returned[: (part + 1) * (owners // 2 + 1)], *behind_sums)
        behind_sums = [totals[0]]
        column_totals = [totals[0]] + [
            swap(totals[bits], "mp", holders, bits) for bits in range(1, holders)
        ]
        held = [a for t in members for a in states[3 * t : 3 * t + 3]]
        results = pl.pallas_call(
            functools.partial(adam_kernel, sizes, members),
            out_shape=tuple(shape(a.shape, a.dtype) for a in held),
            in_specs=[vmem] * (holders + len(held)) + [anywhere] * part,
            compiler_params=small,
            name="adam",
        )(*column_totals, *held, *behind_adam)
        behind_adam = [results[0]]
        for n, t in enumerate(members):
            updated[t] = results[3 * n : 3 * n + 3]
    return tuple(a.T for a in (*updated[0], *updated[1])) + tuple(updated[2])


def solution(mesh):
    block = P(("dp", "mp"), None)
    piece = P("dp", "mp")
    return jax.shard_map(
        local,
        mesh=mesh,
        in_specs=(block, block, block, P(("dp", "mp"), None, None, None)) + (piece,) * 9,
        out_specs=(piece,) * 9,
        check_vma=False,
    )
```

```python
import functools

import jax
import jax.numpy as jnp
from jax import lax
from jax.experimental import pallas as pl
from jax.experimental.pallas import tpu as pltpu
from jax.sharding import PartitionSpec as P

beta_one = 0.9
beta_two = 0.99
bias_one = 1.0 - 0.9**10
bias_two = 1.0 - 0.99**10
learn_rate = 0.01
epsilon = 1e-08
loss_scale = 0.0625

LANES = 128
HOLD = 2
SMALL_VMEM = 16 * 1024 * 1024
BLOCK_VMEM = 48 * 1024 * 1024

f32 = jnp.float32
bf16 = jnp.bfloat16


class Sizes:
    def __init__(self, owners, holders, columns, row_counts, list_counts):
        self.owners = owners
        self.holders = holders
        self.columns = columns
        self.rank = columns * holders
        self.row_counts = row_counts
        self.list_counts = list_counts
        limits = (
            max(2, 3 * list_counts[0] // (2 * owners)),
            max(2, 3 * list_counts[1] // (2 * owners)),
            max(2, 2 * list_counts[2] // owners),
        )
        self.slots = tuple(-(-(limit + t // 2) // 16) * 16 for t, limit in enumerate(limits))
        self.note_row = limits[2]
        self.slot_starts = (0, self.slots[0], self.slots[0] + self.slots[1])
        self.slot_rows = sum(self.slots)
        self.day_parts = LANES // columns
        self.day_packed = -(-(row_counts[2] // self.day_parts) // 16) * 16
        self.piece_rows = 2 * columns + self.day_packed
        self.day_chunks = self.rank // LANES
        self.table_rows = 2 * self.rank + self.day_chunks * row_counts[2]


def iota(shape, dimension):
    return lax.broadcasted_iota(jnp.int32, shape, dimension)


def onehot(condition):
    return jnp.where(condition, 1.0, 0.0).astype(bf16)


def dot_nt(a, b):
    return lax.dot_general(a, b, (((1,), (1,)), ((), ())), preferred_element_type=f32)


def pack_days(sizes, days):
    rows = sizes.row_counts[2] // sizes.day_parts
    parts = [days[p * rows : (p + 1) * rows] for p in range(sizes.day_parts)]
    if rows != sizes.day_packed:
        blank = jnp.zeros((sizes.day_packed - rows, days.shape[1]), days.dtype)
        parts = [jnp.concatenate([part, blank], axis=0) for part in parts]
    return jnp.concatenate(parts, axis=1)


def unpack_days(sizes, packed):
    rows = sizes.row_counts[2] // sizes.day_parts
    return jnp.concatenate(
        [
            packed[:rows, p * sizes.columns : (p + 1) * sizes.columns]
            for p in range(sizes.day_parts)
        ],
        axis=0,
    )


def fetch(sources, targets, semaphores):
    copies = [
        pltpu.make_async_copy(source, target, semaphores.at[n])
        for n, (source, target) in enumerate(zip(sources, targets))
    ]
    for copy in copies:
        copy.start()
    for copy in copies:
        copy.wait()


def pack_kernel(sizes, user_hbm, item_hbm, day_hbm, out_ref, user, item, day, semaphores):
    columns = sizes.columns
    fetch((user_hbm, item_hbm, day_hbm), (user, item, day), semaphores)
    out_ref[:columns, :] = user[...].astype(bf16)
    out_ref[columns : 2 * columns, :] = item[...].astype(bf16)
    out_ref[2 * columns :, :] = pack_days(sizes, day[...]).astype(bf16)


def exchange_order(size):
    order = list(range(1, size))
    return [1] + order[:0:-1]


def slot_kernel(sizes, me_ref, *refs):
    owners = sizes.owners
    picks, places, note_ref, lists = refs[4:7], refs[7:10], refs[10], refs[11:14]
    fetch(refs[:3], lists, refs[14])
    me = me_ref[0]
    notes = [[] for _ in range(owners)]
    for t in range(3):
        count, rows, slots = sizes.list_counts[t], sizes.row_counts[t], sizes.slots[t]
        number = lists[t][...]
        owner = number // rows
        row = number % rows
        partner = lax.bitwise_xor(owner, jnp.full_like(owner, me))
        picks[t][...] = onehot(iota((owners * rows, count), 0) == partner * rows + row)
        earlier = onehot(iota((count, count), 0) < iota((count, count), 1))
        owner_hot = iota((owners, count), 0) == owner
        before = jnp.dot(onehot(owner_hot), earlier, preferred_element_type=f32)
        position = jnp.sum(jnp.where(owner_hot, before, 0.0), axis=0, keepdims=True)
        target = partner * slots + position.astype(jnp.int32)
        place = onehot(iota((owners * slots, count), 0) == target)
        places[t][...] = place
        following = (row + 1).astype(bf16)
        for s in range(owners):
            notes[s].append(dot_nt(following, place[s * slots : (s + 1) * slots]) - 1.0)
    blank = jnp.full((1, sizes.rank - sizes.slot_rows), -1.0, f32)
    note_ref[...] = jnp.concatenate(
        [jnp.concatenate(note + [blank], axis=1) for note in notes], axis=0
    )


def table_kernel(sizes, *refs):
    order = exchange_order(sizes.holders) + [0]
    pieces, out_ref = [refs[order.index(j)] for j in range(sizes.holders)], refs[-1]
    columns, rank, day_rows = sizes.columns, sizes.rank, sizes.row_counts[2]
    for j, ref in enumerate(pieces):
        for t in range(2):
            out_ref[t * rank + j * columns : t * rank + (j + 1) * columns, :] = ref[
                t * columns : (t + 1) * columns, :
            ]
    days = jnp.concatenate(
        [unpack_days(sizes, ref[2 * columns :, :].astype(f32)) for ref in pieces], axis=1
    ).astype(bf16)
    for chunk in range(sizes.day_chunks):
        start = 2 * rank + chunk * day_rows
        out_ref[start : start + day_rows, :] = days[:, chunk * LANES : (chunk + 1) * LANES]


def block_kernel(sizes, *refs):
    owners, rank, day_rows = sizes.owners, sizes.rank, sizes.row_counts[2]
    tables, refs = refs[:owners], refs[owners:]
    picks, places = refs[:3], refs[3:6]
    note_ref, status_hbm, own_ref, other_ref = refs[6:10]
    (
        users,
        users_low,
        items,
        items_half_t,
        days,
        user_gradient,
        item_gradient,
        day_gradient,
        scaled_even,
        scaled_odd,
        residual_even,
        residual_odd,
        status,
        semaphores,
    ) = refs[10:]
    pair = 2
    pairs = status.shape[0] // pair
    chunks = [(0, pair)]
    chunks += [((2 * n - 1) * pair, 2 * pair) for n in range(1, pairs // 2)]
    chunks += [((pairs - 1) * pair, pair)]

    def status_copy(start, size, semaphore):
        part = pl.ds(start, size)
        return pltpu.make_async_copy(
            status_hbm.at[0, part], status.at[part], semaphores.at[semaphore]
        )

    for n, (start, size) in enumerate(chunks):
        status_copy(start, size, n).start()

    def pick(t):
        table = jnp.concatenate([ref[t * rank : (t + 1) * rank, :] for ref in tables], axis=1)
        return jnp.dot(table, picks[t][...], preferred_element_type=f32)

    user_values = pick(0).T
    users[...] = user_values
    users_low[...] = user_values.astype(bf16)
    items_t = pick(1)
    items[...] = items_t.T.astype(bf16)
    items_half_t[...] = (0.5 * items_t).astype(bf16)
    starts = [2 * rank + chunk * day_rows for chunk in range(sizes.day_chunks)]
    day_table = jnp.concatenate(
        [
            jnp.concatenate([ref[start : start + day_rows, :] for start in starts], axis=1)
            for ref in tables
        ],
        axis=0,
    )
    days[...] = lax.dot_general(
        picks[2][...], day_table, (((0,), (0,)), ((), ())), preferred_element_type=f32
    )
    user_gradient[...] = jnp.zeros_like(user_gradient)
    item_gradient[...] = jnp.zeros_like(item_gradient)
    count = users.shape[0]

    def residuals(first, scaled, residual):
        for j in range(pair):
            rows = slice(j * count, (j + 1) * count)
            day = days[pl.ds(first + j, 1), :].astype(bf16)
            scaled_values = day * users_low[...]
            scaled[rows, :] = scaled_values
            half_logits = jnp.dot(scaled_values, items_half_t[...], preferred_element_type=f32)
            state = status[first + j]
            residual[rows, :] = (
                state.astype(f32) * (jnp.tanh(half_logits) + jnp.where(state == 1, -1.0, 1.0))
            ).astype(bf16)

    def gradients(first, scaled, residual):
        total = 0.0
        for j in range(pair):
            rows = slice(j * count, (j + 1) * count)
            day = days[pl.ds(first + j, 1), :]
            projected = jnp.dot(residual[rows, :], items[...], preferred_element_type=f32)
            total = total + projected * day
            day_gradient[pl.ds(first + j, 1), :] = jnp.sum(
                projected * users[...], axis=0, keepdims=True
            )
        user_gradient[...] += total
        item_gradient[...] += lax.dot_general(
            residual[...], scaled[...], (((0,), (0,)), ((), ())), preferred_element_type=f32
        )

    even, odd = (scaled_even, residual_even), (scaled_odd, residual_odd)
    status_copy(*chunks[0], 0).wait()
    residuals(0, *even)

    @pl.loop(0, pairs // 2 - 1)
    def _(n):
        first = 2 * n * pair
        status_copy(first + pair, 2 * pair, n + 1).wait()
        residuals(first + pair, *odd)
        gradients(first, *even)
        residuals(first + 2 * pair, *even)
        gradients(first + pair, *odd)

    last = (pairs - 1) * pair
    status_copy(*chunks[-1], len(chunks) - 1).wait()
    residuals(last, *odd)
    gradients(last - pair, *even)
    gradients(last, *odd)

    for t, gradient in enumerate((user_gradient, item_gradient, day_gradient)):
        start, slots = sizes.slot_starts[t], sizes.slots[t]
        values = (0.5 * loss_scale * gradient[...]).astype(bf16)
        placed = jnp.dot(places[t][...], values, preferred_element_type=f32)
        for s in range(owners):
            rows = placed[s * slots : (s + 1) * slots]
            if t == 2:
                note = iota(rows.shape, 0) == sizes.note_row
                rows = jnp.where(note, note_ref[s : s + 1, :], rows)
            out = (own_ref, other_ref)[s % 2]
            first = (s // 2) * sizes.slot_rows + start
            out[first : first + slots, :] = rows.astype(bf16)


def hold_kernel(arrived_ref, note_ref, out_ref):
    out_ref[...] = arrived_ref[...]


def merge_kernel(sizes, own_ref, crossed_ref, *outs):
    rows = sizes.slot_rows
    for n, out in enumerate(outs):
        start = (n + 1) * rows
        out[:rows, :] = own_ref[start : start + rows, :]
        out[rows:, :] = crossed_ref[start : start + rows, :]


def sum_kernel(sizes, *refs):
    holders, columns = sizes.holders, sizes.columns
    inputs = sizes.owners // 2 + 1
    arrived, outs = refs[:inputs], refs[inputs:]
    day_start = sizes.slot_starts[2]
    totals = [0.0, 0.0, 0.0]
    messages = [ref.at[: sizes.slot_rows] for ref in arrived]
    messages += [ref.at[sizes.slot_rows :] for ref in arrived[2:]]
    for ref in messages:
        notes = ref[day_start : day_start + sizes.slots[2], :].astype(f32)
        rows = notes[sizes.note_row : sizes.note_row + 1, : sizes.slot_rows].astype(jnp.int32)
        for t in range(3):
            start, slots = sizes.slot_starts[t], sizes.slots[t]
            shape = (sizes.row_counts[t], sizes.slot_rows)
            slot = iota(shape, 1)
            mine = (slot >= start) & (slot < start + slots)
            selector = onehot((iota(shape, 0) == rows) & mine)
            totals[t] = totals[t] + jnp.dot(selector, ref[...], preferred_element_type=f32)
    for t in range(3):
        if t < 2:
            turned = totals[t].T.astype(bf16)
            for j in range(holders):
                outs[j][t * columns : (t + 1) * columns, :] = turned[
                    j * columns : (j + 1) * columns
                ]
        else:
            for j in range(holders):
                outs[j][2 * columns :, :] = pack_days(
                    sizes, totals[t][:, j * columns : (j + 1) * columns]
                ).astype(bf16)


def adam_kernel(sizes, *refs):
    holders, columns = sizes.holders, sizes.columns
    pieces = refs[:holders]
    states = refs[holders : holders + 9]
    outs = refs[holders + 9 :]
    total = pieces[0][...].astype(f32)
    for ref in pieces[1:]:
        total = total + ref[...].astype(f32)
    for t in range(3):
        if t < 2:
            gradient = total[t * columns : (t + 1) * columns]
        else:
            gradient = unpack_days(sizes, total[2 * columns :])
        factor, first, second = states[3 * t : 3 * t + 3]
        new_factor, new_first, new_second = outs[3 * t : 3 * t + 3]
        first_value = beta_one * first[...] + (1.0 - beta_one) * gradient
        second_value = beta_two * second[...] + (1.0 - beta_two) * gradient * gradient
        change = (
            learn_rate
            * (first_value / bias_one)
            / (jnp.sqrt(second_value / bias_two) + epsilon)
        )
        new_factor[...] = factor[...] - change
        new_first[...] = first_value
        new_second[...] = second_value


def swap(array, axis, size, bits):
    return lax.ppermute(array, axis, [(i, i ^ bits) for i in range(size)])


def local(
    users_list,
    items_list,
    days_list,
    status,
    user_factor,
    user_first,
    user_second,
    item_factor,
    item_first,
    item_second,
    day_factor,
    day_first,
    day_second,
):
    owners = lax.axis_size("dp")
    holders = lax.axis_size("mp")
    row_counts = (user_factor.shape[0], item_factor.shape[0], day_factor.shape[0])
    list_counts = (users_list.shape[1], items_list.shape[1], days_list.shape[1])
    sizes = Sizes(owners, holders, user_factor.shape[1], row_counts, list_counts)
    shape = jax.ShapeDtypeStruct
    small = pltpu.CompilerParams(vmem_limit_bytes=SMALL_VMEM)

    hbm = pl.BlockSpec(memory_space=pltpu.HBM)
    in_hbm = lambda a: pltpu.with_memory_space_constraint(a, pltpu.HBM)
    tables_in = (user_factor.T, item_factor.T, day_factor)
    piece = pl.pallas_call(
        functools.partial(pack_kernel, sizes),
        out_shape=shape((sizes.piece_rows, LANES), bf16),
        in_specs=[hbm] * 3,
        scratch_shapes=[pltpu.VMEM(a.shape, f32) for a in tables_in]
        + [pltpu.SemaphoreType.DMA((3,))],
        compiler_params=small,
        name="pack",
    )(*[in_hbm(a) for a in tables_in])
    distances = exchange_order(holders)
    pieces = [swap(piece, "mp", holders, bits) for bits in distances] + [piece]

    table = pl.pallas_call(
        functools.partial(table_kernel, sizes),
        out_shape=shape((sizes.table_rows, LANES), bf16),
        compiler_params=small,
        name="table",
    )(*pieces)
    arrived = {bits: swap(table, "dp", owners, bits) for bits in range(2, owners, 2)}
    own_crossed = swap(table, "dp", owners, 1)
    picks_places_notes = pl.pallas_call(
        functools.partial(slot_kernel, sizes),
        out_shape=tuple(
            [shape((owners * row_counts[t], list_counts[t]), bf16) for t in range(3)]
            + [shape((owners * sizes.slots[t], list_counts[t]), bf16) for t in range(3)]
            + [shape((owners, sizes.rank), f32)]
        ),
        in_specs=[pl.BlockSpec(memory_space=pltpu.SMEM)]
        + [hbm] * 3
        + [pl.BlockSpec(memory_space=pl.ANY)],
        scratch_shapes=[pltpu.VMEM((1, count), jnp.int32) for count in list_counts]
        + [pltpu.SemaphoreType.DMA((3,))],
        compiler_params=small,
        name="slots",
    )(
        lax.axis_index("dp").astype(jnp.int32).reshape(1),
        *[in_hbm(a) for a in (users_list, items_list, days_list)],
        table,
    )

    arrived[HOLD] = pl.pallas_call(
        hold_kernel,
        out_shape=shape(table.shape, bf16),
        compiler_params=small,
        name="hold",
    )(arrived[HOLD], picks_places_notes[6])
    tables = [table, own_crossed]
    for bits in range(2, owners, 2):
        tables += [arrived[bits], swap(arrived[bits], "dp", owners, 1)]
    inputs = [*tables, *picks_places_notes]
    users, items, days = list_counts
    half = shape((owners // 2 * sizes.slot_rows, sizes.rank), bf16)
    own, other = pl.pallas_call(
        functools.partial(block_kernel, sizes),
        out_shape=(half, half),
        in_specs=[pl.BlockSpec(memory_space=pltpu.VMEM)] * len(inputs) + [hbm],
        scratch_shapes=[
            pltpu.VMEM((users, sizes.rank), f32),
            pltpu.VMEM((users, sizes.rank), bf16),
            pltpu.VMEM((items, sizes.rank), bf16),
            pltpu.VMEM((sizes.rank, items), bf16),
            pltpu.VMEM((days, sizes.rank), f32),
            pltpu.VMEM((users, sizes.rank), f32),
            pltpu.VMEM((items, sizes.rank), f32),
            pltpu.VMEM((days, sizes.rank), f32),
            pltpu.VMEM((2 * users, sizes.rank), bf16),
            pltpu.VMEM((2 * users, sizes.rank), bf16),
            pltpu.VMEM((2 * users, items), bf16),
            pltpu.VMEM((2 * users, items), bf16),
            pltpu.VMEM((days, users, items), jnp.int32),
            pltpu.SemaphoreType.DMA((days // 4 + 1,)),
        ],
        compiler_params=pltpu.CompilerParams(vmem_limit_bytes=BLOCK_VMEM),
        name="block_gradients",
    )(*inputs, in_hbm(status))
    crossed = swap(other, "dp", owners, 1)
    message = shape((2 * sizes.slot_rows, sizes.rank), bf16)
    merged = pl.pallas_call(
        functools.partial(merge_kernel, sizes),
        out_shape=tuple([message] * (owners // 2 - 1)),
        compiler_params=small,
        name="merge",
    )(own, crossed)
    returned = [own, crossed]
    returned += [
        swap(merged[bits // 2 - 1], "dp", owners, bits) for bits in range(owners - 2, 0, -2)
    ]

    totals = pl.pallas_call(
        functools.partial(sum_kernel, sizes),
        out_shape=tuple([shape(piece.shape, bf16)] * holders),
        compiler_params=small,
        name="row_sums",
    )(*returned)
    column_totals = [totals[0]] + [
        swap(totals[bits], "mp", holders, bits) for bits in range(holders - 1, 0, -1)
    ]

    states = (
        user_factor.T,
        user_first.T,
        user_second.T,
        item_factor.T,
        item_first.T,
        item_second.T,
        day_factor,
        day_first,
        day_second,
    )
    updated = pl.pallas_call(
        functools.partial(adam_kernel, sizes),
        out_shape=tuple(shape(a.shape, a.dtype) for a in states),
        compiler_params=small,
        name="adam",
    )(*column_totals, *states)
    return tuple(a.T for a in updated[:6]) + tuple(updated[6:])


def solution(mesh):
    block = P(("dp", "mp"), None)
    piece = P("dp", "mp")
    return jax.shard_map(
        local,
        mesh=mesh,
        in_specs=(block, block, block, P(("dp", "mp"), None, None, None)) + (piece,) * 9,
        out_specs=(piece,) * 9,
        check_vma=False,
    )
```

```python
import functools

import jax
import jax.numpy as jnp
from jax import lax
from jax.experimental import pallas as pl
from jax.experimental.pallas import tpu as pltpu
from jax.sharding import PartitionSpec as P

beta_one = 0.9
beta_two = 0.99
bias_one = 1.0 - 0.9**10
bias_two = 1.0 - 0.99**10
learn_rate = 0.01
epsilon = 1e-08
loss_scale = 0.0625

LANES = 128
HOLD = 2
SMALL_VMEM = 16 * 1024 * 1024
BLOCK_VMEM = 48 * 1024 * 1024

f32 = jnp.float32
bf16 = jnp.bfloat16


class Sizes:
    def __init__(self, owners, holders, columns, row_counts, list_counts):
        self.owners = owners
        self.holders = holders
        self.columns = columns
        self.rank = columns * holders
        self.row_counts = row_counts
        self.list_counts = list_counts
        limits = (
            max(2, 3 * list_counts[0] // (2 * owners)),
            max(2, 3 * list_counts[1] // (2 * owners)),
            max(2, 2 * list_counts[2] // owners),
        )
        self.slots = tuple(-(-(limit + t // 2) // 16) * 16 for t, limit in enumerate(limits))
        self.note_row = limits[2]
        self.slot_starts = (0, self.slots[0], self.slots[0] + self.slots[1])
        self.slot_rows = sum(self.slots)
        self.chunks = self.rank // LANES
        self.message_rows = self.chunks * self.slot_rows
        self.day_parts = LANES // columns
        self.day_packed = -(-(row_counts[2] // self.day_parts) // 16) * 16
        self.piece_rows = 2 * columns + self.day_packed
        self.day_chunks = self.rank // LANES
        self.table_rows = 2 * self.rank + self.day_chunks * row_counts[2]


def iota(shape, dimension):
    return lax.broadcasted_iota(jnp.int32, shape, dimension)


def onehot(condition):
    return jnp.where(condition, 1.0, 0.0).astype(bf16)


def dot_nt(a, b):
    return lax.dot_general(a, b, (((1,), (1,)), ((), ())), preferred_element_type=f32)


def pack_days(sizes, days):
    rows = sizes.row_counts[2] // sizes.day_parts
    parts = [days[p * rows : (p + 1) * rows] for p in range(sizes.day_parts)]
    if rows != sizes.day_packed:
        blank = jnp.zeros((sizes.day_packed - rows, days.shape[1]), days.dtype)
        parts = [jnp.concatenate([part, blank], axis=0) for part in parts]
    return jnp.concatenate(parts, axis=1)


def unpack_days(sizes, packed):
    rows = sizes.row_counts[2] // sizes.day_parts
    return jnp.concatenate(
        [
            packed[:rows, p * sizes.columns : (p + 1) * sizes.columns]
            for p in range(sizes.day_parts)
        ],
        axis=0,
    )


def fetch(sources, targets, semaphores):
    copies = [
        pltpu.make_async_copy(source, target, semaphores.at[n])
        for n, (source, target) in enumerate(zip(sources, targets))
    ]
    for copy in copies:
        copy.start()
    for copy in copies:
        copy.wait()


def pack_kernel(sizes, user_hbm, item_hbm, day_hbm, out_ref, user, item, day, semaphores):
    columns = sizes.columns
    fetch((user_hbm, item_hbm, day_hbm), (user, item, day), semaphores)
    out_ref[:columns, :] = user[...].astype(bf16)
    out_ref[columns : 2 * columns, :] = item[...].astype(bf16)
    out_ref[2 * columns :, :] = pack_days(sizes, day[...]).astype(bf16)


def exchange_order(size):
    order = list(range(1, size))
    return [1] + order[:0:-1]


def slot_kernel(sizes, me_ref, *refs):
    owners = sizes.owners
    picks, places, note_ref, lists = refs[4:7], refs[7:10], refs[10], refs[11:14]
    fetch(refs[:3], lists, refs[14])
    me = me_ref[0]
    notes = [[] for _ in range(owners)]
    for t in range(3):
        count, rows, slots = sizes.list_counts[t], sizes.row_counts[t], sizes.slots[t]
        number = lists[t][...]
        owner = number // rows
        row = number % rows
        partner = lax.bitwise_xor(owner, jnp.full_like(owner, me))
        picks[t][...] = onehot(iota((owners * rows, count), 0) == partner * rows + row)
        earlier = onehot(iota((count, count), 0) < iota((count, count), 1))
        owner_hot = iota((owners, count), 0) == owner
        before = jnp.dot(onehot(owner_hot), earlier, preferred_element_type=f32)
        position = jnp.sum(jnp.where(owner_hot, before, 0.0), axis=0, keepdims=True)
        target = partner * slots + position.astype(jnp.int32)
        place = onehot(iota((owners * slots, count), 0) == target)
        places[t][...] = place
        following = (row + 1).astype(bf16)
        for s in range(owners):
            notes[s].append(dot_nt(following, place[s * slots : (s + 1) * slots]) - 1.0)
    blank = jnp.full((1, sizes.rank - sizes.slot_rows), -1.0, f32)
    note_ref[...] = jnp.concatenate(
        [jnp.concatenate(note + [blank], axis=1) for note in notes], axis=0
    )


def table_kernel(sizes, *refs):
    order = exchange_order(sizes.holders) + [0]
    pieces, out_ref = [refs[order.index(j)] for j in range(sizes.holders)], refs[-1]
    columns, rank, day_rows = sizes.columns, sizes.rank, sizes.row_counts[2]
    for j, ref in enumerate(pieces):
        for t in range(2):
            out_ref[t * rank + j * columns : t * rank + (j + 1) * columns, :] = ref[
                t * columns : (t + 1) * columns, :
            ]
    days = jnp.concatenate(
        [unpack_days(sizes, ref[2 * columns :, :].astype(f32)) for ref in pieces], axis=1
    ).astype(bf16)
    for chunk in range(sizes.day_chunks):
        start = 2 * rank + chunk * day_rows
        out_ref[start : start + day_rows, :] = days[:, chunk * LANES : (chunk + 1) * LANES]


def block_kernel(sizes, *refs):
    owners, rank, day_rows = sizes.owners, sizes.rank, sizes.row_counts[2]
    tables, refs = refs[:owners], refs[owners:]
    picks, places = refs[:3], refs[3:6]
    note_ref, status_hbm, own_ref, other_ref = refs[6:10]
    (
        users,
        users_low,
        items,
        items_half_t,
        days,
        user_gradient,
        item_gradient,
        day_gradient,
        scaled_even,
        scaled_odd,
        residual_even,
        residual_odd,
        status,
        semaphores,
    ) = refs[10:]
    pair = 2
    pairs = status.shape[0] // pair
    chunks = [(0, pair)]
    chunks += [((2 * n - 1) * pair, 2 * pair) for n in range(1, pairs // 2)]
    chunks += [((pairs - 1) * pair, pair)]

    def status_copy(start, size, semaphore):
        part = pl.ds(start, size)
        return pltpu.make_async_copy(
            status_hbm.at[0, part], status.at[part], semaphores.at[semaphore]
        )

    for n, (start, size) in enumerate(chunks):
        status_copy(start, size, n).start()

    def pick(t):
        table = jnp.concatenate([ref[t * rank : (t + 1) * rank, :] for ref in tables], axis=1)
        return jnp.dot(table, picks[t][...], preferred_element_type=f32)

    user_values = pick(0).T
    users[...] = user_values
    users_low[...] = user_values.astype(bf16)
    items_t = pick(1)
    items[...] = items_t.T.astype(bf16)
    items_half_t[...] = (0.5 * items_t).astype(bf16)
    starts = [2 * rank + chunk * day_rows for chunk in range(sizes.day_chunks)]
    day_table = jnp.concatenate(
        [
            jnp.concatenate([ref[start : start + day_rows, :] for start in starts], axis=1)
            for ref in tables
        ],
        axis=0,
    )
    days[...] = lax.dot_general(
        picks[2][...], day_table, (((0,), (0,)), ((), ())), preferred_element_type=f32
    )
    user_gradient[...] = jnp.zeros_like(user_gradient)
    item_gradient[...] = jnp.zeros_like(item_gradient)
    count = users.shape[0]

    def residuals(first, scaled, residual):
        for j in range(pair):
            rows = slice(j * count, (j + 1) * count)
            day = days[pl.ds(first + j, 1), :].astype(bf16)
            scaled_values = day * users_low[...]
            scaled[rows, :] = scaled_values
            half_logits = jnp.dot(scaled_values, items_half_t[...], preferred_element_type=f32)
            state = status[first + j]
            residual[rows, :] = (
                state.astype(f32) * (jnp.tanh(half_logits) + jnp.where(state == 1, -1.0, 1.0))
            ).astype(bf16)

    def gradients(first, scaled, residual):
        total = 0.0
        for j in range(pair):
            rows = slice(j * count, (j + 1) * count)
            day = days[pl.ds(first + j, 1), :]
            projected = jnp.dot(residual[rows, :], items[...], preferred_element_type=f32)
            total = total + projected * day
            day_gradient[pl.ds(first + j, 1), :] = jnp.sum(
                projected * users[...], axis=0, keepdims=True
            )
        user_gradient[...] += total
        item_gradient[...] += lax.dot_general(
            residual[...], scaled[...], (((0,), (0,)), ((), ())), preferred_element_type=f32
        )

    even, odd = (scaled_even, residual_even), (scaled_odd, residual_odd)
    status_copy(*chunks[0], 0).wait()
    residuals(0, *even)

    @pl.loop(0, pairs // 2 - 1)
    def _(n):
        first = 2 * n * pair
        status_copy(first + pair, 2 * pair, n + 1).wait()
        residuals(first + pair, *odd)
        gradients(first, *even)
        residuals(first + 2 * pair, *even)
        gradients(first + pair, *odd)

    last = (pairs - 1) * pair
    status_copy(*chunks[-1], len(chunks) - 1).wait()
    residuals(last, *odd)
    gradients(last - pair, *even)
    gradients(last, *odd)

    for t, gradient in enumerate((user_gradient, item_gradient, day_gradient)):
        start, slots = sizes.slot_starts[t], sizes.slots[t]
        values = (0.5 * loss_scale * gradient[...]).astype(bf16)
        placed = jnp.dot(places[t][...], values, preferred_element_type=f32)
        for s in range(owners):
            rows = placed[s * slots : (s + 1) * slots]
            if t == 2:
                note = iota(rows.shape, 0) == sizes.note_row
                rows = jnp.where(note, note_ref[s : s + 1, :], rows)
            out = (own_ref, other_ref)[s % 2]
            for chunk in range(sizes.chunks):
                first = (s // 2) * sizes.message_rows + chunk * sizes.slot_rows + start
                out[first : first + slots, :] = rows[
                    :, chunk * LANES : (chunk + 1) * LANES
                ].astype(bf16)


def hold_kernel(arrived_ref, note_ref, out_ref):
    out_ref[...] = arrived_ref[...]


def merge_kernel(sizes, own_ref, crossed_ref, *outs):
    rows = sizes.message_rows
    for n, out in enumerate(outs):
        start = (n + 1) * rows
        out[:rows, :] = own_ref[start : start + rows, :]
        out[rows:, :] = crossed_ref[start : start + rows, :]


def sum_kernel(sizes, *refs):
    holders, columns = sizes.holders, sizes.columns
    inputs = sizes.owners // 2 + 1
    arrived, outs = refs[:inputs], refs[inputs:]
    day_start = sizes.slot_starts[2]
    totals = [0.0, 0.0, 0.0]
    height = sizes.slot_rows
    messages = [ref.at[: sizes.message_rows] for ref in arrived]
    messages += [ref.at[sizes.message_rows :] for ref in arrived[2:]]
    for ref in messages:
        values = jnp.concatenate(
            [ref[c * height : (c + 1) * height, :] for c in range(sizes.chunks)], axis=1
        )
        notes = ref[day_start : day_start + sizes.slots[2], :].astype(f32)
        rows = notes[sizes.note_row : sizes.note_row + 1, : sizes.slot_rows].astype(jnp.int32)
        for t in range(3):
            start, slots = sizes.slot_starts[t], sizes.slots[t]
            shape = (sizes.row_counts[t], sizes.slot_rows)
            slot = iota(shape, 1)
            mine = (slot >= start) & (slot < start + slots)
            selector = onehot((iota(shape, 0) == rows) & mine)
            totals[t] = totals[t] + jnp.dot(selector, values, preferred_element_type=f32)
    for t in range(3):
        if t < 2:
            turned = totals[t].T.astype(bf16)
            for j in range(holders):
                outs[j][t * columns : (t + 1) * columns, :] = turned[
                    j * columns : (j + 1) * columns
                ]
        else:
            for j in range(holders):
                outs[j][2 * columns :, :] = pack_days(
                    sizes, totals[t][:, j * columns : (j + 1) * columns]
                ).astype(bf16)


def adam_kernel(sizes, *refs):
    holders, columns = sizes.holders, sizes.columns
    pieces = refs[:holders]
    states = refs[holders : holders + 9]
    outs = refs[holders + 9 :]
    total = pieces[0][...].astype(f32)
    for ref in pieces[1:]:
        total = total + ref[...].astype(f32)
    for t in range(3):
        if t < 2:
            gradient = total[t * columns : (t + 1) * columns]
        else:
            gradient = unpack_days(sizes, total[2 * columns :])
        factor, first, second = states[3 * t : 3 * t + 3]
        new_factor, new_first, new_second = outs[3 * t : 3 * t + 3]
        first_value = beta_one * first[...] + (1.0 - beta_one) * gradient
        second_value = beta_two * second[...] + (1.0 - beta_two) * gradient * gradient
        change = (
            learn_rate
            * (first_value / bias_one)
            / (jnp.sqrt(second_value / bias_two) + epsilon)
        )
        new_factor[...] = factor[...] - change
        new_first[...] = first_value
        new_second[...] = second_value


def swap(array, axis, size, bits):
    return lax.ppermute(array, axis, [(i, i ^ bits) for i in range(size)])


def local(
    users_list,
    items_list,
    days_list,
    status,
    user_factor,
    user_first,
    user_second,
    item_factor,
    item_first,
    item_second,
    day_factor,
    day_first,
    day_second,
):
    owners = lax.axis_size("dp")
    holders = lax.axis_size("mp")
    row_counts = (user_factor.shape[0], item_factor.shape[0], day_factor.shape[0])
    list_counts = (users_list.shape[1], items_list.shape[1], days_list.shape[1])
    sizes = Sizes(owners, holders, user_factor.shape[1], row_counts, list_counts)
    shape = jax.ShapeDtypeStruct
    small = pltpu.CompilerParams(vmem_limit_bytes=SMALL_VMEM)

    hbm = pl.BlockSpec(memory_space=pltpu.HBM)
    in_hbm = lambda a: pltpu.with_memory_space_constraint(a, pltpu.HBM)
    tables_in = (user_factor.T, item_factor.T, day_factor)
    piece = pl.pallas_call(
        functools.partial(pack_kernel, sizes),
        out_shape=shape((sizes.piece_rows, LANES), bf16),
        in_specs=[hbm] * 3,
        scratch_shapes=[pltpu.VMEM(a.shape, f32) for a in tables_in]
        + [pltpu.SemaphoreType.DMA((3,))],
        compiler_params=small,
        name="pack",
    )(*[in_hbm(a) for a in tables_in])
    distances = exchange_order(holders)
    pieces = [swap(piece, "mp", holders, bits) for bits in distances] + [piece]

    table = pl.pallas_call(
        functools.partial(table_kernel, sizes),
        out_shape=shape((sizes.table_rows, LANES), bf16),
        compiler_params=small,
        name="table",
    )(*pieces)
    arrived = {bits: swap(table, "dp", owners, bits) for bits in range(2, owners, 2)}
    own_crossed = swap(table, "dp", owners, 1)
    picks_places_notes = pl.pallas_call(
        functools.partial(slot_kernel, sizes),
        out_shape=tuple(
            [shape((owners * row_counts[t], list_counts[t]), bf16) for t in range(3)]
            + [shape((owners * sizes.slots[t], list_counts[t]), bf16) for t in range(3)]
            + [shape((owners, sizes.rank), f32)]
        ),
        in_specs=[pl.BlockSpec(memory_space=pltpu.SMEM)]
        + [hbm] * 3
        + [pl.BlockSpec(memory_space=pl.ANY)],
        scratch_shapes=[pltpu.VMEM((1, count), jnp.int32) for count in list_counts]
        + [pltpu.SemaphoreType.DMA((3,))],
        compiler_params=small,
        name="slots",
    )(
        lax.axis_index("dp").astype(jnp.int32).reshape(1),
        *[in_hbm(a) for a in (users_list, items_list, days_list)],
        table,
    )

    arrived[HOLD] = pl.pallas_call(
        hold_kernel,
        out_shape=shape(table.shape, bf16),
        compiler_params=small,
        name="hold",
    )(arrived[HOLD], picks_places_notes[6])
    tables = [table, own_crossed]
    for bits in range(2, owners, 2):
        tables += [arrived[bits], swap(arrived[bits], "dp", owners, 1)]
    inputs = [*tables, *picks_places_notes]
    users, items, days = list_counts
    half = shape((owners // 2 * sizes.message_rows, LANES), bf16)
    own, other = pl.pallas_call(
        functools.partial(block_kernel, sizes),
        out_shape=(half, half),
        in_specs=[pl.BlockSpec(memory_space=pltpu.VMEM)] * len(inputs) + [hbm],
        scratch_shapes=[
            pltpu.VMEM((users, sizes.rank), f32),
            pltpu.VMEM((users, sizes.rank), bf16),
            pltpu.VMEM((items, sizes.rank), bf16),
            pltpu.VMEM((sizes.rank, items), bf16),
            pltpu.VMEM((days, sizes.rank), f32),
            pltpu.VMEM((users, sizes.rank), f32),
            pltpu.VMEM((items, sizes.rank), f32),
            pltpu.VMEM((days, sizes.rank), f32),
            pltpu.VMEM((2 * users, sizes.rank), bf16),
            pltpu.VMEM((2 * users, sizes.rank), bf16),
            pltpu.VMEM((2 * users, items), bf16),
            pltpu.VMEM((2 * users, items), bf16),
            pltpu.VMEM((days, users, items), jnp.int32),
            pltpu.SemaphoreType.DMA((days // 4 + 1,)),
        ],
        compiler_params=pltpu.CompilerParams(vmem_limit_bytes=BLOCK_VMEM),
        name="block_gradients",
    )(*inputs, in_hbm(status))
    crossed = swap(other, "dp", owners, 1)
    message = shape((2 * sizes.message_rows, LANES), bf16)
    merged = pl.pallas_call(
        functools.partial(merge_kernel, sizes),
        out_shape=tuple([message] * (owners // 2 - 1)),
        compiler_params=small,
        name="merge",
    )(own, crossed)
    returned = [own, crossed]
    returned += [
        swap(merged[bits // 2 - 1], "dp", owners, bits) for bits in range(owners - 2, 0, -2)
    ]

    totals = pl.pallas_call(
        functools.partial(sum_kernel, sizes),
        out_shape=tuple([shape(piece.shape, bf16)] * holders),
        compiler_params=small,
        name="row_sums",
    )(*returned)
    column_totals = [totals[0]] + [
        swap(totals[bits], "mp", holders, bits) for bits in range(holders - 1, 0, -1)
    ]

    states = (
        user_factor.T,
        user_first.T,
        user_second.T,
        item_factor.T,
        item_first.T,
        item_second.T,
        day_factor,
        day_first,
        day_second,
    )
    updated = pl.pallas_call(
        functools.partial(adam_kernel, sizes),
        out_shape=tuple(shape(a.shape, a.dtype) for a in states),
        compiler_params=small,
        name="adam",
    )(*column_totals, *states)
    return tuple(a.T for a in updated[:6]) + tuple(updated[6:])


def solution(mesh):
    block = P(("dp", "mp"), None)
    piece = P("dp", "mp")
    return jax.shard_map(
        local,
        mesh=mesh,
        in_specs=(block, block, block, P(("dp", "mp"), None, None, None)) + (piece,) * 9,
        out_specs=(piece,) * 9,
        check_vma=False,
    )
```

```python
import functools

import jax
import jax.numpy as jnp
from jax import lax
from jax.experimental import pallas as pl
from jax.experimental.pallas import tpu as pltpu
from jax.sharding import PartitionSpec as P

beta_one = 0.9
beta_two = 0.99
bias_one = 1.0 - 0.9**10
bias_two = 1.0 - 0.99**10
learn_rate = 0.01
epsilon = 1e-08
loss_scale = 0.0625

LANES = 128
HOLD = 2
SMALL_VMEM = 16 * 1024 * 1024
BLOCK_VMEM = 48 * 1024 * 1024

f32 = jnp.float32
bf16 = jnp.bfloat16


class Sizes:
    def __init__(self, owners, holders, columns, row_counts, list_counts):
        self.owners = owners
        self.holders = holders
        self.columns = columns
        self.rank = columns * holders
        self.row_counts = row_counts
        self.list_counts = list_counts
        limits = (
            max(2, 3 * list_counts[0] // (2 * owners)),
            max(2, 3 * list_counts[1] // (2 * owners)),
            max(2, 2 * list_counts[2] // owners),
        )
        self.slots = tuple(-(-(limit + t // 2) // 16) * 16 for t, limit in enumerate(limits))
        self.note_row = limits[2]
        self.slot_starts = (0, self.slots[0], self.slots[0] + self.slots[1])
        self.slot_rows = sum(self.slots)
        self.day_parts = LANES // columns
        self.day_packed = -(-(row_counts[2] // self.day_parts) // 16) * 16
        self.piece_rows = 2 * columns + self.day_packed
        self.day_chunks = self.rank // LANES
        self.table_rows = 2 * self.rank + self.day_chunks * row_counts[2]


def iota(shape, dimension):
    return lax.broadcasted_iota(jnp.int32, shape, dimension)


def onehot(condition):
    return jnp.where(condition, 1.0, 0.0).astype(bf16)


def dot_nt(a, b):
    return lax.dot_general(a, b, (((1,), (1,)), ((), ())), preferred_element_type=f32)


def pack_days(sizes, days):
    rows = sizes.row_counts[2] // sizes.day_parts
    parts = [days[p * rows : (p + 1) * rows] for p in range(sizes.day_parts)]
    if rows != sizes.day_packed:
        blank = jnp.zeros((sizes.day_packed - rows, days.shape[1]), days.dtype)
        parts = [jnp.concatenate([part, blank], axis=0) for part in parts]
    return jnp.concatenate(parts, axis=1)


def unpack_days(sizes, packed):
    rows = sizes.row_counts[2] // sizes.day_parts
    return jnp.concatenate(
        [
            packed[:rows, p * sizes.columns : (p + 1) * sizes.columns]
            for p in range(sizes.day_parts)
        ],
        axis=0,
    )


def fetch(sources, targets, semaphores):
    copies = [
        pltpu.make_async_copy(source, target, semaphores.at[n])
        for n, (source, target) in enumerate(zip(sources, targets))
    ]
    for copy in copies:
        copy.start()
    for copy in copies:
        copy.wait()


def pack_kernel(sizes, user_hbm, item_hbm, day_hbm, out_ref, user, item, day, semaphores):
    columns = sizes.columns
    fetch((user_hbm, item_hbm, day_hbm), (user, item, day), semaphores)
    out_ref[:columns, :] = user[...].astype(bf16)
    out_ref[columns : 2 * columns, :] = item[...].astype(bf16)
    out_ref[2 * columns :, :] = pack_days(sizes, day[...]).astype(bf16)


def exchange_order(size):
    order = list(range(1, size))
    return [1] + order[:0:-1]


def slot_kernel(sizes, me_ref, *refs):
    owners = sizes.owners
    picks, places, note_ref, lists = refs[4:7], refs[7:10], refs[10], refs[11:14]
    fetch(refs[:3], lists, refs[14])
    me = me_ref[0]
    notes = [[] for _ in range(owners)]
    for t in range(3):
        count, rows, slots = sizes.list_counts[t], sizes.row_counts[t], sizes.slots[t]
        number = lists[t][...]
        owner = number // rows
        row = number % rows
        partner = lax.bitwise_xor(owner, jnp.full_like(owner, me))
        picks[t][...] = onehot(iota((owners * rows, count), 0) == partner * rows + row)
        earlier = onehot(iota((count, count), 0) < iota((count, count), 1))
        owner_hot = iota((owners, count), 0) == owner
        before = jnp.dot(onehot(owner_hot), earlier, preferred_element_type=f32)
        position = jnp.sum(jnp.where(owner_hot, before, 0.0), axis=0, keepdims=True)
        target = partner * slots + position.astype(jnp.int32)
        place = onehot(iota((owners * slots, count), 0) == target)
        places[t][...] = place
        following = (row + 1).astype(bf16)
        for s in range(owners):
            notes[s].append(dot_nt(following, place[s * slots : (s + 1) * slots]) - 1.0)
    blank = jnp.full((1, sizes.rank - sizes.slot_rows), -1.0, f32)
    note_ref[...] = jnp.concatenate(
        [jnp.concatenate(note + [blank], axis=1) for note in notes], axis=0
    )


def table_kernel(sizes, *refs):
    order = exchange_order(sizes.holders) + [0]
    pieces, out_ref = [refs[order.index(j)] for j in range(sizes.holders)], refs[-1]
    columns, rank, day_rows = sizes.columns, sizes.rank, sizes.row_counts[2]
    for j, ref in enumerate(pieces):
        for t in range(2):
            out_ref[t * rank + j * columns : t * rank + (j + 1) * columns, :] = ref[
                t * columns : (t + 1) * columns, :
            ]
    days = jnp.concatenate(
        [unpack_days(sizes, ref[2 * columns :, :].astype(f32)) for ref in pieces], axis=1
    ).astype(bf16)
    for chunk in range(sizes.day_chunks):
        start = 2 * rank + chunk * day_rows
        out_ref[start : start + day_rows, :] = days[:, chunk * LANES : (chunk + 1) * LANES]


def block_kernel(sizes, *refs):
    owners, rank, day_rows = sizes.owners, sizes.rank, sizes.row_counts[2]
    tables, refs = refs[:owners], refs[owners:]
    picks, places = refs[:3], refs[3:6]
    note_ref, status_hbm, own_ref, other_ref = refs[6:10]
    (
        users,
        users_low,
        items,
        items_half_t,
        days,
        user_gradient,
        item_gradient,
        day_gradient,
        scaled_even,
        scaled_odd,
        residual_even,
        residual_odd,
        status,
        semaphores,
    ) = refs[10:]
    pair = 4
    pairs = status.shape[0] // pair
    chunks = [(0, pair)]
    chunks += [((2 * n - 1) * pair, 2 * pair) for n in range(1, pairs // 2)]
    chunks += [((pairs - 1) * pair, pair)]

    def status_copy(start, size, semaphore):
        part = pl.ds(start, size)
        return pltpu.make_async_copy(
            status_hbm.at[0, part], status.at[part], semaphores.at[semaphore]
        )

    for n, (start, size) in enumerate(chunks):
        status_copy(start, size, n).start()

    def pick(t):
        table = jnp.concatenate([ref[t * rank : (t + 1) * rank, :] for ref in tables], axis=1)
        return jnp.dot(table, picks[t][...], preferred_element_type=f32)

    user_values = pick(0).T
    users[...] = user_values
    users_low[...] = user_values.astype(bf16)
    items_t = pick(1)
    items[...] = items_t.T.astype(bf16)
    items_half_t[...] = (0.5 * items_t).astype(bf16)
    starts = [2 * rank + chunk * day_rows for chunk in range(sizes.day_chunks)]
    day_table = jnp.concatenate(
        [
            jnp.concatenate([ref[start : start + day_rows, :] for start in starts], axis=1)
            for ref in tables
        ],
        axis=0,
    )
    days[...] = lax.dot_general(
        picks[2][...], day_table, (((0,), (0,)), ((), ())), preferred_element_type=f32
    )
    user_gradient[...] = jnp.zeros_like(user_gradient)
    item_gradient[...] = jnp.zeros_like(item_gradient)
    count = users.shape[0]

    def residuals(first, scaled, residual):
        for j in range(pair):
            rows = slice(j * count, (j + 1) * count)
            day = days[pl.ds(first + j, 1), :].astype(bf16)
            scaled_values = day * users_low[...]
            scaled[rows, :] = scaled_values
            half_logits = jnp.dot(scaled_values, items_half_t[...], preferred_element_type=f32)
            state = status[first + j]
            residual[rows, :] = (
                state.astype(f32) * (jnp.tanh(half_logits) + jnp.where(state == 1, -1.0, 1.0))
            ).astype(bf16)

    def gradients(first, scaled, residual):
        total = 0.0
        for j in range(pair):
            rows = slice(j * count, (j + 1) * count)
            day = days[pl.ds(first + j, 1), :]
            projected = jnp.dot(residual[rows, :], items[...], preferred_element_type=f32)
            total = total + projected * day
            day_gradient[pl.ds(first + j, 1), :] = jnp.sum(
                projected * users[...], axis=0, keepdims=True
            )
        user_gradient[...] += total
        item_gradient[...] += lax.dot_general(
            residual[...], scaled[...], (((0,), (0,)), ((), ())), preferred_element_type=f32
        )

    even, odd = (scaled_even, residual_even), (scaled_odd, residual_odd)
    status_copy(*chunks[0], 0).wait()
    residuals(0, *even)

    @pl.loop(0, pairs // 2 - 1)
    def _(n):
        first = 2 * n * pair
        status_copy(first + pair, 2 * pair, n + 1).wait()
        residuals(first + pair, *odd)
        gradients(first, *even)
        residuals(first + 2 * pair, *even)
        gradients(first + pair, *odd)

    last = (pairs - 1) * pair
    status_copy(*chunks[-1], len(chunks) - 1).wait()
    residuals(last, *odd)
    gradients(last - pair, *even)
    gradients(last, *odd)

    for t, gradient in enumerate((user_gradient, item_gradient, day_gradient)):
        start, slots = sizes.slot_starts[t], sizes.slots[t]
        values = (0.5 * loss_scale * gradient[...]).astype(bf16)
        placed = jnp.dot(places[t][...], values, preferred_element_type=f32)
        for s in range(owners):
            rows = placed[s * slots : (s + 1) * slots]
            if t == 2:
                note = iota(rows.shape, 0) == sizes.note_row
                rows = jnp.where(note, note_ref[s : s + 1, :], rows)
            out = (own_ref, other_ref)[s % 2]
            first = (s // 2) * sizes.slot_rows + start
            out[first : first + slots, :] = rows.astype(bf16)


def hold_kernel(arrived_ref, note_ref, out_ref):
    out_ref[...] = arrived_ref[...]


def merge_kernel(sizes, own_ref, crossed_ref, *outs):
    rows = sizes.slot_rows
    for n, out in enumerate(outs):
        start = (n + 1) * rows
        out[:rows, :] = own_ref[start : start + rows, :]
        out[rows:, :] = crossed_ref[start : start + rows, :]


def sum_kernel(sizes, *refs):
    holders, columns = sizes.holders, sizes.columns
    inputs = sizes.owners // 2 + 1
    arrived, outs = refs[:inputs], refs[inputs:]
    day_start = sizes.slot_starts[2]
    totals = [0.0, 0.0, 0.0]
    messages = [ref.at[: sizes.slot_rows] for ref in arrived]
    messages += [ref.at[sizes.slot_rows :] for ref in arrived[2:]]
    for ref in messages:
        notes = ref[day_start : day_start + sizes.slots[2], :].astype(f32)
        rows = notes[sizes.note_row : sizes.note_row + 1, : sizes.slot_rows].astype(jnp.int32)
        for t in range(3):
            start, slots = sizes.slot_starts[t], sizes.slots[t]
            shape = (sizes.row_counts[t], sizes.slot_rows)
            slot = iota(shape, 1)
            mine = (slot >= start) & (slot < start + slots)
            selector = onehot((iota(shape, 0) == rows) & mine)
            totals[t] = totals[t] + jnp.dot(selector, ref[...], preferred_element_type=f32)
    for t in range(3):
        if t < 2:
            turned = totals[t].T.astype(bf16)
            for j in range(holders):
                outs[j][t * columns : (t + 1) * columns, :] = turned[
                    j * columns : (j + 1) * columns
                ]
        else:
            for j in range(holders):
                outs[j][2 * columns :, :] = pack_days(
                    sizes, totals[t][:, j * columns : (j + 1) * columns]
                ).astype(bf16)


def adam_kernel(sizes, *refs):
    holders, columns = sizes.holders, sizes.columns
    pieces = refs[:holders]
    states = refs[holders : holders + 9]
    outs = refs[holders + 9 :]
    total = pieces[0][...].astype(f32)
    for ref in pieces[1:]:
        total = total + ref[...].astype(f32)
    for t in range(3):
        if t < 2:
            gradient = total[t * columns : (t + 1) * columns]
        else:
            gradient = unpack_days(sizes, total[2 * columns :])
        factor, first, second = states[3 * t : 3 * t + 3]
        new_factor, new_first, new_second = outs[3 * t : 3 * t + 3]
        first_value = beta_one * first[...] + (1.0 - beta_one) * gradient
        second_value = beta_two * second[...] + (1.0 - beta_two) * gradient * gradient
        change = (
            learn_rate
            * (first_value / bias_one)
            / (jnp.sqrt(second_value / bias_two) + epsilon)
        )
        new_factor[...] = factor[...] - change
        new_first[...] = first_value
        new_second[...] = second_value


def swap(array, axis, size, bits):
    return lax.ppermute(array, axis, [(i, i ^ bits) for i in range(size)])


def local(
    users_list,
    items_list,
    days_list,
    status,
    user_factor,
    user_first,
    user_second,
    item_factor,
    item_first,
    item_second,
    day_factor,
    day_first,
    day_second,
):
    owners = lax.axis_size("dp")
    holders = lax.axis_size("mp")
    row_counts = (user_factor.shape[0], item_factor.shape[0], day_factor.shape[0])
    list_counts = (users_list.shape[1], items_list.shape[1], days_list.shape[1])
    sizes = Sizes(owners, holders, user_factor.shape[1], row_counts, list_counts)
    shape = jax.ShapeDtypeStruct
    small = pltpu.CompilerParams(vmem_limit_bytes=SMALL_VMEM)

    hbm = pl.BlockSpec(memory_space=pltpu.HBM)
    in_hbm = lambda a: pltpu.with_memory_space_constraint(a, pltpu.HBM)
    tables_in = (user_factor.T, item_factor.T, day_factor)
    piece = pl.pallas_call(
        functools.partial(pack_kernel, sizes),
        out_shape=shape((sizes.piece_rows, LANES), bf16),
        in_specs=[hbm] * 3,
        scratch_shapes=[pltpu.VMEM(a.shape, f32) for a in tables_in]
        + [pltpu.SemaphoreType.DMA((3,))],
        compiler_params=small,
        name="pack",
    )(*[in_hbm(a) for a in tables_in])
    distances = exchange_order(holders)
    pieces = [swap(piece, "mp", holders, bits) for bits in distances] + [piece]

    table = pl.pallas_call(
        functools.partial(table_kernel, sizes),
        out_shape=shape((sizes.table_rows, LANES), bf16),
        compiler_params=small,
        name="table",
    )(*pieces)
    arrived = {bits: swap(table, "dp", owners, bits) for bits in range(2, owners, 2)}
    own_crossed = swap(table, "dp", owners, 1)
    picks_places_notes = pl.pallas_call(
        functools.partial(slot_kernel, sizes),
        out_shape=tuple(
            [shape((owners * row_counts[t], list_counts[t]), bf16) for t in range(3)]
            + [shape((owners * sizes.slots[t], list_counts[t]), bf16) for t in range(3)]
            + [shape((owners, sizes.rank), f32)]
        ),
        in_specs=[pl.BlockSpec(memory_space=pltpu.SMEM)]
        + [hbm] * 3
        + [pl.BlockSpec(memory_space=pl.ANY)],
        scratch_shapes=[pltpu.VMEM((1, count), jnp.int32) for count in list_counts]
        + [pltpu.SemaphoreType.DMA((3,))],
        compiler_params=small,
        name="slots",
    )(
        lax.axis_index("dp").astype(jnp.int32).reshape(1),
        *[in_hbm(a) for a in (users_list, items_list, days_list)],
        table,
    )

    arrived[HOLD] = pl.pallas_call(
        hold_kernel,
        out_shape=shape(table.shape, bf16),
        compiler_params=small,
        name="hold",
    )(arrived[HOLD], picks_places_notes[6])
    tables = [table, own_crossed]
    for bits in range(2, owners, 2):
        tables += [arrived[bits], swap(arrived[bits], "dp", owners, 1)]
    inputs = [*tables, *picks_places_notes]
    users, items, days = list_counts
    half = shape((owners // 2 * sizes.slot_rows, sizes.rank), bf16)
    own, other = pl.pallas_call(
        functools.partial(block_kernel, sizes),
        out_shape=(half, half),
        in_specs=[pl.BlockSpec(memory_space=pltpu.VMEM)] * len(inputs) + [hbm],
        scratch_shapes=[
            pltpu.VMEM((users, sizes.rank), f32),
            pltpu.VMEM((users, sizes.rank), bf16),
            pltpu.VMEM((items, sizes.rank), bf16),
            pltpu.VMEM((sizes.rank, items), bf16),
            pltpu.VMEM((days, sizes.rank), f32),
            pltpu.VMEM((users, sizes.rank), f32),
            pltpu.VMEM((items, sizes.rank), f32),
            pltpu.VMEM((days, sizes.rank), f32),
            pltpu.VMEM((4 * users, sizes.rank), bf16),
            pltpu.VMEM((4 * users, sizes.rank), bf16),
            pltpu.VMEM((4 * users, items), bf16),
            pltpu.VMEM((4 * users, items), bf16),
            pltpu.VMEM((days, users, items), jnp.int32),
            pltpu.SemaphoreType.DMA((days // 8 + 1,)),
        ],
        compiler_params=pltpu.CompilerParams(vmem_limit_bytes=BLOCK_VMEM),
        name="block_gradients",
    )(*inputs, in_hbm(status))
    crossed = swap(other, "dp", owners, 1)
    message = shape((2 * sizes.slot_rows, sizes.rank), bf16)
    merged = pl.pallas_call(
        functools.partial(merge_kernel, sizes),
        out_shape=tuple([message] * (owners // 2 - 1)),
        compiler_params=small,
        name="merge",
    )(own, crossed)
    returned = [own, crossed]
    returned += [
        swap(merged[bits // 2 - 1], "dp", owners, bits) for bits in range(owners - 2, 0, -2)
    ]

    totals = pl.pallas_call(
        functools.partial(sum_kernel, sizes),
        out_shape=tuple([shape(piece.shape, bf16)] * holders),
        compiler_params=small,
        name="row_sums",
    )(*returned)
    column_totals = [totals[0]] + [
        swap(totals[bits], "mp", holders, bits) for bits in range(holders - 1, 0, -1)
    ]

    states = (
        user_factor.T,
        user_first.T,
        user_second.T,
        item_factor.T,
        item_first.T,
        item_second.T,
        day_factor,
        day_first,
        day_second,
    )
    updated = pl.pallas_call(
        functools.partial(adam_kernel, sizes),
        out_shape=tuple(shape(a.shape, a.dtype) for a in states),
        compiler_params=small,
        name="adam",
    )(*column_totals, *states)
    return tuple(a.T for a in updated[:6]) + tuple(updated[6:])


def solution(mesh):
    block = P(("dp", "mp"), None)
    piece = P("dp", "mp")
    return jax.shard_map(
        local,
        mesh=mesh,
        in_specs=(block, block, block, P(("dp", "mp"), None, None, None)) + (piece,) * 9,
        out_specs=(piece,) * 9,
        check_vma=False,
    )
```

```python
import functools

import jax
import jax.numpy as jnp
from jax import lax
from jax.experimental import pallas as pl
from jax.experimental.pallas import tpu as pltpu
from jax.sharding import PartitionSpec as P

beta_one = 0.9
beta_two = 0.99
bias_one = 1.0 - 0.9**10
bias_two = 1.0 - 0.99**10
learn_rate = 0.01
epsilon = 1e-08
loss_scale = 0.0625

LANES = 128
HOLD = 2
SMALL_VMEM = 16 * 1024 * 1024
BLOCK_VMEM = 48 * 1024 * 1024

f32 = jnp.float32
bf16 = jnp.bfloat16


class Sizes:
    def __init__(self, owners, holders, columns, row_counts, list_counts):
        self.owners = owners
        self.holders = holders
        self.columns = columns
        self.rank = columns * holders
        self.row_counts = row_counts
        self.list_counts = list_counts
        limits = (
            max(2, 3 * list_counts[0] // (2 * owners)),
            max(2, 3 * list_counts[1] // (2 * owners)),
            max(2, 2 * list_counts[2] // owners),
        )
        self.slots = tuple(-(-(limit + t // 2) // 16) * 16 for t, limit in enumerate(limits))
        self.note_row = limits[2]
        self.slot_starts = (0, self.slots[0], self.slots[0] + self.slots[1])
        self.slot_rows = sum(self.slots)
        self.day_parts = LANES // columns
        self.day_packed = -(-(row_counts[2] // self.day_parts) // 16) * 16
        self.piece_rows = 2 * columns + self.day_packed
        self.day_chunks = self.rank // LANES
        self.table_rows = 2 * self.rank + self.day_chunks * row_counts[2]


def iota(shape, dimension):
    return lax.broadcasted_iota(jnp.int32, shape, dimension)


def onehot(condition):
    return jnp.where(condition, 1.0, 0.0).astype(bf16)


def dot_nt(a, b):
    return lax.dot_general(a, b, (((1,), (1,)), ((), ())), preferred_element_type=f32)


def pack_days(sizes, days):
    rows = sizes.row_counts[2] // sizes.day_parts
    parts = [days[p * rows : (p + 1) * rows] for p in range(sizes.day_parts)]
    if rows != sizes.day_packed:
        blank = jnp.zeros((sizes.day_packed - rows, days.shape[1]), days.dtype)
        parts = [jnp.concatenate([part, blank], axis=0) for part in parts]
    return jnp.concatenate(parts, axis=1)


def unpack_days(sizes, packed):
    rows = sizes.row_counts[2] // sizes.day_parts
    return jnp.concatenate(
        [
            packed[:rows, p * sizes.columns : (p + 1) * sizes.columns]
            for p in range(sizes.day_parts)
        ],
        axis=0,
    )


def fetch(sources, targets, semaphores):
    copies = [
        pltpu.make_async_copy(source, target, semaphores.at[n])
        for n, (source, target) in enumerate(zip(sources, targets))
    ]
    for copy in copies:
        copy.start()
    for copy in copies:
        copy.wait()


def pack_kernel(sizes, user_hbm, item_hbm, day_hbm, out_ref, user, item, day, semaphores):
    columns = sizes.columns
    fetch((user_hbm, item_hbm, day_hbm), (user, item, day), semaphores)
    out_ref[:columns, :] = user[...].astype(bf16)
    out_ref[columns : 2 * columns, :] = item[...].astype(bf16)
    out_ref[2 * columns :, :] = pack_days(sizes, day[...]).astype(bf16)


def exchange_order(size):
    order = list(range(1, size))
    return [1] + order[:0:-1]


def slot_kernel(sizes, me_ref, *refs):
    owners = sizes.owners
    picks, places, note_ref, lists = refs[4:7], refs[7:10], refs[10], refs[11:14]
    fetch(refs[:3], lists, refs[14])
    me = me_ref[0]
    notes = [[] for _ in range(owners)]
    for t in range(3):
        count, rows, slots = sizes.list_counts[t], sizes.row_counts[t], sizes.slots[t]
        number = lists[t][...]
        owner = number // rows
        row = number % rows
        partner = lax.bitwise_xor(owner, jnp.full_like(owner, me))
        picks[t][...] = onehot(iota((owners * rows, count), 0) == partner * rows + row)
        earlier = onehot(iota((count, count), 0) < iota((count, count), 1))
        owner_hot = iota((owners, count), 0) == owner
        before = jnp.dot(onehot(owner_hot), earlier, preferred_element_type=f32)
        position = jnp.sum(jnp.where(owner_hot, before, 0.0), axis=0, keepdims=True)
        target = partner * slots + position.astype(jnp.int32)
        place = onehot(iota((owners * slots, count), 0) == target)
        places[t][...] = place
        following = (row + 1).astype(bf16)
        for s in range(owners):
            notes[s].append(dot_nt(following, place[s * slots : (s + 1) * slots]) - 1.0)
    blank = jnp.full((1, sizes.rank - sizes.slot_rows), -1.0, f32)
    note_ref[...] = jnp.concatenate(
        [jnp.concatenate(note + [blank], axis=1) for note in notes], axis=0
    )


def table_kernel(sizes, *refs):
    order = exchange_order(sizes.holders) + [0]
    pieces, out_ref = [refs[order.index(j)] for j in range(sizes.holders)], refs[-1]
    columns, rank, day_rows = sizes.columns, sizes.rank, sizes.row_counts[2]
    for j, ref in enumerate(pieces):
        for t in range(2):
            out_ref[t * rank + j * columns : t * rank + (j + 1) * columns, :] = ref[
                t * columns : (t + 1) * columns, :
            ]
    days = jnp.concatenate(
        [unpack_days(sizes, ref[2 * columns :, :].astype(f32)) for ref in pieces], axis=1
    ).astype(bf16)
    for chunk in range(sizes.day_chunks):
        start = 2 * rank + chunk * day_rows
        out_ref[start : start + day_rows, :] = days[:, chunk * LANES : (chunk + 1) * LANES]


def block_kernel(sizes, *refs):
    owners, rank, day_rows = sizes.owners, sizes.rank, sizes.row_counts[2]
    tables, refs = refs[:owners], refs[owners:]
    picks, places = refs[:3], refs[3:6]
    note_ref, status_hbm, own_ref, other_ref = refs[6:10]
    (
        users,
        users_low,
        items,
        items_half_t,
        days,
        user_gradient,
        item_gradient,
        day_gradient,
        scaled_even,
        scaled_odd,
        residual_even,
        residual_odd,
        status,
        semaphores,
    ) = refs[10:]
    pair = 4
    pairs = status.shape[0] // pair
    chunks = [(0, pair)]
    chunks += [((2 * n - 1) * pair, 2 * pair) for n in range(1, pairs // 2)]
    chunks += [((pairs - 1) * pair, pair)]

    def status_copy(start, size, semaphore):
        part = pl.ds(start, size)
        return pltpu.make_async_copy(
            status_hbm.at[0, part], status.at[part], semaphores.at[semaphore]
        )

    for n, (start, size) in enumerate(chunks):
        status_copy(start, size, n).start()

    def pick(t):
        table = jnp.concatenate([ref[t * rank : (t + 1) * rank, :] for ref in tables], axis=1)
        return jnp.dot(table, picks[t][...], preferred_element_type=f32)

    user_values = pick(0).T
    users[...] = user_values
    users_low[...] = user_values.astype(bf16)
    items_t = pick(1)
    items[...] = items_t.T.astype(bf16)
    items_half_t[...] = (0.5 * items_t).astype(bf16)
    starts = [2 * rank + chunk * day_rows for chunk in range(sizes.day_chunks)]
    day_table = jnp.concatenate(
        [
            jnp.concatenate([ref[start : start + day_rows, :] for start in starts], axis=1)
            for ref in tables
        ],
        axis=0,
    )
    days[...] = lax.dot_general(
        picks[2][...], day_table, (((0,), (0,)), ((), ())), preferred_element_type=f32
    )
    user_gradient[...] = jnp.zeros_like(user_gradient)
    item_gradient[...] = jnp.zeros_like(item_gradient)
    count = users.shape[0]

    def residuals(first, scaled, residual):
        for j in range(pair):
            day = days[pl.ds(first + j, 1), :].astype(bf16)
            scaled[j * count : (j + 1) * count, :] = day * users_low[...]
        half_logits = jnp.dot(scaled[...], items_half_t[...], preferred_element_type=f32)
        for j in range(pair):
            rows = slice(j * count, (j + 1) * count)
            state = status[first + j]
            residual[rows, :] = (
                state.astype(f32)
                * (jnp.tanh(half_logits[rows]) + jnp.where(state == 1, -1.0, 1.0))
            ).astype(bf16)

    def gradients(first, scaled, residual):
        projected = jnp.dot(residual[...], items[...], preferred_element_type=f32)
        total = 0.0
        for j in range(pair):
            part = projected[j * count : (j + 1) * count]
            day = days[pl.ds(first + j, 1), :]
            total = total + part * day
            day_gradient[pl.ds(first + j, 1), :] = jnp.sum(
                part * users[...], axis=0, keepdims=True
            )
        user_gradient[...] += total
        item_gradient[...] += lax.dot_general(
            residual[...], scaled[...], (((0,), (0,)), ((), ())), preferred_element_type=f32
        )

    even, odd = (scaled_even, residual_even), (scaled_odd, residual_odd)
    status_copy(*chunks[0], 0).wait()
    residuals(0, *even)

    @pl.loop(0, pairs // 2 - 1)
    def _(n):
        first = 2 * n * pair
        status_copy(first + pair, 2 * pair, n + 1).wait()
        residuals(first + pair, *odd)
        gradients(first, *even)
        residuals(first + 2 * pair, *even)
        gradients(first + pair, *odd)

    last = (pairs - 1) * pair
    status_copy(*chunks[-1], len(chunks) - 1).wait()
    residuals(last, *odd)
    gradients(last - pair, *even)
    gradients(last, *odd)

    for t, gradient in enumerate((user_gradient, item_gradient, day_gradient)):
        start, slots = sizes.slot_starts[t], sizes.slots[t]
        values = (0.5 * loss_scale * gradient[...]).astype(bf16)
        placed = jnp.dot(places[t][...], values, preferred_element_type=f32)
        for s in range(owners):
            rows = placed[s * slots : (s + 1) * slots]
            if t == 2:
                note = iota(rows.shape, 0) == sizes.note_row
                rows = jnp.where(note, note_ref[s : s + 1, :], rows)
            out = (own_ref, other_ref)[s % 2]
            first = (s // 2) * sizes.slot_rows + start
            out[first : first + slots, :] = rows.astype(bf16)


def hold_kernel(arrived_ref, note_ref, out_ref):
    out_ref[...] = arrived_ref[...]


def merge_kernel(sizes, own_ref, crossed_ref, *outs):
    rows = sizes.slot_rows
    for n, out in enumerate(outs):
        start = (n + 1) * rows
        out[:rows, :] = own_ref[start : start + rows, :]
        out[rows:, :] = crossed_ref[start : start + rows, :]


def sum_kernel(sizes, *refs):
    holders, columns = sizes.holders, sizes.columns
    inputs = sizes.owners // 2 + 1
    arrived, outs = refs[:inputs], refs[inputs:]
    day_start = sizes.slot_starts[2]
    totals = [0.0, 0.0, 0.0]
    messages = [ref.at[: sizes.slot_rows] for ref in arrived]
    messages += [ref.at[sizes.slot_rows :] for ref in arrived[2:]]
    for ref in messages:
        notes = ref[day_start : day_start + sizes.slots[2], :].astype(f32)
        rows = notes[sizes.note_row : sizes.note_row + 1, : sizes.slot_rows].astype(jnp.int32)
        for t in range(3):
            start, slots = sizes.slot_starts[t], sizes.slots[t]
            shape = (sizes.row_counts[t], sizes.slot_rows)
            slot = iota(shape, 1)
            mine = (slot >= start) & (slot < start + slots)
            selector = onehot((iota(shape, 0) == rows) & mine)
            totals[t] = totals[t] + jnp.dot(selector, ref[...], preferred_element_type=f32)
    for t in range(3):
        if t < 2:
            turned = totals[t].T.astype(bf16)
            for j in range(holders):
                outs[j][t * columns : (t + 1) * columns, :] = turned[
                    j * columns : (j + 1) * columns
                ]
        else:
            for j in range(holders):
                outs[j][2 * columns :, :] = pack_days(
                    sizes, totals[t][:, j * columns : (j + 1) * columns]
                ).astype(bf16)


def adam_kernel(sizes, *refs):
    holders, columns = sizes.holders, sizes.columns
    pieces = refs[:holders]
    states = refs[holders : holders + 9]
    outs = refs[holders + 9 :]
    total = pieces[0][...].astype(f32)
    for ref in pieces[1:]:
        total = total + ref[...].astype(f32)
    for t in range(3):
        if t < 2:
            gradient = total[t * columns : (t + 1) * columns]
        else:
            gradient = unpack_days(sizes, total[2 * columns :])
        factor, first, second = states[3 * t : 3 * t + 3]
        new_factor, new_first, new_second = outs[3 * t : 3 * t + 3]
        first_value = beta_one * first[...] + (1.0 - beta_one) * gradient
        second_value = beta_two * second[...] + (1.0 - beta_two) * gradient * gradient
        change = (
            learn_rate
            * (first_value / bias_one)
            / (jnp.sqrt(second_value / bias_two) + epsilon)
        )
        new_factor[...] = factor[...] - change
        new_first[...] = first_value
        new_second[...] = second_value


def swap(array, axis, size, bits):
    return lax.ppermute(array, axis, [(i, i ^ bits) for i in range(size)])


def local(
    users_list,
    items_list,
    days_list,
    status,
    user_factor,
    user_first,
    user_second,
    item_factor,
    item_first,
    item_second,
    day_factor,
    day_first,
    day_second,
):
    owners = lax.axis_size("dp")
    holders = lax.axis_size("mp")
    row_counts = (user_factor.shape[0], item_factor.shape[0], day_factor.shape[0])
    list_counts = (users_list.shape[1], items_list.shape[1], days_list.shape[1])
    sizes = Sizes(owners, holders, user_factor.shape[1], row_counts, list_counts)
    shape = jax.ShapeDtypeStruct
    small = pltpu.CompilerParams(vmem_limit_bytes=SMALL_VMEM)

    hbm = pl.BlockSpec(memory_space=pltpu.HBM)
    in_hbm = lambda a: pltpu.with_memory_space_constraint(a, pltpu.HBM)
    tables_in = (user_factor.T, item_factor.T, day_factor)
    piece = pl.pallas_call(
        functools.partial(pack_kernel, sizes),
        out_shape=shape((sizes.piece_rows, LANES), bf16),
        in_specs=[hbm] * 3,
        scratch_shapes=[pltpu.VMEM(a.shape, f32) for a in tables_in]
        + [pltpu.SemaphoreType.DMA((3,))],
        compiler_params=small,
        name="pack",
    )(*[in_hbm(a) for a in tables_in])
    distances = exchange_order(holders)
    pieces = [swap(piece, "mp", holders, bits) for bits in distances] + [piece]

    table = pl.pallas_call(
        functools.partial(table_kernel, sizes),
        out_shape=shape((sizes.table_rows, LANES), bf16),
        compiler_params=small,
        name="table",
    )(*pieces)
    arrived = {bits: swap(table, "dp", owners, bits) for bits in range(2, owners, 2)}
    own_crossed = swap(table, "dp", owners, 1)
    picks_places_notes = pl.pallas_call(
        functools.partial(slot_kernel, sizes),
        out_shape=tuple(
            [shape((owners * row_counts[t], list_counts[t]), bf16) for t in range(3)]
            + [shape((owners * sizes.slots[t], list_counts[t]), bf16) for t in range(3)]
            + [shape((owners, sizes.rank), f32)]
        ),
        in_specs=[pl.BlockSpec(memory_space=pltpu.SMEM)]
        + [hbm] * 3
        + [pl.BlockSpec(memory_space=pl.ANY)],
        scratch_shapes=[pltpu.VMEM((1, count), jnp.int32) for count in list_counts]
        + [pltpu.SemaphoreType.DMA((3,))],
        compiler_params=small,
        name="slots",
    )(
        lax.axis_index("dp").astype(jnp.int32).reshape(1),
        *[in_hbm(a) for a in (users_list, items_list, days_list)],
        table,
    )

    arrived[HOLD] = pl.pallas_call(
        hold_kernel,
        out_shape=shape(table.shape, bf16),
        compiler_params=small,
        name="hold",
    )(arrived[HOLD], picks_places_notes[6])
    tables = [table, own_crossed]
    for bits in range(2, owners, 2):
        tables += [arrived[bits], swap(arrived[bits], "dp", owners, 1)]
    inputs = [*tables, *picks_places_notes]
    users, items, days = list_counts
    half = shape((owners // 2 * sizes.slot_rows, sizes.rank), bf16)
    own, other = pl.pallas_call(
        functools.partial(block_kernel, sizes),
        out_shape=(half, half),
        in_specs=[pl.BlockSpec(memory_space=pltpu.VMEM)] * len(inputs) + [hbm],
        scratch_shapes=[
            pltpu.VMEM((users, sizes.rank), f32),
            pltpu.VMEM((users, sizes.rank), bf16),
            pltpu.VMEM((items, sizes.rank), bf16),
            pltpu.VMEM((sizes.rank, items), bf16),
            pltpu.VMEM((days, sizes.rank), f32),
            pltpu.VMEM((users, sizes.rank), f32),
            pltpu.VMEM((items, sizes.rank), f32),
            pltpu.VMEM((days, sizes.rank), f32),
            pltpu.VMEM((4 * users, sizes.rank), bf16),
            pltpu.VMEM((4 * users, sizes.rank), bf16),
            pltpu.VMEM((4 * users, items), bf16),
            pltpu.VMEM((4 * users, items), bf16),
            pltpu.VMEM((days, users, items), jnp.int32),
            pltpu.SemaphoreType.DMA((days // 8 + 1,)),
        ],
        compiler_params=pltpu.CompilerParams(vmem_limit_bytes=BLOCK_VMEM),
        name="block_gradients",
    )(*inputs, in_hbm(status))
    crossed = swap(other, "dp", owners, 1)
    message = shape((2 * sizes.slot_rows, sizes.rank), bf16)
    merged = pl.pallas_call(
        functools.partial(merge_kernel, sizes),
        out_shape=tuple([message] * (owners // 2 - 1)),
        compiler_params=small,
        name="merge",
    )(own, crossed)
    returned = [own, crossed]
    returned += [
        swap(merged[bits // 2 - 1], "dp", owners, bits) for bits in range(owners - 2, 0, -2)
    ]

    totals = pl.pallas_call(
        functools.partial(sum_kernel, sizes),
        out_shape=tuple([shape(piece.shape, bf16)] * holders),
        compiler_params=small,
        name="row_sums",
    )(*returned)
    column_totals = [totals[0]] + [
        swap(totals[bits], "mp", holders, bits) for bits in range(holders - 1, 0, -1)
    ]

    states = (
        user_factor.T,
        user_first.T,
        user_second.T,
        item_factor.T,
        item_first.T,
        item_second.T,
        day_factor,
        day_first,
        day_second,
    )
    updated = pl.pallas_call(
        functools.partial(adam_kernel, sizes),
        out_shape=tuple(shape(a.shape, a.dtype) for a in states),
        compiler_params=small,
        name="adam",
    )(*column_totals, *states)
    return tuple(a.T for a in updated[:6]) + tuple(updated[6:])


def solution(mesh):
    block = P(("dp", "mp"), None)
    piece = P("dp", "mp")
    return jax.shard_map(
        local,
        mesh=mesh,
        in_specs=(block, block, block, P(("dp", "mp"), None, None, None)) + (piece,) * 9,
        out_specs=(piece,) * 9,
        check_vma=False,
    )
```

```python
import functools

import jax
import jax.numpy as jnp
from jax import lax
from jax.experimental import pallas as pl
from jax.experimental.pallas import tpu as pltpu
from jax.sharding import PartitionSpec as P

beta_one = 0.9
beta_two = 0.99
bias_one = 1.0 - 0.9**10
bias_two = 1.0 - 0.99**10
learn_rate = 0.01
epsilon = 1e-08
loss_scale = 0.0625

LANES = 128
HOLD = 2
SMALL_VMEM = 16 * 1024 * 1024
BLOCK_VMEM = 24 * 1024 * 1024

f32 = jnp.float32
bf16 = jnp.bfloat16


class Sizes:
    def __init__(self, owners, holders, columns, row_counts, list_counts):
        self.owners = owners
        self.holders = holders
        self.columns = columns
        self.rank = columns * holders
        self.row_counts = row_counts
        self.list_counts = list_counts
        limits = (
            max(2, 3 * list_counts[0] // (2 * owners)),
            max(2, 3 * list_counts[1] // (2 * owners)),
            max(2, 2 * list_counts[2] // owners),
        )
        self.slots = tuple(-(-(limit + t // 2) // 16) * 16 for t, limit in enumerate(limits))
        self.note_row = limits[2]
        self.slot_starts = (0, self.slots[0], self.slots[0] + self.slots[1])
        self.slot_rows = sum(self.slots)
        self.day_parts = LANES // columns
        self.day_packed = -(-(row_counts[2] // self.day_parts) // 16) * 16
        self.piece_rows = 2 * columns + self.day_packed
        self.day_chunks = self.rank // LANES
        self.table_rows = 2 * self.rank + self.day_chunks * row_counts[2]


def iota(shape, dimension):
    return lax.broadcasted_iota(jnp.int32, shape, dimension)


def onehot(condition):
    return jnp.where(condition, 1.0, 0.0).astype(bf16)


def dot_nt(a, b):
    return lax.dot_general(a, b, (((1,), (1,)), ((), ())), preferred_element_type=f32)


def pack_days(sizes, days):
    rows = sizes.row_counts[2] // sizes.day_parts
    parts = [days[p * rows : (p + 1) * rows] for p in range(sizes.day_parts)]
    if rows != sizes.day_packed:
        blank = jnp.zeros((sizes.day_packed - rows, days.shape[1]), days.dtype)
        parts = [jnp.concatenate([part, blank], axis=0) for part in parts]
    return jnp.concatenate(parts, axis=1)


def unpack_days(sizes, packed):
    rows = sizes.row_counts[2] // sizes.day_parts
    return jnp.concatenate(
        [
            packed[:rows, p * sizes.columns : (p + 1) * sizes.columns]
            for p in range(sizes.day_parts)
        ],
        axis=0,
    )


def fetch(sources, targets, semaphores):
    copies = [
        pltpu.make_async_copy(source, target, semaphores.at[n])
        for n, (source, target) in enumerate(zip(sources, targets))
    ]
    for copy in copies:
        copy.start()
    for copy in copies:
        copy.wait()


def pack_kernel(sizes, user_hbm, item_hbm, day_hbm, out_ref, user, item, day, semaphores):
    columns = sizes.columns
    fetch((user_hbm, item_hbm, day_hbm), (user, item, day), semaphores)
    out_ref[:columns, :] = user[...].astype(bf16)
    out_ref[columns : 2 * columns, :] = item[...].astype(bf16)
    out_ref[2 * columns :, :] = pack_days(sizes, day[...]).astype(bf16)


def exchange_order(size):
    order = list(range(1, size))
    return [1] + order[:0:-1]


def slot_kernel(sizes, me_ref, *refs):
    owners = sizes.owners
    picks, places, note_ref, status_ref = refs[5:8], refs[8:11], refs[11], refs[12]
    lists, semaphores, status_semaphore = refs[13:16], refs[16], refs[17]
    status_copy = pltpu.make_async_copy(refs[4].at[0], status_ref, status_semaphore.at[0])
    fetch(refs[:3], lists, semaphores)
    status_copy.start()
    me = me_ref[0]
    notes = [[] for _ in range(owners)]
    for t in range(3):
        count, rows, slots = sizes.list_counts[t], sizes.row_counts[t], sizes.slots[t]
        number = lists[t][...]
        owner = number // rows
        row = number % rows
        partner = lax.bitwise_xor(owner, jnp.full_like(owner, me))
        picks[t][...] = onehot(iota((owners * rows, count), 0) == partner * rows + row)
        earlier = onehot(iota((count, count), 0) < iota((count, count), 1))
        owner_hot = iota((owners, count), 0) == owner
        before = jnp.dot(onehot(owner_hot), earlier, preferred_element_type=f32)
        position = jnp.sum(jnp.where(owner_hot, before, 0.0), axis=0, keepdims=True)
        target = partner * slots + position.astype(jnp.int32)
        place = onehot(iota((owners * slots, count), 0) == target)
        places[t][...] = place
        following = (row + 1).astype(bf16)
        for s in range(owners):
            notes[s].append(dot_nt(following, place[s * slots : (s + 1) * slots]) - 1.0)
    blank = jnp.full((1, sizes.rank - sizes.slot_rows), -1.0, f32)
    note_ref[...] = jnp.concatenate(
        [jnp.concatenate(note + [blank], axis=1) for note in notes], axis=0
    )
    status_copy.wait()


def table_kernel(sizes, *refs):
    order = exchange_order(sizes.holders) + [0]
    pieces, out_ref = [refs[order.index(j)] for j in range(sizes.holders)], refs[-1]
    columns, rank, day_rows = sizes.columns, sizes.rank, sizes.row_counts[2]
    for j, ref in enumerate(pieces):
        for t in range(2):
            out_ref[t * rank + j * columns : t * rank + (j + 1) * columns, :] = ref[
                t * columns : (t + 1) * columns, :
            ]
    days = jnp.concatenate(
        [unpack_days(sizes, ref[2 * columns :, :].astype(f32)) for ref in pieces], axis=1
    ).astype(bf16)
    for chunk in range(sizes.day_chunks):
        start = 2 * rank + chunk * day_rows
        out_ref[start : start + day_rows, :] = days[:, chunk * LANES : (chunk + 1) * LANES]


def block_kernel(sizes, *refs):
    owners, rank, day_rows = sizes.owners, sizes.rank, sizes.row_counts[2]
    tables, refs = refs[:owners], refs[owners:]
    picks, places = refs[:3], refs[3:6]
    note_ref, status, own_ref, other_ref = refs[6:10]
    (
        users,
        users_low,
        items,
        items_half_t,
        days,
        user_gradient,
        item_gradient,
        day_gradient,
        scaled_even,
        scaled_odd,
        residual_even,
        residual_odd,
    ) = refs[10:]
    pair = 4
    pairs = status.shape[0] // pair
    def pick(t):
        table = jnp.concatenate([ref[t * rank : (t + 1) * rank, :] for ref in tables], axis=1)
        return jnp.dot(table, picks[t][...], preferred_element_type=f32)

    user_values = pick(0).T
    users[...] = user_values
    users_low[...] = user_values.astype(bf16)
    items_t = pick(1)
    items[...] = items_t.T.astype(bf16)
    items_half_t[...] = (0.5 * items_t).astype(bf16)
    starts = [2 * rank + chunk * day_rows for chunk in range(sizes.day_chunks)]
    day_table = jnp.concatenate(
        [
            jnp.concatenate([ref[start : start + day_rows, :] for start in starts], axis=1)
            for ref in tables
        ],
        axis=0,
    )
    days[...] = lax.dot_general(
        picks[2][...], day_table, (((0,), (0,)), ((), ())), preferred_element_type=f32
    )
    user_gradient[...] = jnp.zeros_like(user_gradient)
    item_gradient[...] = jnp.zeros_like(item_gradient)
    count = users.shape[0]

    def residuals(first, scaled, residual):
        for j in range(pair):
            day = days[pl.ds(first + j, 1), :].astype(bf16)
            scaled[j * count : (j + 1) * count, :] = day * users_low[...]
        half_logits = jnp.dot(scaled[...], items_half_t[...], preferred_element_type=f32)
        for j in range(pair):
            rows = slice(j * count, (j + 1) * count)
            state = status[first + j]
            residual[rows, :] = (
                state.astype(f32)
                * (jnp.tanh(half_logits[rows]) + jnp.where(state == 1, -1.0, 1.0))
            ).astype(bf16)

    def gradients(first, scaled, residual):
        projected = jnp.dot(residual[...], items[...], preferred_element_type=f32)
        total = 0.0
        for j in range(pair):
            part = projected[j * count : (j + 1) * count]
            day = days[pl.ds(first + j, 1), :]
            total = total + part * day
            day_gradient[pl.ds(first + j, 1), :] = jnp.sum(
                part * users[...], axis=0, keepdims=True
            )
        user_gradient[...] += total
        item_gradient[...] += lax.dot_general(
            residual[...], scaled[...], (((0,), (0,)), ((), ())), preferred_element_type=f32
        )

    even, odd = (scaled_even, residual_even), (scaled_odd, residual_odd)
    residuals(0, *even)

    @pl.loop(0, pairs // 2 - 1)
    def _(n):
        first = 2 * n * pair
        residuals(first + pair, *odd)
        gradients(first, *even)
        residuals(first + 2 * pair, *even)
        gradients(first + pair, *odd)

    last = (pairs - 1) * pair
    residuals(last, *odd)
    gradients(last - pair, *even)
    gradients(last, *odd)

    for t, gradient in enumerate((user_gradient, item_gradient, day_gradient)):
        start, slots = sizes.slot_starts[t], sizes.slots[t]
        values = (0.5 * loss_scale * gradient[...]).astype(bf16)
        placed = jnp.dot(places[t][...], values, preferred_element_type=f32)
        for s in range(owners):
            rows = placed[s * slots : (s + 1) * slots]
            if t == 2:
                note = iota(rows.shape, 0) == sizes.note_row
                rows = jnp.where(note, note_ref[s : s + 1, :], rows)
            out = (own_ref, other_ref)[s % 2]
            first = (s // 2) * sizes.slot_rows + start
            out[first : first + slots, :] = rows.astype(bf16)


def hold_kernel(arrived_ref, note_ref, out_ref):
    out_ref[...] = arrived_ref[...]


def merge_kernel(sizes, own_ref, crossed_ref, *outs):
    rows = sizes.slot_rows
    for n, out in enumerate(outs):
        start = (n + 1) * rows
        out[:rows, :] = own_ref[start : start + rows, :]
        out[rows:, :] = crossed_ref[start : start + rows, :]


def sum_kernel(sizes, *refs):
    holders, columns = sizes.holders, sizes.columns
    inputs = sizes.owners // 2 + 1
    arrived, outs = refs[:inputs], refs[inputs:]
    day_start = sizes.slot_starts[2]
    totals = [0.0, 0.0, 0.0]
    messages = [ref.at[: sizes.slot_rows] for ref in arrived]
    messages += [ref.at[sizes.slot_rows :] for ref in arrived[2:]]
    for ref in messages:
        notes = ref[day_start : day_start + sizes.slots[2], :].astype(f32)
        rows = notes[sizes.note_row : sizes.note_row + 1, : sizes.slot_rows].astype(jnp.int32)
        for t in range(3):
            start, slots = sizes.slot_starts[t], sizes.slots[t]
            shape = (sizes.row_counts[t], sizes.slot_rows)
            slot = iota(shape, 1)
            mine = (slot >= start) & (slot < start + slots)
            selector = onehot((iota(shape, 0) == rows) & mine)
            totals[t] = totals[t] + jnp.dot(selector, ref[...], preferred_element_type=f32)
    for t in range(3):
        if t < 2:
            turned = totals[t].T.astype(bf16)
            for j in range(holders):
                outs[j][t * columns : (t + 1) * columns, :] = turned[
                    j * columns : (j + 1) * columns
                ]
        else:
            for j in range(holders):
                outs[j][2 * columns :, :] = pack_days(
                    sizes, totals[t][:, j * columns : (j + 1) * columns]
                ).astype(bf16)


def adam_kernel(sizes, *refs):
    holders, columns = sizes.holders, sizes.columns
    pieces = refs[:holders]
    states = refs[holders : holders + 9]
    outs = refs[holders + 9 :]
    total = pieces[0][...].astype(f32)
    for ref in pieces[1:]:
        total = total + ref[...].astype(f32)
    for t in range(3):
        if t < 2:
            gradient = total[t * columns : (t + 1) * columns]
        else:
            gradient = unpack_days(sizes, total[2 * columns :])
        factor, first, second = states[3 * t : 3 * t + 3]
        new_factor, new_first, new_second = outs[3 * t : 3 * t + 3]
        first_value = beta_one * first[...] + (1.0 - beta_one) * gradient
        second_value = beta_two * second[...] + (1.0 - beta_two) * gradient * gradient
        change = (
            learn_rate
            * (first_value / bias_one)
            / (jnp.sqrt(second_value / bias_two) + epsilon)
        )
        new_factor[...] = factor[...] - change
        new_first[...] = first_value
        new_second[...] = second_value


def swap(array, axis, size, bits):
    return lax.ppermute(array, axis, [(i, i ^ bits) for i in range(size)])


def local(
    users_list,
    items_list,
    days_list,
    status,
    user_factor,
    user_first,
    user_second,
    item_factor,
    item_first,
    item_second,
    day_factor,
    day_first,
    day_second,
):
    owners = lax.axis_size("dp")
    holders = lax.axis_size("mp")
    row_counts = (user_factor.shape[0], item_factor.shape[0], day_factor.shape[0])
    list_counts = (users_list.shape[1], items_list.shape[1], days_list.shape[1])
    sizes = Sizes(owners, holders, user_factor.shape[1], row_counts, list_counts)
    shape = jax.ShapeDtypeStruct
    small = pltpu.CompilerParams(vmem_limit_bytes=SMALL_VMEM)

    hbm = pl.BlockSpec(memory_space=pltpu.HBM)
    in_hbm = lambda a: pltpu.with_memory_space_constraint(a, pltpu.HBM)
    tables_in = (user_factor.T, item_factor.T, day_factor)
    piece = pl.pallas_call(
        functools.partial(pack_kernel, sizes),
        out_shape=shape((sizes.piece_rows, LANES), bf16),
        in_specs=[hbm] * 3,
        scratch_shapes=[pltpu.VMEM(a.shape, f32) for a in tables_in]
        + [pltpu.SemaphoreType.DMA((3,))],
        compiler_params=small,
        name="pack",
    )(*[in_hbm(a) for a in tables_in])
    distances = exchange_order(holders)
    pieces = [swap(piece, "mp", holders, bits) for bits in distances] + [piece]

    table = pl.pallas_call(
        functools.partial(table_kernel, sizes),
        out_shape=shape((sizes.table_rows, LANES), bf16),
        compiler_params=small,
        name="table",
    )(*pieces)
    arrived = {bits: swap(table, "dp", owners, bits) for bits in range(2, owners, 2)}
    own_crossed = swap(table, "dp", owners, 1)
    picks_places_notes = pl.pallas_call(
        functools.partial(slot_kernel, sizes),
        out_shape=tuple(
            [shape((owners * row_counts[t], list_counts[t]), bf16) for t in range(3)]
            + [shape((owners * sizes.slots[t], list_counts[t]), bf16) for t in range(3)]
            + [shape((owners, sizes.rank), f32), shape(status.shape[1:], jnp.int32)]
        ),
        in_specs=[pl.BlockSpec(memory_space=pltpu.SMEM)]
        + [hbm] * 3
        + [pl.BlockSpec(memory_space=pl.ANY), hbm],
        scratch_shapes=[pltpu.VMEM((1, count), jnp.int32) for count in list_counts]
        + [pltpu.SemaphoreType.DMA((3,)), pltpu.SemaphoreType.DMA((1,))],
        compiler_params=small,
        name="slots",
    )(
        lax.axis_index("dp").astype(jnp.int32).reshape(1),
        *[in_hbm(a) for a in (users_list, items_list, days_list)],
        table,
        in_hbm(status),
    )

    arrived[HOLD] = pl.pallas_call(
        hold_kernel,
        out_shape=shape(table.shape, bf16),
        compiler_params=small,
        name="hold",
    )(arrived[HOLD], picks_places_notes[6])
    tables = [table, own_crossed]
    for bits in range(2, owners, 2):
        tables += [arrived[bits], swap(arrived[bits], "dp", owners, 1)]
    inputs = [*tables, *picks_places_notes]
    users, items, days = list_counts
    half = shape((owners // 2 * sizes.slot_rows, sizes.rank), bf16)
    own, other = pl.pallas_call(
        functools.partial(block_kernel, sizes),
        out_shape=(half, half),
        in_specs=[pl.BlockSpec(memory_space=pltpu.VMEM)] * len(inputs),
        scratch_shapes=[
            pltpu.VMEM((users, sizes.rank), f32),
            pltpu.VMEM((users, sizes.rank), bf16),
            pltpu.VMEM((items, sizes.rank), bf16),
            pltpu.VMEM((sizes.rank, items), bf16),
            pltpu.VMEM((days, sizes.rank), f32),
            pltpu.VMEM((users, sizes.rank), f32),
            pltpu.VMEM((items, sizes.rank), f32),
            pltpu.VMEM((days, sizes.rank), f32),
            pltpu.VMEM((4 * users, sizes.rank), bf16),
            pltpu.VMEM((4 * users, sizes.rank), bf16),
            pltpu.VMEM((4 * users, items), bf16),
            pltpu.VMEM((4 * users, items), bf16),
        ],
        compiler_params=pltpu.CompilerParams(vmem_limit_bytes=BLOCK_VMEM),
        name="block_gradients",
    )(*inputs)
    crossed = swap(other, "dp", owners, 1)
    message = shape((2 * sizes.slot_rows, sizes.rank), bf16)
    merged = pl.pallas_call(
        functools.partial(merge_kernel, sizes),
        out_shape=tuple([message] * (owners // 2 - 1)),
        compiler_params=small,
        name="merge",
    )(own, crossed)
    returned = [own, crossed]
    returned += [
        swap(merged[bits // 2 - 1], "dp", owners, bits) for bits in range(owners - 2, 0, -2)
    ]

    totals = pl.pallas_call(
        functools.partial(sum_kernel, sizes),
        out_shape=tuple([shape(piece.shape, bf16)] * holders),
        compiler_params=small,
        name="row_sums",
    )(*returned)
    column_totals = [totals[0]] + [
        swap(totals[bits], "mp", holders, bits) for bits in range(holders - 1, 0, -1)
    ]

    states = (
        user_factor.T,
        user_first.T,
        user_second.T,
        item_factor.T,
        item_first.T,
        item_second.T,
        day_factor,
        day_first,
        day_second,
    )
    updated = pl.pallas_call(
        functools.partial(adam_kernel, sizes),
        out_shape=tuple(shape(a.shape, a.dtype) for a in states),
        compiler_params=small,
        name="adam",
    )(*column_totals, *states)
    return tuple(a.T for a in updated[:6]) + tuple(updated[6:])


def solution(mesh):
    block = P(("dp", "mp"), None)
    piece = P("dp", "mp")
    return jax.shard_map(
        local,
        mesh=mesh,
        in_specs=(block, block, block, P(("dp", "mp"), None, None, None)) + (piece,) * 9,
        out_specs=(piece,) * 9,
        check_vma=False,
    )
```

```python
import functools

import jax
import jax.numpy as jnp
from jax import lax
from jax.experimental import pallas as pl
from jax.experimental.pallas import tpu as pltpu
from jax.sharding import PartitionSpec as P

beta_one = 0.9
beta_two = 0.99
bias_one = 1.0 - 0.9**10
bias_two = 1.0 - 0.99**10
learn_rate = 0.01
epsilon = 1e-08
loss_scale = 0.0625

LANES = 128
HOLD = 2
SMALL_VMEM = 16 * 1024 * 1024
LARGE_VMEM = 32 * 1024 * 1024
STATUS_PARTS = 4

f32 = jnp.float32
bf16 = jnp.bfloat16


class Sizes:
    def __init__(self, owners, holders, columns, row_counts, list_counts):
        self.owners = owners
        self.holders = holders
        self.columns = columns
        self.rank = columns * holders
        self.row_counts = row_counts
        self.list_counts = list_counts
        limits = (
            max(2, 3 * list_counts[0] // (2 * owners)),
            max(2, 3 * list_counts[1] // (2 * owners)),
            max(2, 2 * list_counts[2] // owners),
        )
        self.slots = tuple(-(-(limit + t // 2) // 16) * 16 for t, limit in enumerate(limits))
        self.note_row = limits[2]
        self.slot_starts = (0, self.slots[0], self.slots[0] + self.slots[1])
        self.slot_rows = sum(self.slots)
        self.day_parts = LANES // columns
        self.day_packed = -(-(row_counts[2] // self.day_parts) // 16) * 16
        self.piece_rows = 2 * columns + self.day_packed
        self.day_chunks = self.rank // LANES
        self.table_rows = 2 * self.rank + self.day_chunks * row_counts[2]


def iota(shape, dimension):
    return lax.broadcasted_iota(jnp.int32, shape, dimension)


def onehot(condition):
    return jnp.where(condition, 1.0, 0.0).astype(bf16)


def dot_nt(a, b):
    return lax.dot_general(a, b, (((1,), (1,)), ((), ())), preferred_element_type=f32)


def pack_days(sizes, days):
    rows = sizes.row_counts[2] // sizes.day_parts
    parts = [days[p * rows : (p + 1) * rows] for p in range(sizes.day_parts)]
    if rows != sizes.day_packed:
        blank = jnp.zeros((sizes.day_packed - rows, days.shape[1]), days.dtype)
        parts = [jnp.concatenate([part, blank], axis=0) for part in parts]
    return jnp.concatenate(parts, axis=1)


def unpack_days(sizes, packed):
    rows = sizes.row_counts[2] // sizes.day_parts
    return jnp.concatenate(
        [
            packed[:rows, p * sizes.columns : (p + 1) * sizes.columns]
            for p in range(sizes.day_parts)
        ],
        axis=0,
    )


def fetch(sources, targets, semaphores):
    copies = [
        pltpu.make_async_copy(source, target, semaphores.at[n])
        for n, (source, target) in enumerate(zip(sources, targets))
    ]
    for copy in copies:
        copy.start()
    for copy in copies:
        copy.wait()


def pack_kernel(sizes, user_hbm, item_hbm, day_hbm, out_ref, user, item, day, semaphores):
    columns = sizes.columns
    fetch((user_hbm, item_hbm, day_hbm), (user, item, day), semaphores)
    out_ref[:columns, :] = user[...].astype(bf16)
    out_ref[columns : 2 * columns, :] = item[...].astype(bf16)
    out_ref[2 * columns :, :] = pack_days(sizes, day[...]).astype(bf16)


def exchange_order(size):
    order = list(range(1, size))
    return [1] + order[:0:-1]


def slot_kernel(sizes, me_ref, *refs):
    owners = sizes.owners
    picks, places, note_ref, weight_ref, shift_ref = refs[5:8], refs[8:11], *refs[11:14]
    lists, semaphores, status, status_semaphores = refs[14:17], *refs[17:20]
    size = status.shape[0] // STATUS_PARTS

    def status_copy(n):
        part = pl.ds(n * size, size)
        return pltpu.make_async_copy(
            refs[4].at[0, part], status.at[part], status_semaphores.at[n]
        )

    fetch(refs[:3], lists, semaphores)
    for n in range(STATUS_PARTS):
        status_copy(n).start()
    me = me_ref[0]
    notes = [[] for _ in range(owners)]
    for t in range(3):
        count, rows, slots = sizes.list_counts[t], sizes.row_counts[t], sizes.slots[t]
        number = lists[t][...]
        owner = number // rows
        row = number % rows
        partner = lax.bitwise_xor(owner, jnp.full_like(owner, me))
        picks[t][...] = onehot(iota((owners * rows, count), 0) == partner * rows + row)
        earlier = onehot(iota((count, count), 0) < iota((count, count), 1))
        owner_hot = iota((owners, count), 0) == owner
        before = jnp.dot(onehot(owner_hot), earlier, preferred_element_type=f32)
        position = jnp.sum(jnp.where(owner_hot, before, 0.0), axis=0, keepdims=True)
        target = partner * slots + position.astype(jnp.int32)
        place = onehot(iota((owners * slots, count), 0) == target)
        places[t][...] = place
        following = (row + 1).astype(bf16)
        for s in range(owners):
            notes[s].append(dot_nt(following, place[s * slots : (s + 1) * slots]) - 1.0)
    blank = jnp.full((1, sizes.rank - sizes.slot_rows), -1.0, f32)
    note_ref[...] = jnp.concatenate(
        [jnp.concatenate(note + [blank], axis=1) for note in notes], axis=0
    )
    for n in range(STATUS_PARTS):
        status_copy(n).wait()

        @pl.loop(n * size, (n + 1) * size)
        def _(k):
            state = status[k]
            weight = state.astype(f32)
            weight_ref[k] = weight
            shift_ref[k] = jnp.where(state == 1, -weight, weight)


def table_kernel(sizes, *refs):
    order = exchange_order(sizes.holders) + [0]
    pieces, out_ref = [refs[order.index(j)] for j in range(sizes.holders)], refs[-1]
    columns, rank, day_rows = sizes.columns, sizes.rank, sizes.row_counts[2]
    for j, ref in enumerate(pieces):
        for t in range(2):
            out_ref[t * rank + j * columns : t * rank + (j + 1) * columns, :] = ref[
                t * columns : (t + 1) * columns, :
            ]
    days = jnp.concatenate(
        [unpack_days(sizes, ref[2 * columns :, :].astype(f32)) for ref in pieces], axis=1
    ).astype(bf16)
    for chunk in range(sizes.day_chunks):
        start = 2 * rank + chunk * day_rows
        out_ref[start : start + day_rows, :] = days[:, chunk * LANES : (chunk + 1) * LANES]


def block_kernel(sizes, *refs):
    owners, rank, day_rows = sizes.owners, sizes.rank, sizes.row_counts[2]
    tables, refs = refs[:owners], refs[owners:]
    picks, places = refs[:3], refs[3:6]
    note_ref, weights, shifts, own_ref, other_ref = refs[6:11]
    (
        users,
        users_low,
        items,
        items_half_t,
        days,
        user_gradient,
        item_gradient,
        day_gradient,
        scaled_even,
        scaled_odd,
        residual_even,
        residual_odd,
    ) = refs[11:]
    pair = 4
    pairs = weights.shape[0] // pair
    def pick(t):
        table = jnp.concatenate([ref[t * rank : (t + 1) * rank, :] for ref in tables], axis=1)
        return jnp.dot(table, picks[t][...], preferred_element_type=f32)

    user_values = pick(0).T
    users[...] = user_values
    users_low[...] = user_values.astype(bf16)
    items_t = pick(1)
    items[...] = items_t.T.astype(bf16)
    items_half_t[...] = (0.5 * items_t).astype(bf16)
    starts = [2 * rank + chunk * day_rows for chunk in range(sizes.day_chunks)]
    day_table = jnp.concatenate(
        [
            jnp.concatenate([ref[start : start + day_rows, :] for start in starts], axis=1)
            for ref in tables
        ],
        axis=0,
    )
    days[...] = lax.dot_general(
        picks[2][...], day_table, (((0,), (0,)), ((), ())), preferred_element_type=f32
    )
    user_gradient[...] = jnp.zeros_like(user_gradient)
    item_gradient[...] = jnp.zeros_like(item_gradient)
    count = users.shape[0]

    def residuals(first, scaled, residual):
        for j in range(pair):
            day = days[pl.ds(first + j, 1), :].astype(bf16)
            scaled[j * count : (j + 1) * count, :] = day * users_low[...]
        half_logits = jnp.dot(scaled[...], items_half_t[...], preferred_element_type=f32)
        for j in range(pair):
            rows = slice(j * count, (j + 1) * count)
            residual[rows, :] = (
                weights[first + j] * jnp.tanh(half_logits[rows]) + shifts[first + j]
            ).astype(bf16)

    def gradients(first, scaled, residual):
        projected = jnp.dot(residual[...], items[...], preferred_element_type=f32)
        total = 0.0
        for j in range(pair):
            part = projected[j * count : (j + 1) * count]
            day = days[pl.ds(first + j, 1), :]
            total = total + part * day
            day_gradient[pl.ds(first + j, 1), :] = jnp.sum(
                part * users[...], axis=0, keepdims=True
            )
        user_gradient[...] += total
        item_gradient[...] += lax.dot_general(
            residual[...], scaled[...], (((0,), (0,)), ((), ())), preferred_element_type=f32
        )

    even, odd = (scaled_even, residual_even), (scaled_odd, residual_odd)
    residuals(0, *even)

    @pl.loop(0, pairs // 2 - 1)
    def _(n):
        first = 2 * n * pair
        residuals(first + pair, *odd)
        gradients(first, *even)
        residuals(first + 2 * pair, *even)
        gradients(first + pair, *odd)

    last = (pairs - 1) * pair
    residuals(last, *odd)
    gradients(last - pair, *even)
    gradients(last, *odd)

    for t, gradient in enumerate((user_gradient, item_gradient, day_gradient)):
        start, slots = sizes.slot_starts[t], sizes.slots[t]
        values = (0.5 * loss_scale * gradient[...]).astype(bf16)
        placed = jnp.dot(places[t][...], values, preferred_element_type=f32)
        for s in range(owners):
            rows = placed[s * slots : (s + 1) * slots]
            if t == 2:
                note = iota(rows.shape, 0) == sizes.note_row
                rows = jnp.where(note, note_ref[s : s + 1, :], rows)
            out = (own_ref, other_ref)[s % 2]
            first = (s // 2) * sizes.slot_rows + start
            out[first : first + slots, :] = rows.astype(bf16)


def hold_kernel(arrived_ref, note_ref, out_ref):
    out_ref[...] = arrived_ref[...]


def merge_kernel(sizes, own_ref, crossed_ref, *outs):
    rows = sizes.slot_rows
    for n, out in enumerate(outs):
        start = (n + 1) * rows
        out[:rows, :] = own_ref[start : start + rows, :]
        out[rows:, :] = crossed_ref[start : start + rows, :]


def sum_kernel(sizes, *refs):
    holders, columns = sizes.holders, sizes.columns
    inputs = sizes.owners // 2 + 1
    arrived, outs = refs[:inputs], refs[inputs:]
    day_start = sizes.slot_starts[2]
    totals = [0.0, 0.0, 0.0]
    messages = [ref.at[: sizes.slot_rows] for ref in arrived]
    messages += [ref.at[sizes.slot_rows :] for ref in arrived[2:]]
    for ref in messages:
        notes = ref[day_start : day_start + sizes.slots[2], :].astype(f32)
        rows = notes[sizes.note_row : sizes.note_row + 1, : sizes.slot_rows].astype(jnp.int32)
        for t in range(3):
            start, slots = sizes.slot_starts[t], sizes.slots[t]
            shape = (sizes.row_counts[t], sizes.slot_rows)
            slot = iota(shape, 1)
            mine = (slot >= start) & (slot < start + slots)
            selector = onehot((iota(shape, 0) == rows) & mine)
            totals[t] = totals[t] + jnp.dot(selector, ref[...], preferred_element_type=f32)
    for t in range(3):
        if t < 2:
            turned = totals[t].T.astype(bf16)
            for j in range(holders):
                outs[j][t * columns : (t + 1) * columns, :] = turned[
                    j * columns : (j + 1) * columns
                ]
        else:
            for j in range(holders):
                outs[j][2 * columns :, :] = pack_days(
                    sizes, totals[t][:, j * columns : (j + 1) * columns]
                ).astype(bf16)


def adam_kernel(sizes, *refs):
    holders, columns = sizes.holders, sizes.columns
    pieces = refs[:holders]
    states = refs[holders : holders + 9]
    outs = refs[holders + 9 :]
    total = pieces[0][...].astype(f32)
    for ref in pieces[1:]:
        total = total + ref[...].astype(f32)
    for t in range(3):
        if t < 2:
            gradient = total[t * columns : (t + 1) * columns]
        else:
            gradient = unpack_days(sizes, total[2 * columns :])
        factor, first, second = states[3 * t : 3 * t + 3]
        new_factor, new_first, new_second = outs[3 * t : 3 * t + 3]
        first_value = beta_one * first[...] + (1.0 - beta_one) * gradient
        second_value = beta_two * second[...] + (1.0 - beta_two) * gradient * gradient
        change = (
            learn_rate
            * (first_value / bias_one)
            / (jnp.sqrt(second_value / bias_two) + epsilon)
        )
        new_factor[...] = factor[...] - change
        new_first[...] = first_value
        new_second[...] = second_value


def swap(array, axis, size, bits):
    return lax.ppermute(array, axis, [(i, i ^ bits) for i in range(size)])


def local(
    users_list,
    items_list,
    days_list,
    status,
    user_factor,
    user_first,
    user_second,
    item_factor,
    item_first,
    item_second,
    day_factor,
    day_first,
    day_second,
):
    owners = lax.axis_size("dp")
    holders = lax.axis_size("mp")
    row_counts = (user_factor.shape[0], item_factor.shape[0], day_factor.shape[0])
    list_counts = (users_list.shape[1], items_list.shape[1], days_list.shape[1])
    sizes = Sizes(owners, holders, user_factor.shape[1], row_counts, list_counts)
    shape = jax.ShapeDtypeStruct
    small = pltpu.CompilerParams(vmem_limit_bytes=SMALL_VMEM)
    large = pltpu.CompilerParams(vmem_limit_bytes=LARGE_VMEM)

    hbm = pl.BlockSpec(memory_space=pltpu.HBM)
    in_hbm = lambda a: pltpu.with_memory_space_constraint(a, pltpu.HBM)
    tables_in = (user_factor.T, item_factor.T, day_factor)
    piece = pl.pallas_call(
        functools.partial(pack_kernel, sizes),
        out_shape=shape((sizes.piece_rows, LANES), bf16),
        in_specs=[hbm] * 3,
        scratch_shapes=[pltpu.VMEM(a.shape, f32) for a in tables_in]
        + [pltpu.SemaphoreType.DMA((3,))],
        compiler_params=small,
        name="pack",
    )(*[in_hbm(a) for a in tables_in])
    distances = exchange_order(holders)
    pieces = [swap(piece, "mp", holders, bits) for bits in distances] + [piece]

    table = pl.pallas_call(
        functools.partial(table_kernel, sizes),
        out_shape=shape((sizes.table_rows, LANES), bf16),
        compiler_params=small,
        name="table",
    )(*pieces)
    arrived = {bits: swap(table, "dp", owners, bits) for bits in range(2, owners, 2)}
    own_crossed = swap(table, "dp", owners, 1)
    picks_places_notes = pl.pallas_call(
        functools.partial(slot_kernel, sizes),
        out_shape=tuple(
            [shape((owners * row_counts[t], list_counts[t]), bf16) for t in range(3)]
            + [shape((owners * sizes.slots[t], list_counts[t]), bf16) for t in range(3)]
            + [shape((owners, sizes.rank), f32)]
            + [shape(status.shape[1:], f32)] * 2
        ),
        in_specs=[pl.BlockSpec(memory_space=pltpu.SMEM)]
        + [hbm] * 3
        + [pl.BlockSpec(memory_space=pl.ANY), hbm],
        scratch_shapes=[pltpu.VMEM((1, count), jnp.int32) for count in list_counts]
        + [
            pltpu.SemaphoreType.DMA((3,)),
            pltpu.VMEM(status.shape[1:], jnp.int32),
            pltpu.SemaphoreType.DMA((STATUS_PARTS,)),
        ],
        compiler_params=large,
        name="slots",
    )(
        lax.axis_index("dp").astype(jnp.int32).reshape(1),
        *[in_hbm(a) for a in (users_list, items_list, days_list)],
        table,
        in_hbm(status),
    )

    arrived[HOLD] = pl.pallas_call(
        hold_kernel,
        out_shape=shape(table.shape, bf16),
        compiler_params=small,
        name="hold",
    )(arrived[HOLD], picks_places_notes[6])
    tables = [table, own_crossed]
    for bits in range(2, owners, 2):
        tables += [arrived[bits], swap(arrived[bits], "dp", owners, 1)]
    inputs = [*tables, *picks_places_notes]
    users, items, days = list_counts
    half = shape((owners // 2 * sizes.slot_rows, sizes.rank), bf16)
    own, other = pl.pallas_call(
        functools.partial(block_kernel, sizes),
        out_shape=(half, half),
        in_specs=[pl.BlockSpec(memory_space=pltpu.VMEM)] * len(inputs),
        scratch_shapes=[
            pltpu.VMEM((users, sizes.rank), f32),
            pltpu.VMEM((users, sizes.rank), bf16),
            pltpu.VMEM((items, sizes.rank), bf16),
            pltpu.VMEM((sizes.rank, items), bf16),
            pltpu.VMEM((days, sizes.rank), f32),
            pltpu.VMEM((users, sizes.rank), f32),
            pltpu.VMEM((items, sizes.rank), f32),
            pltpu.VMEM((days, sizes.rank), f32),
            pltpu.VMEM((4 * users, sizes.rank), bf16),
            pltpu.VMEM((4 * users, sizes.rank), bf16),
            pltpu.VMEM((4 * users, items), bf16),
            pltpu.VMEM((4 * users, items), bf16),
        ],
        compiler_params=large,
        name="block_gradients",
    )(*inputs)
    crossed = swap(other, "dp", owners, 1)
    message = shape((2 * sizes.slot_rows, sizes.rank), bf16)
    merged = pl.pallas_call(
        functools.partial(merge_kernel, sizes),
        out_shape=tuple([message] * (owners // 2 - 1)),
        compiler_params=small,
        name="merge",
    )(own, crossed)
    returned = [own, crossed]
    returned += [swap(merged[bits // 2 - 1], "dp", owners, bits) for bits in range(2, owners, 2)]

    totals = pl.pallas_call(
        functools.partial(sum_kernel, sizes),
        out_shape=tuple([shape(piece.shape, bf16)] * holders),
        compiler_params=small,
        name="row_sums",
    )(*returned)
    column_totals = [totals[0]] + [
        swap(totals[bits], "mp", holders, bits) for bits in range(holders - 1, 0, -1)
    ]

    states = (
        user_factor.T,
        user_first.T,
        user_second.T,
        item_factor.T,
        item_first.T,
        item_second.T,
        day_factor,
        day_first,
        day_second,
    )
    updated = pl.pallas_call(
        functools.partial(adam_kernel, sizes),
        out_shape=tuple(shape(a.shape, a.dtype) for a in states),
        compiler_params=small,
        name="adam",
    )(*column_totals, *states)
    return tuple(a.T for a in updated[:6]) + tuple(updated[6:])


def solution(mesh):
    block = P(("dp", "mp"), None)
    piece = P("dp", "mp")
    return jax.shard_map(
        local,
        mesh=mesh,
        in_specs=(block, block, block, P(("dp", "mp"), None, None, None)) + (piece,) * 9,
        out_specs=(piece,) * 9,
        check_vma=False,
    )
```

```python
import functools

import jax
import jax.numpy as jnp
from jax import lax
from jax.experimental import pallas as pl
from jax.experimental.pallas import tpu as pltpu
from jax.sharding import PartitionSpec as P

beta_one = 0.9
beta_two = 0.99
bias_one = 1.0 - 0.9**10
bias_two = 1.0 - 0.99**10
learn_rate = 0.01
epsilon = 1e-08
loss_scale = 0.0625

LANES = 128
HOLD = 2
SMALL_VMEM = 16 * 1024 * 1024
BLOCK_VMEM = 24 * 1024 * 1024

f32 = jnp.float32
bf16 = jnp.bfloat16


class Sizes:
    def __init__(self, owners, holders, columns, row_counts, list_counts):
        self.owners = owners
        self.holders = holders
        self.columns = columns
        self.rank = columns * holders
        self.row_counts = row_counts
        self.list_counts = list_counts
        limits = (
            max(2, 3 * list_counts[0] // (2 * owners)),
            max(2, 3 * list_counts[1] // (2 * owners)),
            max(2, 2 * list_counts[2] // owners),
        )
        self.slots = tuple(-(-(limit + t // 2) // 16) * 16 for t, limit in enumerate(limits))
        self.note_row = limits[2]
        self.slot_starts = (0, self.slots[0], self.slots[0] + self.slots[1])
        self.slot_rows = sum(self.slots)
        self.day_parts = LANES // columns
        self.day_packed = -(-(row_counts[2] // self.day_parts) // 16) * 16
        self.piece_rows = 2 * columns + self.day_packed
        self.day_chunks = self.rank // LANES
        self.table_rows = 2 * self.rank + self.day_chunks * row_counts[2]


def iota(shape, dimension):
    return lax.broadcasted_iota(jnp.int32, shape, dimension)


def onehot(condition):
    return jnp.where(condition, 1.0, 0.0).astype(bf16)


def dot_nt(a, b):
    return lax.dot_general(a, b, (((1,), (1,)), ((), ())), preferred_element_type=f32)


def pack_days(sizes, days):
    rows = sizes.row_counts[2] // sizes.day_parts
    parts = [days[p * rows : (p + 1) * rows] for p in range(sizes.day_parts)]
    if rows != sizes.day_packed:
        blank = jnp.zeros((sizes.day_packed - rows, days.shape[1]), days.dtype)
        parts = [jnp.concatenate([part, blank], axis=0) for part in parts]
    return jnp.concatenate(parts, axis=1)


def unpack_days(sizes, packed):
    rows = sizes.row_counts[2] // sizes.day_parts
    return jnp.concatenate(
        [
            packed[:rows, p * sizes.columns : (p + 1) * sizes.columns]
            for p in range(sizes.day_parts)
        ],
        axis=0,
    )


def fetch(sources, targets, semaphores):
    copies = [
        pltpu.make_async_copy(source, target, semaphores.at[n])
        for n, (source, target) in enumerate(zip(sources, targets))
    ]
    for copy in copies:
        copy.start()
    for copy in copies:
        copy.wait()


def pack_kernel(sizes, user_hbm, item_hbm, day_hbm, out_ref, user, item, day, semaphores):
    columns = sizes.columns
    fetch((user_hbm, item_hbm, day_hbm), (user, item, day), semaphores)
    out_ref[:columns, :] = user[...].astype(bf16)
    out_ref[columns : 2 * columns, :] = item[...].astype(bf16)
    out_ref[2 * columns :, :] = pack_days(sizes, day[...]).astype(bf16)


def exchange_order(size):
    order = list(range(1, size))
    return [1] + order[:0:-1]


def slot_kernel(sizes, me_ref, *refs):
    owners = sizes.owners
    picks, places, note_ref, status_ref = refs[5:8], refs[8:11], refs[11], refs[12]
    lists, semaphores, status_semaphore = refs[13:16], refs[16], refs[17]
    status_copy = pltpu.make_async_copy(refs[4].at[0], status_ref, status_semaphore.at[0])
    fetch(refs[:3], lists, semaphores)
    status_copy.start()
    me = me_ref[0]
    notes = [[] for _ in range(owners)]
    for t in range(3):
        count, rows, slots = sizes.list_counts[t], sizes.row_counts[t], sizes.slots[t]
        number = lists[t][...]
        owner = number // rows
        row = number % rows
        partner = lax.bitwise_xor(owner, jnp.full_like(owner, me))
        picks[t][...] = onehot(iota((owners * rows, count), 0) == partner * rows + row)
        earlier = onehot(iota((count, count), 0) < iota((count, count), 1))
        owner_hot = iota((owners, count), 0) == owner
        before = jnp.dot(onehot(owner_hot), earlier, preferred_element_type=f32)
        position = jnp.sum(jnp.where(owner_hot, before, 0.0), axis=0, keepdims=True)
        target = partner * slots + position.astype(jnp.int32)
        place = onehot(iota((owners * slots, count), 0) == target)
        places[t][...] = place
        following = (row + 1).astype(bf16)
        for s in range(owners):
            notes[s].append(dot_nt(following, place[s * slots : (s + 1) * slots]) - 1.0)
    blank = jnp.full((1, sizes.rank - sizes.slot_rows), -1.0, f32)
    note_ref[...] = jnp.concatenate(
        [jnp.concatenate(note + [blank], axis=1) for note in notes], axis=0
    )
    status_copy.wait()


def table_kernel(sizes, *refs):
    order = exchange_order(sizes.holders) + [0]
    pieces, out_ref = [refs[order.index(j)] for j in range(sizes.holders)], refs[-1]
    columns, rank, day_rows = sizes.columns, sizes.rank, sizes.row_counts[2]
    for j, ref in enumerate(pieces):
        for t in range(2):
            out_ref[t * rank + j * columns : t * rank + (j + 1) * columns, :] = ref[
                t * columns : (t + 1) * columns, :
            ]
    days = jnp.concatenate(
        [unpack_days(sizes, ref[2 * columns :, :].astype(f32)) for ref in pieces], axis=1
    ).astype(bf16)
    for chunk in range(sizes.day_chunks):
        start = 2 * rank + chunk * day_rows
        out_ref[start : start + day_rows, :] = days[:, chunk * LANES : (chunk + 1) * LANES]


def block_kernel(sizes, *refs):
    owners, rank, day_rows = sizes.owners, sizes.rank, sizes.row_counts[2]
    tables, refs = refs[:owners], refs[owners:]
    picks, places = refs[:3], refs[3:6]
    note_ref, status, own_ref, other_ref = refs[6:10]
    (
        users,
        users_low,
        items,
        items_half_t,
        days,
        user_gradient,
        item_gradient,
        day_gradient,
        scaled_even,
        scaled_odd,
        residual_even,
        residual_odd,
    ) = refs[10:]
    pair = 2
    pairs = status.shape[0] // pair
    def pick(t):
        table = jnp.concatenate([ref[t * rank : (t + 1) * rank, :] for ref in tables], axis=1)
        return jnp.dot(table, picks[t][...], preferred_element_type=f32)

    user_values = pick(0).T
    users[...] = user_values
    users_low[...] = user_values.astype(bf16)
    items_t = pick(1)
    items[...] = items_t.T.astype(bf16)
    items_half_t[...] = (0.5 * items_t).astype(bf16)
    starts = [2 * rank + chunk * day_rows for chunk in range(sizes.day_chunks)]
    day_table = jnp.concatenate(
        [
            jnp.concatenate([ref[start : start + day_rows, :] for start in starts], axis=1)
            for ref in tables
        ],
        axis=0,
    )
    days[...] = lax.dot_general(
        picks[2][...], day_table, (((0,), (0,)), ((), ())), preferred_element_type=f32
    )
    user_gradient[...] = jnp.zeros_like(user_gradient)
    item_gradient[...] = jnp.zeros_like(item_gradient)
    count = users.shape[0]

    def residuals(first, scaled, residual):
        for j in range(pair):
            day = days[pl.ds(first + j, 1), :].astype(bf16)
            scaled[j * count : (j + 1) * count, :] = day * users_low[...]
        half_logits = jnp.dot(scaled[...], items_half_t[...], preferred_element_type=f32)
        for j in range(pair):
            rows = slice(j * count, (j + 1) * count)
            state = status[first + j]
            residual[rows, :] = (
                state.astype(f32)
                * (jnp.tanh(half_logits[rows]) + jnp.where(state == 1, -1.0, 1.0))
            ).astype(bf16)

    def gradients(first, scaled, residual):
        projected = jnp.dot(residual[...], items[...], preferred_element_type=f32)
        total = 0.0
        for j in range(pair):
            part = projected[j * count : (j + 1) * count]
            day = days[pl.ds(first + j, 1), :]
            total = total + part * day
            day_gradient[pl.ds(first + j, 1), :] = jnp.sum(
                part * users[...], axis=0, keepdims=True
            )
        user_gradient[...] += total
        item_gradient[...] += lax.dot_general(
            residual[...], scaled[...], (((0,), (0,)), ((), ())), preferred_element_type=f32
        )

    even, odd = (scaled_even, residual_even), (scaled_odd, residual_odd)
    residuals(0, *even)

    @pl.loop(0, pairs // 2 - 1)
    def _(n):
        first = 2 * n * pair
        residuals(first + pair, *odd)
        gradients(first, *even)
        residuals(first + 2 * pair, *even)
        gradients(first + pair, *odd)

    last = (pairs - 1) * pair
    residuals(last, *odd)
    gradients(last - pair, *even)
    gradients(last, *odd)

    for t, gradient in enumerate((user_gradient, item_gradient, day_gradient)):
        start, slots = sizes.slot_starts[t], sizes.slots[t]
        values = (0.5 * loss_scale * gradient[...]).astype(bf16)
        placed = jnp.dot(places[t][...], values, preferred_element_type=f32)
        for s in range(owners):
            rows = placed[s * slots : (s + 1) * slots]
            if t == 2:
                note = iota(rows.shape, 0) == sizes.note_row
                rows = jnp.where(note, note_ref[s : s + 1, :], rows)
            out = (own_ref, other_ref)[s % 2]
            first = (s // 2) * sizes.slot_rows + start
            out[first : first + slots, :] = rows.astype(bf16)


def hold_kernel(arrived_ref, note_ref, out_ref):
    out_ref[...] = arrived_ref[...]


def merge_kernel(sizes, own_ref, crossed_ref, *outs):
    rows = sizes.slot_rows
    for n, out in enumerate(outs):
        start = (n + 1) * rows
        out[:rows, :] = own_ref[start : start + rows, :]
        out[rows:, :] = crossed_ref[start : start + rows, :]


def sum_kernel(sizes, *refs):
    holders, columns = sizes.holders, sizes.columns
    inputs = sizes.owners // 2 + 1
    arrived, outs = refs[:inputs], refs[inputs:]
    day_start = sizes.slot_starts[2]
    totals = [0.0, 0.0, 0.0]
    messages = [ref.at[: sizes.slot_rows] for ref in arrived]
    messages += [ref.at[sizes.slot_rows :] for ref in arrived[2:]]
    for ref in messages:
        notes = ref[day_start : day_start + sizes.slots[2], :].astype(f32)
        rows = notes[sizes.note_row : sizes.note_row + 1, : sizes.slot_rows].astype(jnp.int32)
        for t in range(3):
            start, slots = sizes.slot_starts[t], sizes.slots[t]
            shape = (sizes.row_counts[t], sizes.slot_rows)
            slot = iota(shape, 1)
            mine = (slot >= start) & (slot < start + slots)
            selector = onehot((iota(shape, 0) == rows) & mine)
            totals[t] = totals[t] + jnp.dot(selector, ref[...], preferred_element_type=f32)
    for t in range(3):
        if t < 2:
            turned = totals[t].T.astype(bf16)
            for j in range(holders):
                outs[j][t * columns : (t + 1) * columns, :] = turned[
                    j * columns : (j + 1) * columns
                ]
        else:
            for j in range(holders):
                outs[j][2 * columns :, :] = pack_days(
                    sizes, totals[t][:, j * columns : (j + 1) * columns]
                ).astype(bf16)


def adam_kernel(sizes, *refs):
    holders, columns = sizes.holders, sizes.columns
    pieces = refs[:holders]
    states = refs[holders : holders + 9]
    outs = refs[holders + 9 :]
    total = pieces[0][...].astype(f32)
    for ref in pieces[1:]:
        total = total + ref[...].astype(f32)
    for t in range(3):
        if t < 2:
            gradient = total[t * columns : (t + 1) * columns]
        else:
            gradient = unpack_days(sizes, total[2 * columns :])
        factor, first, second = states[3 * t : 3 * t + 3]
        new_factor, new_first, new_second = outs[3 * t : 3 * t + 3]
        first_value = beta_one * first[...] + (1.0 - beta_one) * gradient
        second_value = beta_two * second[...] + (1.0 - beta_two) * gradient * gradient
        change = (
            learn_rate
            * (first_value / bias_one)
            / (jnp.sqrt(second_value / bias_two) + epsilon)
        )
        new_factor[...] = factor[...] - change
        new_first[...] = first_value
        new_second[...] = second_value


def swap(array, axis, size, bits):
    return lax.ppermute(array, axis, [(i, i ^ bits) for i in range(size)])


def local(
    users_list,
    items_list,
    days_list,
    status,
    user_factor,
    user_first,
    user_second,
    item_factor,
    item_first,
    item_second,
    day_factor,
    day_first,
    day_second,
):
    owners = lax.axis_size("dp")
    holders = lax.axis_size("mp")
    row_counts = (user_factor.shape[0], item_factor.shape[0], day_factor.shape[0])
    list_counts = (users_list.shape[1], items_list.shape[1], days_list.shape[1])
    sizes = Sizes(owners, holders, user_factor.shape[1], row_counts, list_counts)
    shape = jax.ShapeDtypeStruct
    small = pltpu.CompilerParams(vmem_limit_bytes=SMALL_VMEM)

    hbm = pl.BlockSpec(memory_space=pltpu.HBM)
    in_hbm = lambda a: pltpu.with_memory_space_constraint(a, pltpu.HBM)
    tables_in = (user_factor.T, item_factor.T, day_factor)
    piece = pl.pallas_call(
        functools.partial(pack_kernel, sizes),
        out_shape=shape((sizes.piece_rows, LANES), bf16),
        in_specs=[hbm] * 3,
        scratch_shapes=[pltpu.VMEM(a.shape, f32) for a in tables_in]
        + [pltpu.SemaphoreType.DMA((3,))],
        compiler_params=small,
        name="pack",
    )(*[in_hbm(a) for a in tables_in])
    distances = exchange_order(holders)
    pieces = [swap(piece, "mp", holders, bits) for bits in distances] + [piece]

    table = pl.pallas_call(
        functools.partial(table_kernel, sizes),
        out_shape=shape((sizes.table_rows, LANES), bf16),
        compiler_params=small,
        name="table",
    )(*pieces)
    arrived = {bits: swap(table, "dp", owners, bits) for bits in range(2, owners, 2)}
    own_crossed = swap(table, "dp", owners, 1)
    picks_places_notes = pl.pallas_call(
        functools.partial(slot_kernel, sizes),
        out_shape=tuple(
            [shape((owners * row_counts[t], list_counts[t]), bf16) for t in range(3)]
            + [shape((owners * sizes.slots[t], list_counts[t]), bf16) for t in range(3)]
            + [shape((owners, sizes.rank), f32), shape(status.shape[1:], jnp.int32)]
        ),
        in_specs=[pl.BlockSpec(memory_space=pltpu.SMEM)]
        + [hbm] * 3
        + [pl.BlockSpec(memory_space=pl.ANY), hbm],
        scratch_shapes=[pltpu.VMEM((1, count), jnp.int32) for count in list_counts]
        + [pltpu.SemaphoreType.DMA((3,)), pltpu.SemaphoreType.DMA((1,))],
        compiler_params=small,
        name="slots",
    )(
        lax.axis_index("dp").astype(jnp.int32).reshape(1),
        *[in_hbm(a) for a in (users_list, items_list, days_list)],
        table,
        in_hbm(status),
    )

    arrived[HOLD] = pl.pallas_call(
        hold_kernel,
        out_shape=shape(table.shape, bf16),
        compiler_params=small,
        name="hold",
    )(arrived[HOLD], picks_places_notes[6])
    tables = [table, own_crossed]
    for bits in range(2, owners, 2):
        tables += [arrived[bits], swap(arrived[bits], "dp", owners, 1)]
    inputs = [*tables, *picks_places_notes]
    users, items, days = list_counts
    half = shape((owners // 2 * sizes.slot_rows, sizes.rank), bf16)
    own, other = pl.pallas_call(
        functools.partial(block_kernel, sizes),
        out_shape=(half, half),
        in_specs=[pl.BlockSpec(memory_space=pltpu.VMEM)] * len(inputs),
        scratch_shapes=[
            pltpu.VMEM((users, sizes.rank), f32),
            pltpu.VMEM((users, sizes.rank), bf16),
            pltpu.VMEM((items, sizes.rank), bf16),
            pltpu.VMEM((sizes.rank, items), bf16),
            pltpu.VMEM((days, sizes.rank), f32),
            pltpu.VMEM((users, sizes.rank), f32),
            pltpu.VMEM((items, sizes.rank), f32),
            pltpu.VMEM((days, sizes.rank), f32),
            pltpu.VMEM((2 * users, sizes.rank), bf16),
            pltpu.VMEM((2 * users, sizes.rank), bf16),
            pltpu.VMEM((2 * users, items), bf16),
            pltpu.VMEM((2 * users, items), bf16),
        ],
        compiler_params=pltpu.CompilerParams(vmem_limit_bytes=BLOCK_VMEM),
        name="block_gradients",
    )(*inputs)
    crossed = swap(other, "dp", owners, 1)
    message = shape((2 * sizes.slot_rows, sizes.rank), bf16)
    merged = pl.pallas_call(
        functools.partial(merge_kernel, sizes),
        out_shape=tuple([message] * (owners // 2 - 1)),
        compiler_params=small,
        name="merge",
    )(own, crossed)
    returned = [own, crossed]
    returned += [
        swap(merged[bits // 2 - 1], "dp", owners, bits) for bits in range(owners - 2, 0, -2)
    ]

    totals = pl.pallas_call(
        functools.partial(sum_kernel, sizes),
        out_shape=tuple([shape(piece.shape, bf16)] * holders),
        compiler_params=small,
        name="row_sums",
    )(*returned)
    column_totals = [totals[0]] + [
        swap(totals[bits], "mp", holders, bits) for bits in range(holders - 1, 0, -1)
    ]

    states = (
        user_factor.T,
        user_first.T,
        user_second.T,
        item_factor.T,
        item_first.T,
        item_second.T,
        day_factor,
        day_first,
        day_second,
    )
    updated = pl.pallas_call(
        functools.partial(adam_kernel, sizes),
        out_shape=tuple(shape(a.shape, a.dtype) for a in states),
        compiler_params=small,
        name="adam",
    )(*column_totals, *states)
    return tuple(a.T for a in updated[:6]) + tuple(updated[6:])


def solution(mesh):
    block = P(("dp", "mp"), None)
    piece = P("dp", "mp")
    return jax.shard_map(
        local,
        mesh=mesh,
        in_specs=(block, block, block, P(("dp", "mp"), None, None, None)) + (piece,) * 9,
        out_specs=(piece,) * 9,
        check_vma=False,
    )
```

```python
import functools

import jax
import jax.numpy as jnp
from jax import lax
from jax.experimental import pallas as pl
from jax.experimental.pallas import tpu as pltpu
from jax.sharding import PartitionSpec as P

beta_one = 0.9
beta_two = 0.99
bias_one = 1.0 - 0.9**10
bias_two = 1.0 - 0.99**10
learn_rate = 0.01
epsilon = 1e-08
loss_scale = 0.0625

LANES = 128
HOLD = 2
SMALL_VMEM = 16 * 1024 * 1024
BLOCK_VMEM = 24 * 1024 * 1024

f32 = jnp.float32
bf16 = jnp.bfloat16


class Sizes:
    def __init__(self, owners, holders, columns, row_counts, list_counts):
        self.owners = owners
        self.holders = holders
        self.columns = columns
        self.rank = columns * holders
        self.row_counts = row_counts
        self.list_counts = list_counts
        limits = (
            max(2, 3 * list_counts[0] // (2 * owners)),
            max(2, 3 * list_counts[1] // (2 * owners)),
            max(2, 2 * list_counts[2] // owners),
        )
        self.slots = tuple(-(-(limit + t // 2) // 16) * 16 for t, limit in enumerate(limits))
        self.note_row = limits[2]
        self.slot_starts = (0, self.slots[0], self.slots[0] + self.slots[1])
        self.slot_rows = sum(self.slots)
        self.day_parts = LANES // columns
        self.day_packed = -(-(row_counts[2] // self.day_parts) // 16) * 16
        self.piece_rows = 2 * columns + self.day_packed
        self.day_chunks = self.rank // LANES
        self.table_rows = 2 * self.rank + self.day_chunks * row_counts[2]


def iota(shape, dimension):
    return lax.broadcasted_iota(jnp.int32, shape, dimension)


def onehot(condition):
    return jnp.where(condition, 1.0, 0.0).astype(bf16)


def dot_nt(a, b):
    return lax.dot_general(a, b, (((1,), (1,)), ((), ())), preferred_element_type=f32)


def pack_days(sizes, days):
    rows = sizes.row_counts[2] // sizes.day_parts
    parts = [days[p * rows : (p + 1) * rows] for p in range(sizes.day_parts)]
    if rows != sizes.day_packed:
        blank = jnp.zeros((sizes.day_packed - rows, days.shape[1]), days.dtype)
        parts = [jnp.concatenate([part, blank], axis=0) for part in parts]
    return jnp.concatenate(parts, axis=1)


def unpack_days(sizes, packed):
    rows = sizes.row_counts[2] // sizes.day_parts
    return jnp.concatenate(
        [
            packed[:rows, p * sizes.columns : (p + 1) * sizes.columns]
            for p in range(sizes.day_parts)
        ],
        axis=0,
    )


def fetch(sources, targets, semaphores):
    copies = [
        pltpu.make_async_copy(source, target, semaphores.at[n])
        for n, (source, target) in enumerate(zip(sources, targets))
    ]
    for copy in copies:
        copy.start()
    for copy in copies:
        copy.wait()


def pack_kernel(sizes, user_hbm, item_hbm, day_hbm, out_ref, user, item, day, semaphores):
    columns = sizes.columns
    fetch((user_hbm, item_hbm, day_hbm), (user, item, day), semaphores)
    out_ref[:columns, :] = user[...].astype(bf16)
    out_ref[columns : 2 * columns, :] = item[...].astype(bf16)
    out_ref[2 * columns :, :] = pack_days(sizes, day[...]).astype(bf16)


def exchange_order(size):
    order = list(range(1, size))
    return [1] + order[:0:-1]


def slot_kernel(sizes, me_ref, *refs):
    owners = sizes.owners
    picks, places, note_ref, status_ref = refs[5:8], refs[8:11], refs[11], refs[12]
    lists, semaphores, status_semaphore = refs[13:16], refs[16], refs[17]
    status_copy = pltpu.make_async_copy(refs[4].at[0], status_ref, status_semaphore.at[0])
    fetch(refs[:3], lists, semaphores)
    status_copy.start()
    me = me_ref[0]
    notes = [[] for _ in range(owners)]
    for t in range(3):
        count, rows, slots = sizes.list_counts[t], sizes.row_counts[t], sizes.slots[t]
        number = lists[t][...]
        owner = number // rows
        row = number % rows
        partner = lax.bitwise_xor(owner, jnp.full_like(owner, me))
        picks[t][...] = onehot(iota((owners * rows, count), 0) == partner * rows + row)
        earlier = onehot(iota((count, count), 0) < iota((count, count), 1))
        owner_hot = iota((owners, count), 0) == owner
        before = jnp.dot(onehot(owner_hot), earlier, preferred_element_type=f32)
        position = jnp.sum(jnp.where(owner_hot, before, 0.0), axis=0, keepdims=True)
        target = partner * slots + position.astype(jnp.int32)
        place = onehot(iota((owners * slots, count), 0) == target)
        places[t][...] = place
        following = (row + 1).astype(bf16)
        for s in range(owners):
            notes[s].append(dot_nt(following, place[s * slots : (s + 1) * slots]) - 1.0)
    blank = jnp.full((1, sizes.rank - sizes.slot_rows), -1.0, f32)
    note_ref[...] = jnp.concatenate(
        [jnp.concatenate(note + [blank], axis=1) for note in notes], axis=0
    )
    status_copy.wait()


def table_kernel(sizes, *refs):
    order = exchange_order(sizes.holders) + [0]
    pieces, out_ref = [refs[order.index(j)] for j in range(sizes.holders)], refs[-1]
    columns, rank, day_rows = sizes.columns, sizes.rank, sizes.row_counts[2]
    for j, ref in enumerate(pieces):
        for t in range(2):
            out_ref[t * rank + j * columns : t * rank + (j + 1) * columns, :] = ref[
                t * columns : (t + 1) * columns, :
            ]
    days = jnp.concatenate(
        [unpack_days(sizes, ref[2 * columns :, :].astype(f32)) for ref in pieces], axis=1
    ).astype(bf16)
    for chunk in range(sizes.day_chunks):
        start = 2 * rank + chunk * day_rows
        out_ref[start : start + day_rows, :] = days[:, chunk * LANES : (chunk + 1) * LANES]


def block_kernel(sizes, *refs):
    owners, rank, day_rows = sizes.owners, sizes.rank, sizes.row_counts[2]
    tables, refs = refs[:owners], refs[owners:]
    picks, places = refs[:3], refs[3:6]
    note_ref, status, own_ref, other_ref = refs[6:10]
    (
        users,
        users_low,
        items,
        items_half_t,
        days,
        user_gradient,
        item_gradient,
        day_gradient,
        scaled_even,
        scaled_odd,
        residual_even,
        residual_odd,
    ) = refs[10:]
    pair = 4
    pairs = status.shape[0] // pair

    def pick(t):
        table = jnp.concatenate([ref[t * rank : (t + 1) * rank, :] for ref in tables], axis=1)
        return jnp.dot(table, picks[t][...], preferred_element_type=f32)

    user_values = pick(0).T
    users[...] = user_values
    users_low[...] = user_values.astype(bf16)
    items_t = pick(1)
    items[...] = items_t.T.astype(bf16)
    items_half_t[...] = (0.5 * items_t).astype(bf16)
    starts = [2 * rank + chunk * day_rows for chunk in range(sizes.day_chunks)]
    day_table = jnp.concatenate(
        [
            jnp.concatenate([ref[start : start + day_rows, :] for start in starts], axis=1)
            for ref in tables
        ],
        axis=0,
    )
    days[...] = lax.dot_general(
        picks[2][...], day_table, (((0,), (0,)), ((), ())), preferred_element_type=f32
    )
    user_gradient[...] = jnp.zeros_like(user_gradient)
    item_gradient[...] = jnp.zeros_like(item_gradient)
    count = users.shape[0]

    def residuals(first, scaled, residual):
        for j in range(pair):
            day = days[pl.ds(first + j, 1), :].astype(bf16)
            scaled[j * count : (j + 1) * count, :] = day * users_low[...]
        half_logits = jnp.dot(scaled[...], items_half_t[...], preferred_element_type=f32)
        for j in range(pair):
            rows = slice(j * count, (j + 1) * count)
            state = status[first + j]
            residual[rows, :] = (
                state.astype(f32)
                * (jnp.tanh(half_logits[rows]) + jnp.where(state == 1, -1.0, 1.0))
            ).astype(bf16)

    def gradients(first, scaled, residual):
        projected = jnp.dot(residual[...], items[...], preferred_element_type=f32)
        total = 0.0
        for j in range(pair):
            part = projected[j * count : (j + 1) * count]
            day = days[pl.ds(first + j, 1), :]
            total = total + part * day
            day_gradient[pl.ds(first + j, 1), :] = jnp.sum(
                part * users[...], axis=0, keepdims=True
            )
        user_gradient[...] += total
        item_gradient[...] += lax.dot_general(
            residual[...], scaled[...], (((0,), (0,)), ((), ())), preferred_element_type=f32
        )

    even, odd = (scaled_even, residual_even), (scaled_odd, residual_odd)
    residuals(0, *even)

    for n in range(pairs // 2 - 1):
        first = 2 * n * pair
        residuals(first + pair, *odd)
        gradients(first, *even)
        residuals(first + 2 * pair, *even)
        gradients(first + pair, *odd)

    last = (pairs - 1) * pair
    residuals(last, *odd)
    gradients(last - pair, *even)
    gradients(last, *odd)

    for t, gradient in enumerate((user_gradient, item_gradient, day_gradient)):
        start, slots = sizes.slot_starts[t], sizes.slots[t]
        values = (0.5 * loss_scale * gradient[...]).astype(bf16)
        placed = jnp.dot(places[t][...], values, preferred_element_type=f32)
        for s in range(owners):
            rows = placed[s * slots : (s + 1) * slots]
            if t == 2:
                note = iota(rows.shape, 0) == sizes.note_row
                rows = jnp.where(note, note_ref[s : s + 1, :], rows)
            out = (own_ref, other_ref)[s % 2]
            first = (s // 2) * sizes.slot_rows + start
            out[first : first + slots, :] = rows.astype(bf16)


def hold_kernel(arrived_ref, note_ref, out_ref):
    out_ref[...] = arrived_ref[...]


def merge_kernel(sizes, own_ref, crossed_ref, *outs):
    rows = sizes.slot_rows
    for n, out in enumerate(outs):
        start = (n + 1) * rows
        out[:rows, :] = own_ref[start : start + rows, :]
        out[rows:, :] = crossed_ref[start : start + rows, :]


def sum_kernel(sizes, *refs):
    holders, columns = sizes.holders, sizes.columns
    inputs = sizes.owners // 2 + 1
    arrived, outs = refs[:inputs], refs[inputs:]
    day_start = sizes.slot_starts[2]
    totals = [0.0, 0.0, 0.0]
    messages = [ref.at[: sizes.slot_rows] for ref in arrived]
    messages += [ref.at[sizes.slot_rows :] for ref in arrived[2:]]
    for ref in messages:
        notes = ref[day_start : day_start + sizes.slots[2], :].astype(f32)
        rows = notes[sizes.note_row : sizes.note_row + 1, : sizes.slot_rows].astype(jnp.int32)
        for t in range(3):
            start, slots = sizes.slot_starts[t], sizes.slots[t]
            shape = (sizes.row_counts[t], sizes.slot_rows)
            slot = iota(shape, 1)
            mine = (slot >= start) & (slot < start + slots)
            selector = onehot((iota(shape, 0) == rows) & mine)
            totals[t] = totals[t] + jnp.dot(selector, ref[...], preferred_element_type=f32)
    for t in range(3):
        if t < 2:
            turned = totals[t].T.astype(bf16)
            for j in range(holders):
                outs[j][t * columns : (t + 1) * columns, :] = turned[
                    j * columns : (j + 1) * columns
                ]
        else:
            for j in range(holders):
                outs[j][2 * columns :, :] = pack_days(
                    sizes, totals[t][:, j * columns : (j + 1) * columns]
                ).astype(bf16)


def adam_kernel(sizes, *refs):
    holders, columns = sizes.holders, sizes.columns
    pieces = refs[:holders]
    states = refs[holders : holders + 9]
    outs = refs[holders + 9 :]
    total = pieces[0][...].astype(f32)
    for ref in pieces[1:]:
        total = total + ref[...].astype(f32)
    for t in range(3):
        if t < 2:
            gradient = total[t * columns : (t + 1) * columns]
        else:
            gradient = unpack_days(sizes, total[2 * columns :])
        factor, first, second = states[3 * t : 3 * t + 3]
        new_factor, new_first, new_second = outs[3 * t : 3 * t + 3]
        first_value = beta_one * first[...] + (1.0 - beta_one) * gradient
        second_value = beta_two * second[...] + (1.0 - beta_two) * gradient * gradient
        change = (
            learn_rate
            * (first_value / bias_one)
            / (jnp.sqrt(second_value / bias_two) + epsilon)
        )
        new_factor[...] = factor[...] - change
        new_first[...] = first_value
        new_second[...] = second_value


def swap(array, axis, size, bits):
    return lax.ppermute(array, axis, [(i, i ^ bits) for i in range(size)])


def local(
    users_list,
    items_list,
    days_list,
    status,
    user_factor,
    user_first,
    user_second,
    item_factor,
    item_first,
    item_second,
    day_factor,
    day_first,
    day_second,
):
    owners = lax.axis_size("dp")
    holders = lax.axis_size("mp")
    row_counts = (user_factor.shape[0], item_factor.shape[0], day_factor.shape[0])
    list_counts = (users_list.shape[1], items_list.shape[1], days_list.shape[1])
    sizes = Sizes(owners, holders, user_factor.shape[1], row_counts, list_counts)
    shape = jax.ShapeDtypeStruct
    small = pltpu.CompilerParams(vmem_limit_bytes=SMALL_VMEM)

    hbm = pl.BlockSpec(memory_space=pltpu.HBM)
    in_hbm = lambda a: pltpu.with_memory_space_constraint(a, pltpu.HBM)
    tables_in = (user_factor.T, item_factor.T, day_factor)
    piece = pl.pallas_call(
        functools.partial(pack_kernel, sizes),
        out_shape=shape((sizes.piece_rows, LANES), bf16),
        in_specs=[hbm] * 3,
        scratch_shapes=[pltpu.VMEM(a.shape, f32) for a in tables_in]
        + [pltpu.SemaphoreType.DMA((3,))],
        compiler_params=small,
        name="pack",
    )(*[in_hbm(a) for a in tables_in])
    distances = exchange_order(holders)
    pieces = [swap(piece, "mp", holders, bits) for bits in distances] + [piece]

    table = pl.pallas_call(
        functools.partial(table_kernel, sizes),
        out_shape=shape((sizes.table_rows, LANES), bf16),
        compiler_params=small,
        name="table",
    )(*pieces)
    arrived = {bits: swap(table, "dp", owners, bits) for bits in range(2, owners, 2)}
    own_crossed = swap(table, "dp", owners, 1)
    picks_places_notes = pl.pallas_call(
        functools.partial(slot_kernel, sizes),
        out_shape=tuple(
            [shape((owners * row_counts[t], list_counts[t]), bf16) for t in range(3)]
            + [shape((owners * sizes.slots[t], list_counts[t]), bf16) for t in range(3)]
            + [shape((owners, sizes.rank), f32), shape(status.shape[1:], jnp.int32)]
        ),
        in_specs=[pl.BlockSpec(memory_space=pltpu.SMEM)]
        + [hbm] * 3
        + [pl.BlockSpec(memory_space=pl.ANY), hbm],
        scratch_shapes=[pltpu.VMEM((1, count), jnp.int32) for count in list_counts]
        + [pltpu.SemaphoreType.DMA((3,)), pltpu.SemaphoreType.DMA((1,))],
        compiler_params=small,
        name="slots",
    )(
        lax.axis_index("dp").astype(jnp.int32).reshape(1),
        *[in_hbm(a) for a in (users_list, items_list, days_list)],
        table,
        in_hbm(status),
    )

    arrived[HOLD] = pl.pallas_call(
        hold_kernel,
        out_shape=shape(table.shape, bf16),
        compiler_params=small,
        name="hold",
    )(arrived[HOLD], picks_places_notes[6])
    tables = [table, own_crossed]
    for bits in range(2, owners, 2):
        tables += [arrived[bits], swap(arrived[bits], "dp", owners, 1)]
    inputs = [*tables, *picks_places_notes]
    users, items, days = list_counts
    half = shape((owners // 2 * sizes.slot_rows, sizes.rank), bf16)
    own, other = pl.pallas_call(
        functools.partial(block_kernel, sizes),
        out_shape=(half, half),
        in_specs=[pl.BlockSpec(memory_space=pltpu.VMEM)] * len(inputs),
        scratch_shapes=[
            pltpu.VMEM((users, sizes.rank), f32),
            pltpu.VMEM((users, sizes.rank), bf16),
            pltpu.VMEM((items, sizes.rank), bf16),
            pltpu.VMEM((sizes.rank, items), bf16),
            pltpu.VMEM((days, sizes.rank), f32),
            pltpu.VMEM((users, sizes.rank), f32),
            pltpu.VMEM((items, sizes.rank), f32),
            pltpu.VMEM((days, sizes.rank), f32),
            pltpu.VMEM((4 * users, sizes.rank), bf16),
            pltpu.VMEM((4 * users, sizes.rank), bf16),
            pltpu.VMEM((4 * users, items), bf16),
            pltpu.VMEM((4 * users, items), bf16),
        ],
        compiler_params=pltpu.CompilerParams(vmem_limit_bytes=BLOCK_VMEM),
        name="block_gradients",
    )(*inputs)
    crossed = swap(other, "dp", owners, 1)
    message = shape((2 * sizes.slot_rows, sizes.rank), bf16)
    merged = pl.pallas_call(
        functools.partial(merge_kernel, sizes),
        out_shape=tuple([message] * (owners // 2 - 1)),
        compiler_params=small,
        name="merge",
    )(own, crossed)
    returned = [own, crossed]
    returned += [
        swap(merged[bits // 2 - 1], "dp", owners, bits) for bits in range(owners - 2, 0, -2)
    ]

    totals = pl.pallas_call(
        functools.partial(sum_kernel, sizes),
        out_shape=tuple([shape(piece.shape, bf16)] * holders),
        compiler_params=small,
        name="row_sums",
    )(*returned)
    column_totals = [totals[0]] + [
        swap(totals[bits], "mp", holders, bits) for bits in range(holders - 1, 0, -1)
    ]

    states = (
        user_factor.T,
        user_first.T,
        user_second.T,
        item_factor.T,
        item_first.T,
        item_second.T,
        day_factor,
        day_first,
        day_second,
    )
    updated = pl.pallas_call(
        functools.partial(adam_kernel, sizes),
        out_shape=tuple(shape(a.shape, a.dtype) for a in states),
        compiler_params=small,
        name="adam",
    )(*column_totals, *states)
    return tuple(a.T for a in updated[:6]) + tuple(updated[6:])


def solution(mesh):
    block = P(("dp", "mp"), None)
    piece = P("dp", "mp")
    return jax.shard_map(
        local,
        mesh=mesh,
        in_specs=(block, block, block, P(("dp", "mp"), None, None, None)) + (piece,) * 9,
        out_specs=(piece,) * 9,
        check_vma=False,
    )
```

```python
import functools

import jax
import jax.numpy as jnp
from jax import lax
from jax.experimental import pallas as pl
from jax.experimental.pallas import tpu as pltpu
from jax.sharding import PartitionSpec as P

beta_one = 0.9
beta_two = 0.99
bias_one = 1.0 - 0.9**10
bias_two = 1.0 - 0.99**10
learn_rate = 0.01
epsilon = 1e-08
loss_scale = 0.0625

LANES = 128
HOLD = 2
SMALL_VMEM = 16 * 1024 * 1024
BLOCK_VMEM = 24 * 1024 * 1024

f32 = jnp.float32
bf16 = jnp.bfloat16


class Sizes:
    def __init__(self, owners, holders, columns, row_counts, list_counts):
        self.owners = owners
        self.holders = holders
        self.columns = columns
        self.rank = columns * holders
        self.row_counts = row_counts
        self.list_counts = list_counts
        limits = (
            max(2, 3 * list_counts[0] // (2 * owners)),
            max(2, 3 * list_counts[1] // (2 * owners)),
            max(2, 2 * list_counts[2] // owners),
        )
        self.slots = tuple(-(-(limit + t // 2) // 16) * 16 for t, limit in enumerate(limits))
        self.note_row = limits[2]
        self.slot_starts = (0, self.slots[0], self.slots[0] + self.slots[1])
        self.slot_rows = sum(self.slots)
        self.day_parts = LANES // columns
        self.day_packed = -(-(row_counts[2] // self.day_parts) // 16) * 16
        self.piece_rows = 2 * columns + self.day_packed
        self.day_chunks = self.rank // LANES
        self.table_rows = 2 * self.rank + self.day_chunks * row_counts[2]


def iota(shape, dimension):
    return lax.broadcasted_iota(jnp.int32, shape, dimension)


def onehot(condition):
    return jnp.where(condition, 1.0, 0.0).astype(bf16)


def dot_nt(a, b):
    return lax.dot_general(a, b, (((1,), (1,)), ((), ())), preferred_element_type=f32)


def pack_days(sizes, days):
    rows = sizes.row_counts[2] // sizes.day_parts
    parts = [days[p * rows : (p + 1) * rows] for p in range(sizes.day_parts)]
    if rows != sizes.day_packed:
        blank = jnp.zeros((sizes.day_packed - rows, days.shape[1]), days.dtype)
        parts = [jnp.concatenate([part, blank], axis=0) for part in parts]
    return jnp.concatenate(parts, axis=1)


def unpack_days(sizes, packed):
    rows = sizes.row_counts[2] // sizes.day_parts
    return jnp.concatenate(
        [
            packed[:rows, p * sizes.columns : (p + 1) * sizes.columns]
            for p in range(sizes.day_parts)
        ],
        axis=0,
    )


def fetch(sources, targets, semaphores):
    copies = [
        pltpu.make_async_copy(source, target, semaphores.at[n])
        for n, (source, target) in enumerate(zip(sources, targets))
    ]
    for copy in copies:
        copy.start()
    for copy in copies:
        copy.wait()


def pack_kernel(sizes, user_hbm, item_hbm, day_hbm, out_ref, user, item, day, semaphores):
    columns = sizes.columns
    fetch((user_hbm, item_hbm, day_hbm), (user, item, day), semaphores)
    out_ref[:columns, :] = user[...].astype(bf16)
    out_ref[columns : 2 * columns, :] = item[...].astype(bf16)
    out_ref[2 * columns :, :] = pack_days(sizes, day[...]).astype(bf16)


def exchange_order(size):
    order = list(range(1, size))
    return [1] + order[:0:-1]


def slot_kernel(sizes, me_ref, *refs):
    owners = sizes.owners
    picks, places, note_ref, status_ref = refs[5:8], refs[8:11], refs[11], refs[12]
    lists, semaphores, status_semaphore = refs[13:16], refs[16], refs[17]
    status_copy = pltpu.make_async_copy(refs[4].at[0], status_ref, status_semaphore.at[0])
    fetch(refs[:3], lists, semaphores)
    status_copy.start()
    me = me_ref[0]
    notes = [[] for _ in range(owners)]
    for t in range(3):
        count, rows, slots = sizes.list_counts[t], sizes.row_counts[t], sizes.slots[t]
        number = lists[t][...]
        owner = number // rows
        row = number % rows
        partner = lax.bitwise_xor(owner, jnp.full_like(owner, me))
        picks[t][...] = onehot(iota((owners * rows, count), 0) == partner * rows + row)
        earlier = onehot(iota((count, count), 0) < iota((count, count), 1))
        owner_hot = iota((owners, count), 0) == owner
        before = jnp.dot(onehot(owner_hot), earlier, preferred_element_type=f32)
        position = jnp.sum(jnp.where(owner_hot, before, 0.0), axis=0, keepdims=True)
        target = partner * slots + position.astype(jnp.int32)
        place = onehot(iota((owners * slots, count), 0) == target)
        places[t][...] = place
        following = (row + 1).astype(bf16)
        for s in range(owners):
            notes[s].append(dot_nt(following, place[s * slots : (s + 1) * slots]) - 1.0)
    blank = jnp.full((1, sizes.rank - sizes.slot_rows), -1.0, f32)
    note_ref[...] = jnp.concatenate(
        [jnp.concatenate(note + [blank], axis=1) for note in notes], axis=0
    )
    status_copy.wait()


def table_kernel(sizes, *refs):
    order = exchange_order(sizes.holders) + [0]
    pieces, out_ref = [refs[order.index(j)] for j in range(sizes.holders)], refs[-1]
    columns, rank, day_rows = sizes.columns, sizes.rank, sizes.row_counts[2]
    for j, ref in enumerate(pieces):
        for t in range(2):
            out_ref[t * rank + j * columns : t * rank + (j + 1) * columns, :] = ref[
                t * columns : (t + 1) * columns, :
            ]
    days = jnp.concatenate(
        [unpack_days(sizes, ref[2 * columns :, :].astype(f32)) for ref in pieces], axis=1
    ).astype(bf16)
    for chunk in range(sizes.day_chunks):
        start = 2 * rank + chunk * day_rows
        out_ref[start : start + day_rows, :] = days[:, chunk * LANES : (chunk + 1) * LANES]


def block_kernel(sizes, *refs):
    owners, rank, day_rows = sizes.owners, sizes.rank, sizes.row_counts[2]
    tables, refs = refs[:owners], refs[owners:]
    picks, places = refs[:3], refs[3:6]
    note_ref, status, own_ref, other_ref = refs[6:10]
    (
        users,
        users_low,
        items,
        items_half_t,
        days,
        user_gradient,
        item_gradient,
        day_gradient,
        scaled_even,
        scaled_odd,
        residual_even,
        residual_odd,
    ) = refs[10:]
    pair = 8
    pairs = status.shape[0] // pair

    def pick(t):
        table = jnp.concatenate([ref[t * rank : (t + 1) * rank, :] for ref in tables], axis=1)
        return jnp.dot(table, picks[t][...], preferred_element_type=f32)

    user_values = pick(0).T
    users[...] = user_values
    users_low[...] = user_values.astype(bf16)
    items_t = pick(1)
    items[...] = items_t.T.astype(bf16)
    items_half_t[...] = (0.5 * items_t).astype(bf16)
    starts = [2 * rank + chunk * day_rows for chunk in range(sizes.day_chunks)]
    day_table = jnp.concatenate(
        [
            jnp.concatenate([ref[start : start + day_rows, :] for start in starts], axis=1)
            for ref in tables
        ],
        axis=0,
    )
    days[...] = lax.dot_general(
        picks[2][...], day_table, (((0,), (0,)), ((), ())), preferred_element_type=f32
    )
    user_gradient[...] = jnp.zeros_like(user_gradient)
    item_gradient[...] = jnp.zeros_like(item_gradient)
    count = users.shape[0]

    def residuals(first, scaled, residual):
        for j in range(pair):
            day = days[pl.ds(first + j, 1), :].astype(bf16)
            scaled[j * count : (j + 1) * count, :] = day * users_low[...]
        half_logits = jnp.dot(scaled[...], items_half_t[...], preferred_element_type=f32)
        for j in range(pair):
            rows = slice(j * count, (j + 1) * count)
            state = status[first + j]
            residual[rows, :] = (
                state.astype(f32)
                * (jnp.tanh(half_logits[rows]) + jnp.where(state == 1, -1.0, 1.0))
            ).astype(bf16)

    def gradients(first, scaled, residual):
        projected = jnp.dot(residual[...], items[...], preferred_element_type=f32)
        total = 0.0
        for j in range(pair):
            part = projected[j * count : (j + 1) * count]
            day = days[pl.ds(first + j, 1), :]
            total = total + part * day
            day_gradient[pl.ds(first + j, 1), :] = jnp.sum(
                part * users[...], axis=0, keepdims=True
            )
        user_gradient[...] += total
        item_gradient[...] += lax.dot_general(
            residual[...], scaled[...], (((0,), (0,)), ((), ())), preferred_element_type=f32
        )

    even, odd = (scaled_even, residual_even), (scaled_odd, residual_odd)
    residuals(0, *even)

    for n in range(pairs // 2 - 1):
        first = 2 * n * pair
        residuals(first + pair, *odd)
        gradients(first, *even)
        residuals(first + 2 * pair, *even)
        gradients(first + pair, *odd)

    last = (pairs - 1) * pair
    residuals(last, *odd)
    gradients(last - pair, *even)
    gradients(last, *odd)

    for t, gradient in enumerate((user_gradient, item_gradient, day_gradient)):
        start, slots = sizes.slot_starts[t], sizes.slots[t]
        values = (0.5 * loss_scale * gradient[...]).astype(bf16)
        placed = jnp.dot(places[t][...], values, preferred_element_type=f32)
        for s in range(owners):
            rows = placed[s * slots : (s + 1) * slots]
            if t == 2:
                note = iota(rows.shape, 0) == sizes.note_row
                rows = jnp.where(note, note_ref[s : s + 1, :], rows)
            out = (own_ref, other_ref)[s % 2]
            first = (s // 2) * sizes.slot_rows + start
            out[first : first + slots, :] = rows.astype(bf16)


def hold_kernel(arrived_ref, note_ref, out_ref):
    out_ref[...] = arrived_ref[...]


def merge_kernel(sizes, own_ref, crossed_ref, *outs):
    rows = sizes.slot_rows
    for n, out in enumerate(outs):
        start = (n + 1) * rows
        out[:rows, :] = own_ref[start : start + rows, :]
        out[rows:, :] = crossed_ref[start : start + rows, :]


def add_messages(sizes, totals, messages):
    day_start = sizes.slot_starts[2]
    for ref in messages:
        notes = ref[day_start : day_start + sizes.slots[2], :].astype(f32)
        rows = notes[sizes.note_row : sizes.note_row + 1, : sizes.slot_rows].astype(jnp.int32)
        for t in range(3):
            start, slots = sizes.slot_starts[t], sizes.slots[t]
            shape = (sizes.row_counts[t], sizes.slot_rows)
            slot = iota(shape, 1)
            mine = (slot >= start) & (slot < start + slots)
            selector = onehot((iota(shape, 0) == rows) & mine)
            totals[t] = totals[t] + jnp.dot(selector, ref[...], preferred_element_type=f32)
    return totals


def early_sum_kernel(sizes, own_ref, crossed_ref, arrived_ref, *outs):
    rows = sizes.slot_rows
    messages = [own_ref.at[:rows], crossed_ref.at[:rows]]
    messages += [arrived_ref.at[:rows], arrived_ref.at[rows:]]
    for out, total in zip(outs, add_messages(sizes, [0.0, 0.0, 0.0], messages)):
        out[...] = total


def sum_kernel(sizes, *refs):
    holders, columns, rows = sizes.holders, sizes.columns, sizes.slot_rows
    early, arrived, outs = refs[:3], refs[3:-holders], refs[-holders:]
    messages = [ref.at[:rows] for ref in arrived] + [ref.at[rows:] for ref in arrived]
    totals = add_messages(sizes, [ref[...] for ref in early], messages)
    for t in range(3):
        if t < 2:
            turned = totals[t].T.astype(bf16)
            for j in range(holders):
                outs[j][t * columns : (t + 1) * columns, :] = turned[
                    j * columns : (j + 1) * columns
                ]
        else:
            for j in range(holders):
                outs[j][2 * columns :, :] = pack_days(
                    sizes, totals[t][:, j * columns : (j + 1) * columns]
                ).astype(bf16)


def adam_kernel(sizes, *refs):
    holders, columns = sizes.holders, sizes.columns
    pieces = refs[:holders]
    states = refs[holders : holders + 9]
    outs = refs[holders + 9 :]
    total = pieces[0][...].astype(f32)
    for ref in pieces[1:]:
        total = total + ref[...].astype(f32)
    for t in range(3):
        if t < 2:
            gradient = total[t * columns : (t + 1) * columns]
        else:
            gradient = unpack_days(sizes, total[2 * columns :])
        factor, first, second = states[3 * t : 3 * t + 3]
        new_factor, new_first, new_second = outs[3 * t : 3 * t + 3]
        first_value = beta_one * first[...] + (1.0 - beta_one) * gradient
        second_value = beta_two * second[...] + (1.0 - beta_two) * gradient * gradient
        change = (
            learn_rate
            * (first_value / bias_one)
            / (jnp.sqrt(second_value / bias_two) + epsilon)
        )
        new_factor[...] = factor[...] - change
        new_first[...] = first_value
        new_second[...] = second_value


def swap(array, axis, size, bits):
    return lax.ppermute(array, axis, [(i, i ^ bits) for i in range(size)])


def local(
    users_list,
    items_list,
    days_list,
    status,
    user_factor,
    user_first,
    user_second,
    item_factor,
    item_first,
    item_second,
    day_factor,
    day_first,
    day_second,
):
    owners = lax.axis_size("dp")
    holders = lax.axis_size("mp")
    row_counts = (user_factor.shape[0], item_factor.shape[0], day_factor.shape[0])
    list_counts = (users_list.shape[1], items_list.shape[1], days_list.shape[1])
    sizes = Sizes(owners, holders, user_factor.shape[1], row_counts, list_counts)
    shape = jax.ShapeDtypeStruct
    small = pltpu.CompilerParams(vmem_limit_bytes=SMALL_VMEM)

    hbm = pl.BlockSpec(memory_space=pltpu.HBM)
    in_hbm = lambda a: pltpu.with_memory_space_constraint(a, pltpu.HBM)
    tables_in = (user_factor.T, item_factor.T, day_factor)
    piece = pl.pallas_call(
        functools.partial(pack_kernel, sizes),
        out_shape=shape((sizes.piece_rows, LANES), bf16),
        in_specs=[hbm] * 3,
        scratch_shapes=[pltpu.VMEM(a.shape, f32) for a in tables_in]
        + [pltpu.SemaphoreType.DMA((3,))],
        compiler_params=small,
        name="pack",
    )(*[in_hbm(a) for a in tables_in])
    distances = exchange_order(holders)
    pieces = [swap(piece, "mp", holders, bits) for bits in distances] + [piece]

    table = pl.pallas_call(
        functools.partial(table_kernel, sizes),
        out_shape=shape((sizes.table_rows, LANES), bf16),
        compiler_params=small,
        name="table",
    )(*pieces)
    arrived = {bits: swap(table, "dp", owners, bits) for bits in range(2, owners, 2)}
    own_crossed = swap(table, "dp", owners, 1)
    picks_places_notes = pl.pallas_call(
        functools.partial(slot_kernel, sizes),
        out_shape=tuple(
            [shape((owners * row_counts[t], list_counts[t]), bf16) for t in range(3)]
            + [shape((owners * sizes.slots[t], list_counts[t]), bf16) for t in range(3)]
            + [shape((owners, sizes.rank), f32), shape(status.shape[1:], jnp.int32)]
        ),
        in_specs=[pl.BlockSpec(memory_space=pltpu.SMEM)]
        + [hbm] * 3
        + [pl.BlockSpec(memory_space=pl.ANY), hbm],
        scratch_shapes=[pltpu.VMEM((1, count), jnp.int32) for count in list_counts]
        + [pltpu.SemaphoreType.DMA((3,)), pltpu.SemaphoreType.DMA((1,))],
        compiler_params=small,
        name="slots",
    )(
        lax.axis_index("dp").astype(jnp.int32).reshape(1),
        *[in_hbm(a) for a in (users_list, items_list, days_list)],
        table,
        in_hbm(status),
    )

    arrived[HOLD] = pl.pallas_call(
        hold_kernel,
        out_shape=shape(table.shape, bf16),
        compiler_params=small,
        name="hold",
    )(arrived[HOLD], picks_places_notes[6])
    tables = [table, own_crossed]
    for bits in range(2, owners, 2):
        tables += [arrived[bits], swap(arrived[bits], "dp", owners, 1)]
    inputs = [*tables, *picks_places_notes]
    users, items, days = list_counts
    half = shape((owners // 2 * sizes.slot_rows, sizes.rank), bf16)
    own, other = pl.pallas_call(
        functools.partial(block_kernel, sizes),
        out_shape=(half, half),
        in_specs=[pl.BlockSpec(memory_space=pltpu.VMEM)] * len(inputs),
        scratch_shapes=[
            pltpu.VMEM((users, sizes.rank), f32),
            pltpu.VMEM((users, sizes.rank), bf16),
            pltpu.VMEM((items, sizes.rank), bf16),
            pltpu.VMEM((sizes.rank, items), bf16),
            pltpu.VMEM((days, sizes.rank), f32),
            pltpu.VMEM((users, sizes.rank), f32),
            pltpu.VMEM((items, sizes.rank), f32),
            pltpu.VMEM((days, sizes.rank), f32),
            pltpu.VMEM((8 * users, sizes.rank), bf16),
            pltpu.VMEM((8 * users, sizes.rank), bf16),
            pltpu.VMEM((8 * users, items), bf16),
            pltpu.VMEM((8 * users, items), bf16),
        ],
        compiler_params=pltpu.CompilerParams(vmem_limit_bytes=BLOCK_VMEM),
        name="block_gradients",
    )(*inputs)
    crossed = swap(other, "dp", owners, 1)
    message = shape((2 * sizes.slot_rows, sizes.rank), bf16)
    merged = pl.pallas_call(
        functools.partial(merge_kernel, sizes),
        out_shape=tuple([message] * (owners // 2 - 1)),
        compiler_params=small,
        name="merge",
    )(own, crossed)
    returned = [own, crossed]
    returned += [
        swap(merged[bits // 2 - 1], "dp", owners, bits) for bits in range(owners - 2, 0, -2)
    ]

    early = pl.pallas_call(
        functools.partial(early_sum_kernel, sizes),
        out_shape=tuple(shape((rows, sizes.rank), f32) for rows in row_counts),
        compiler_params=small,
        name="early_sums",
    )(*returned[:3])
    totals = pl.pallas_call(
        functools.partial(sum_kernel, sizes),
        out_shape=tuple([shape(piece.shape, bf16)] * holders),
        compiler_params=small,
        name="row_sums",
    )(*early, *returned[3:])
    column_totals = [totals[0]] + [
        swap(totals[bits], "mp", holders, bits) for bits in range(holders - 1, 0, -1)
    ]

    states = (
        user_factor.T,
        user_first.T,
        user_second.T,
        item_factor.T,
        item_first.T,
        item_second.T,
        day_factor,
        day_first,
        day_second,
    )
    updated = pl.pallas_call(
        functools.partial(adam_kernel, sizes),
        out_shape=tuple(shape(a.shape, a.dtype) for a in states),
        compiler_params=small,
        name="adam",
    )(*column_totals, *states)
    return tuple(a.T for a in updated[:6]) + tuple(updated[6:])


def solution(mesh):
    block = P(("dp", "mp"), None)
    piece = P("dp", "mp")
    return jax.shard_map(
        local,
        mesh=mesh,
        in_specs=(block, block, block, P(("dp", "mp"), None, None, None)) + (piece,) * 9,
        out_specs=(piece,) * 9,
        check_vma=False,
    )
```

```python
import functools

import jax
import jax.numpy as jnp
from jax import lax
from jax.experimental import pallas as pl
from jax.experimental.pallas import tpu as pltpu
from jax.sharding import PartitionSpec as P

beta_one = 0.9
beta_two = 0.99
bias_one = 1.0 - 0.9**10
bias_two = 1.0 - 0.99**10
learn_rate = 0.01
epsilon = 1e-08
loss_scale = 0.0625

LANES = 128
HOLD = 2
SMALL_VMEM = 16 * 1024 * 1024
BLOCK_VMEM = 24 * 1024 * 1024

f32 = jnp.float32
bf16 = jnp.bfloat16


class Sizes:
    def __init__(self, owners, holders, columns, row_counts, list_counts):
        self.owners = owners
        self.holders = holders
        self.columns = columns
        self.rank = columns * holders
        self.row_counts = row_counts
        self.list_counts = list_counts
        limits = (
            max(2, 3 * list_counts[0] // (2 * owners)),
            max(2, 3 * list_counts[1] // (2 * owners)),
            max(2, 2 * list_counts[2] // owners),
        )
        self.slots = tuple(-(-(limit + t // 2) // 16) * 16 for t, limit in enumerate(limits))
        self.note_row = limits[2]
        self.slot_starts = (0, self.slots[0], self.slots[0] + self.slots[1])
        self.slot_rows = sum(self.slots)
        self.day_parts = LANES // columns
        self.day_packed = -(-(row_counts[2] // self.day_parts) // 16) * 16
        self.piece_rows = 2 * columns + self.day_packed
        self.day_chunks = self.rank // LANES
        self.table_rows = 2 * self.rank + self.day_chunks * row_counts[2]


def iota(shape, dimension):
    return lax.broadcasted_iota(jnp.int32, shape, dimension)


def onehot(condition):
    return jnp.where(condition, 1.0, 0.0).astype(bf16)


def dot_nt(a, b):
    return lax.dot_general(a, b, (((1,), (1,)), ((), ())), preferred_element_type=f32)


def pack_days(sizes, days):
    rows = sizes.row_counts[2] // sizes.day_parts
    parts = [days[p * rows : (p + 1) * rows] for p in range(sizes.day_parts)]
    if rows != sizes.day_packed:
        blank = jnp.zeros((sizes.day_packed - rows, days.shape[1]), days.dtype)
        parts = [jnp.concatenate([part, blank], axis=0) for part in parts]
    return jnp.concatenate(parts, axis=1)


def unpack_days(sizes, packed):
    rows = sizes.row_counts[2] // sizes.day_parts
    return jnp.concatenate(
        [
            packed[:rows, p * sizes.columns : (p + 1) * sizes.columns]
            for p in range(sizes.day_parts)
        ],
        axis=0,
    )


def fetch(sources, targets, semaphores):
    copies = [
        pltpu.make_async_copy(source, target, semaphores.at[n])
        for n, (source, target) in enumerate(zip(sources, targets))
    ]
    for copy in copies:
        copy.start()
    for copy in copies:
        copy.wait()


def pack_kernel(sizes, user_hbm, item_hbm, day_hbm, out_ref, user, item, day, semaphores):
    columns = sizes.columns
    fetch((user_hbm, item_hbm, day_hbm), (user, item, day), semaphores)
    out_ref[:columns, :] = user[...].astype(bf16)
    out_ref[columns : 2 * columns, :] = item[...].astype(bf16)
    out_ref[2 * columns :, :] = pack_days(sizes, day[...]).astype(bf16)


def exchange_order(size):
    order = list(range(1, size))
    return [1] + order[:0:-1]


def slot_kernel(sizes, me_ref, *refs):
    owners = sizes.owners
    picks, places, note_ref, status_ref = refs[5:8], refs[8:11], refs[11], refs[12]
    lists, semaphores, status_semaphore = refs[13:16], refs[16], refs[17]
    status_copy = pltpu.make_async_copy(refs[4].at[0], status_ref, status_semaphore.at[0])
    fetch(refs[:3], lists, semaphores)
    status_copy.start()
    me = me_ref[0]
    notes = [[] for _ in range(owners)]
    for t in range(3):
        count, rows, slots = sizes.list_counts[t], sizes.row_counts[t], sizes.slots[t]
        number = lists[t][...]
        owner = number // rows
        row = number % rows
        partner = lax.bitwise_xor(owner, jnp.full_like(owner, me))
        picks[t][...] = onehot(iota((owners * rows, count), 0) == partner * rows + row)
        earlier = onehot(iota((count, count), 0) < iota((count, count), 1))
        owner_hot = iota((owners, count), 0) == owner
        before = jnp.dot(onehot(owner_hot), earlier, preferred_element_type=f32)
        position = jnp.sum(jnp.where(owner_hot, before, 0.0), axis=0, keepdims=True)
        target = partner * slots + position.astype(jnp.int32)
        place = onehot(iota((owners * slots, count), 0) == target)
        places[t][...] = place
        following = (row + 1).astype(bf16)
        for s in range(owners):
            notes[s].append(dot_nt(following, place[s * slots : (s + 1) * slots]) - 1.0)
    blank = jnp.full((1, sizes.rank - sizes.slot_rows), -1.0, f32)
    note_ref[...] = jnp.concatenate(
        [jnp.concatenate(note + [blank], axis=1) for note in notes], axis=0
    )
    status_copy.wait()


def table_kernel(sizes, *refs):
    order = exchange_order(sizes.holders) + [0]
    pieces, out_ref = [refs[order.index(j)] for j in range(sizes.holders)], refs[-1]
    columns, rank, day_rows = sizes.columns, sizes.rank, sizes.row_counts[2]
    for j, ref in enumerate(pieces):
        for t in range(2):
            out_ref[t * rank + j * columns : t * rank + (j + 1) * columns, :] = ref[
                t * columns : (t + 1) * columns, :
            ]
    days = jnp.concatenate(
        [unpack_days(sizes, ref[2 * columns :, :].astype(f32)) for ref in pieces], axis=1
    ).astype(bf16)
    for chunk in range(sizes.day_chunks):
        start = 2 * rank + chunk * day_rows
        out_ref[start : start + day_rows, :] = days[:, chunk * LANES : (chunk + 1) * LANES]


def table_order(owners):
    return [0, 2] + list(range(owners - 2, 2, -2))


def block_kernel(sizes, *refs):
    owners, rank, day_rows = sizes.owners, sizes.rank, sizes.row_counts[2]
    order = table_order(owners)
    tables = [refs[2 * order.index(n - n % 2) + n % 2] for n in range(owners)]
    refs = refs[owners:]
    picks, places = refs[:3], refs[3:6]
    note_ref, status, own_ref, other_ref = refs[6:10]
    (
        users,
        users_low,
        items,
        items_half_t,
        days,
        user_gradient,
        item_gradient,
        day_gradient,
        scaled_even,
        scaled_odd,
        residual_even,
        residual_odd,
    ) = refs[10:]
    pair = 2
    pairs = status.shape[0] // pair

    def pick(t):
        table = jnp.concatenate([ref[t * rank : (t + 1) * rank, :] for ref in tables], axis=1)
        return jnp.dot(table, picks[t][...], preferred_element_type=f32)

    user_values = pick(0).T
    users[...] = user_values
    users_low[...] = user_values.astype(bf16)
    items_t = pick(1)
    items[...] = items_t.T.astype(bf16)
    items_half_t[...] = (0.5 * items_t).astype(bf16)
    starts = [2 * rank + chunk * day_rows for chunk in range(sizes.day_chunks)]
    day_table = jnp.concatenate(
        [
            jnp.concatenate([ref[start : start + day_rows, :] for start in starts], axis=1)
            for ref in tables
        ],
        axis=0,
    )
    days[...] = lax.dot_general(
        picks[2][...], day_table, (((0,), (0,)), ((), ())), preferred_element_type=f32
    )
    user_gradient[...] = jnp.zeros_like(user_gradient)
    item_gradient[...] = jnp.zeros_like(item_gradient)
    count = users.shape[0]

    def residuals(first, scaled, residual):
        for j in range(pair):
            day = days[pl.ds(first + j, 1), :].astype(bf16)
            scaled[j * count : (j + 1) * count, :] = day * users_low[...]
        half_logits = jnp.dot(scaled[...], items_half_t[...], preferred_element_type=f32)
        for j in range(pair):
            rows = slice(j * count, (j + 1) * count)
            state = status[first + j]
            residual[rows, :] = (
                state.astype(f32)
                * (jnp.tanh(half_logits[rows]) + jnp.where(state == 1, -1.0, 1.0))
            ).astype(bf16)

    def gradients(first, scaled, residual):
        projected = jnp.dot(residual[...], items[...], preferred_element_type=f32)
        total = 0.0
        for j in range(pair):
            part = projected[j * count : (j + 1) * count]
            day = days[pl.ds(first + j, 1), :]
            total = total + part * day
            day_gradient[pl.ds(first + j, 1), :] = jnp.sum(
                part * users[...], axis=0, keepdims=True
            )
        user_gradient[...] += total
        item_gradient[...] += lax.dot_general(
            residual[...], scaled[...], (((0,), (0,)), ((), ())), preferred_element_type=f32
        )

    even, odd = (scaled_even, residual_even), (scaled_odd, residual_odd)
    residuals(0, *even)

    for n in range(pairs // 2 - 1):
        first = 2 * n * pair
        residuals(first + pair, *odd)
        gradients(first, *even)
        residuals(first + 2 * pair, *even)
        gradients(first + pair, *odd)

    last = (pairs - 1) * pair
    residuals(last, *odd)
    gradients(last - pair, *even)
    gradients(last, *odd)

    for t, gradient in enumerate((user_gradient, item_gradient, day_gradient)):
        start, slots = sizes.slot_starts[t], sizes.slots[t]
        values = (0.5 * loss_scale * gradient[...]).astype(bf16)
        placed = jnp.dot(places[t][...], values, preferred_element_type=f32)
        for s in range(owners):
            rows = placed[s * slots : (s + 1) * slots]
            if t == 2:
                note = iota(rows.shape, 0) == sizes.note_row
                rows = jnp.where(note, note_ref[s : s + 1, :], rows)
            out = (own_ref, other_ref)[s % 2]
            first = (s // 2) * sizes.slot_rows + start
            out[first : first + slots, :] = rows.astype(bf16)


def hold_kernel(arrived_ref, note_ref, out_ref):
    out_ref[...] = arrived_ref[...]


def merge_kernel(sizes, own_ref, crossed_ref, *outs):
    rows = sizes.slot_rows
    for n, out in enumerate(outs):
        start = (n + 1) * rows
        out[:rows, :] = own_ref[start : start + rows, :]
        out[rows:, :] = crossed_ref[start : start + rows, :]


def add_messages(sizes, totals, messages):
    day_start = sizes.slot_starts[2]
    for ref in messages:
        notes = ref[day_start : day_start + sizes.slots[2], :].astype(f32)
        rows = notes[sizes.note_row : sizes.note_row + 1, : sizes.slot_rows].astype(jnp.int32)
        for t in range(3):
            start, slots = sizes.slot_starts[t], sizes.slots[t]
            shape = (sizes.row_counts[t], sizes.slot_rows)
            slot = iota(shape, 1)
            mine = (slot >= start) & (slot < start + slots)
            selector = onehot((iota(shape, 0) == rows) & mine)
            totals[t] = totals[t] + jnp.dot(selector, ref[...], preferred_element_type=f32)
    return totals


def early_sum_kernel(sizes, own_ref, crossed_ref, arrived_ref, *outs):
    rows = sizes.slot_rows
    messages = [own_ref.at[:rows], crossed_ref.at[:rows]]
    messages += [arrived_ref.at[:rows], arrived_ref.at[rows:]]
    for out, total in zip(outs, add_messages(sizes, [0.0, 0.0, 0.0], messages)):
        out[...] = total


def sum_kernel(sizes, *refs):
    holders, columns, rows = sizes.holders, sizes.columns, sizes.slot_rows
    early, arrived, outs = refs[:3], refs[3:-holders], refs[-holders:]
    messages = [ref.at[:rows] for ref in arrived] + [ref.at[rows:] for ref in arrived]
    totals = add_messages(sizes, [ref[...] for ref in early], messages)
    for t in range(3):
        if t < 2:
            turned = totals[t].T.astype(bf16)
            for j in range(holders):
                outs[j][t * columns : (t + 1) * columns, :] = turned[
                    j * columns : (j + 1) * columns
                ]
        else:
            for j in range(holders):
                outs[j][2 * columns :, :] = pack_days(
                    sizes, totals[t][:, j * columns : (j + 1) * columns]
                ).astype(bf16)


def adam_kernel(sizes, *refs):
    holders, columns = sizes.holders, sizes.columns
    pieces = refs[:holders]
    states = refs[holders : holders + 9]
    outs = refs[holders + 9 :]
    total = pieces[0][...].astype(f32)
    for ref in pieces[1:]:
        total = total + ref[...].astype(f32)
    for t in range(3):
        if t < 2:
            gradient = total[t * columns : (t + 1) * columns]
        else:
            gradient = unpack_days(sizes, total[2 * columns :])
        factor, first, second = states[3 * t : 3 * t + 3]
        new_factor, new_first, new_second = outs[3 * t : 3 * t + 3]
        first_value = beta_one * first[...] + (1.0 - beta_one) * gradient
        second_value = beta_two * second[...] + (1.0 - beta_two) * gradient * gradient
        change = (
            learn_rate
            * (first_value / bias_one)
            / (jnp.sqrt(second_value / bias_two) + epsilon)
        )
        new_factor[...] = factor[...] - change
        new_first[...] = first_value
        new_second[...] = second_value


def swap(array, axis, size, bits):
    return lax.ppermute(array, axis, [(i, i ^ bits) for i in range(size)])


def local(
    users_list,
    items_list,
    days_list,
    status,
    user_factor,
    user_first,
    user_second,
    item_factor,
    item_first,
    item_second,
    day_factor,
    day_first,
    day_second,
):
    owners = lax.axis_size("dp")
    holders = lax.axis_size("mp")
    row_counts = (user_factor.shape[0], item_factor.shape[0], day_factor.shape[0])
    list_counts = (users_list.shape[1], items_list.shape[1], days_list.shape[1])
    sizes = Sizes(owners, holders, user_factor.shape[1], row_counts, list_counts)
    shape = jax.ShapeDtypeStruct
    small = pltpu.CompilerParams(vmem_limit_bytes=SMALL_VMEM)

    hbm = pl.BlockSpec(memory_space=pltpu.HBM)
    in_hbm = lambda a: pltpu.with_memory_space_constraint(a, pltpu.HBM)
    tables_in = (user_factor.T, item_factor.T, day_factor)
    piece = pl.pallas_call(
        functools.partial(pack_kernel, sizes),
        out_shape=shape((sizes.piece_rows, LANES), bf16),
        in_specs=[hbm] * 3,
        scratch_shapes=[pltpu.VMEM(a.shape, f32) for a in tables_in]
        + [pltpu.SemaphoreType.DMA((3,))],
        compiler_params=small,
        name="pack",
    )(*[in_hbm(a) for a in tables_in])
    distances = exchange_order(holders)
    pieces = [swap(piece, "mp", holders, bits) for bits in distances] + [piece]

    table = pl.pallas_call(
        functools.partial(table_kernel, sizes),
        out_shape=shape((sizes.table_rows, LANES), bf16),
        compiler_params=small,
        name="table",
    )(*pieces)
    arrived = {bits: swap(table, "dp", owners, bits) for bits in range(2, owners, 2)}
    own_crossed = swap(table, "dp", owners, 1)
    picks_places_notes = pl.pallas_call(
        functools.partial(slot_kernel, sizes),
        out_shape=tuple(
            [shape((owners * row_counts[t], list_counts[t]), bf16) for t in range(3)]
            + [shape((owners * sizes.slots[t], list_counts[t]), bf16) for t in range(3)]
            + [shape((owners, sizes.rank), f32), shape(status.shape[1:], jnp.int32)]
        ),
        in_specs=[pl.BlockSpec(memory_space=pltpu.SMEM)]
        + [hbm] * 3
        + [pl.BlockSpec(memory_space=pl.ANY), hbm],
        scratch_shapes=[pltpu.VMEM((1, count), jnp.int32) for count in list_counts]
        + [pltpu.SemaphoreType.DMA((3,)), pltpu.SemaphoreType.DMA((1,))],
        compiler_params=small,
        name="slots",
    )(
        lax.axis_index("dp").astype(jnp.int32).reshape(1),
        *[in_hbm(a) for a in (users_list, items_list, days_list)],
        table,
        in_hbm(status),
    )

    arrived[HOLD] = pl.pallas_call(
        hold_kernel,
        out_shape=shape(table.shape, bf16),
        compiler_params=small,
        name="hold",
    )(arrived[HOLD], picks_places_notes[6])
    tables = [table, own_crossed]
    for bits in table_order(owners)[1:]:
        tables += [arrived[bits], swap(arrived[bits], "dp", owners, 1)]
    inputs = [*tables, *picks_places_notes]
    users, items, days = list_counts
    half = shape((owners // 2 * sizes.slot_rows, sizes.rank), bf16)
    own, other = pl.pallas_call(
        functools.partial(block_kernel, sizes),
        out_shape=(half, half),
        in_specs=[pl.BlockSpec(memory_space=pltpu.VMEM)] * len(inputs),
        scratch_shapes=[
            pltpu.VMEM((users, sizes.rank), f32),
            pltpu.VMEM((users, sizes.rank), bf16),
            pltpu.VMEM((items, sizes.rank), bf16),
            pltpu.VMEM((sizes.rank, items), bf16),
            pltpu.VMEM((days, sizes.rank), f32),
            pltpu.VMEM((users, sizes.rank), f32),
            pltpu.VMEM((items, sizes.rank), f32),
            pltpu.VMEM((days, sizes.rank), f32),
            pltpu.VMEM((2 * users, sizes.rank), bf16),
            pltpu.VMEM((2 * users, sizes.rank), bf16),
            pltpu.VMEM((2 * users, items), bf16),
            pltpu.VMEM((2 * users, items), bf16),
        ],
        compiler_params=pltpu.CompilerParams(vmem_limit_bytes=BLOCK_VMEM),
        name="block_gradients",
    )(*inputs)
    crossed = swap(other, "dp", owners, 1)
    message = shape((2 * sizes.slot_rows, sizes.rank), bf16)
    merged = pl.pallas_call(
        functools.partial(merge_kernel, sizes),
        out_shape=tuple([message] * (owners // 2 - 1)),
        compiler_params=small,
        name="merge",
    )(own, crossed)
    returned = [own, crossed]
    returned += [
        swap(merged[bits // 2 - 1], "dp", owners, bits) for bits in range(owners - 2, 0, -2)
    ]

    early = pl.pallas_call(
        functools.partial(early_sum_kernel, sizes),
        out_shape=tuple(shape((rows, sizes.rank), f32) for rows in row_counts),
        compiler_params=small,
        name="early_sums",
    )(*returned[:3])
    totals = pl.pallas_call(
        functools.partial(sum_kernel, sizes),
        out_shape=tuple([shape(piece.shape, bf16)] * holders),
        compiler_params=small,
        name="row_sums",
    )(*early, *returned[3:])
    column_totals = [totals[0]] + [
        swap(totals[bits], "mp", holders, bits) for bits in range(holders - 1, 0, -1)
    ]

    states = (
        user_factor.T,
        user_first.T,
        user_second.T,
        item_factor.T,
        item_first.T,
        item_second.T,
        day_factor,
        day_first,
        day_second,
    )
    updated = pl.pallas_call(
        functools.partial(adam_kernel, sizes),
        out_shape=tuple(shape(a.shape, a.dtype) for a in states),
        compiler_params=small,
        name="adam",
    )(*column_totals, *states)
    return tuple(a.T for a in updated[:6]) + tuple(updated[6:])


def solution(mesh):
    block = P(("dp", "mp"), None)
    piece = P("dp", "mp")
    return jax.shard_map(
        local,
        mesh=mesh,
        in_specs=(block, block, block, P(("dp", "mp"), None, None, None)) + (piece,) * 9,
        out_specs=(piece,) * 9,
        check_vma=False,
    )
```

```python
import functools

import jax
import jax.numpy as jnp
from jax import lax
from jax.experimental import pallas as pl
from jax.experimental.pallas import tpu as pltpu
from jax.sharding import PartitionSpec as P

beta_one = 0.9
beta_two = 0.99
bias_one = 1.0 - 0.9**10
bias_two = 1.0 - 0.99**10
learn_rate = 0.01
epsilon = 1e-08
loss_scale = 0.0625

LANES = 128
HOLD = 2
SMALL_VMEM = 16 * 1024 * 1024
BLOCK_VMEM = 24 * 1024 * 1024

f32 = jnp.float32
bf16 = jnp.bfloat16


class Sizes:
    def __init__(self, owners, holders, columns, row_counts, list_counts):
        self.owners = owners
        self.holders = holders
        self.columns = columns
        self.rank = columns * holders
        self.row_counts = row_counts
        self.list_counts = list_counts
        limits = (
            max(2, 3 * list_counts[0] // (2 * owners)),
            max(2, 3 * list_counts[1] // (2 * owners)),
            max(2, 2 * list_counts[2] // owners),
        )
        self.slots = tuple(-(-(limit + t // 2) // 16) * 16 for t, limit in enumerate(limits))
        self.note_row = limits[2]
        self.slot_starts = (0, self.slots[0], self.slots[0] + self.slots[1])
        self.slot_rows = sum(self.slots)
        self.day_parts = LANES // columns
        self.day_packed = -(-(row_counts[2] // self.day_parts) // 16) * 16
        self.piece_rows = 2 * columns + self.day_packed
        self.day_chunks = self.rank // LANES
        self.table_rows = 2 * self.rank + self.day_chunks * row_counts[2]


def iota(shape, dimension):
    return lax.broadcasted_iota(jnp.int32, shape, dimension)


def onehot(condition):
    return jnp.where(condition, 1.0, 0.0).astype(bf16)


def dot_nt(a, b):
    return lax.dot_general(a, b, (((1,), (1,)), ((), ())), preferred_element_type=f32)


def pack_days(sizes, days):
    rows = sizes.row_counts[2] // sizes.day_parts
    parts = [days[p * rows : (p + 1) * rows] for p in range(sizes.day_parts)]
    if rows != sizes.day_packed:
        blank = jnp.zeros((sizes.day_packed - rows, days.shape[1]), days.dtype)
        parts = [jnp.concatenate([part, blank], axis=0) for part in parts]
    return jnp.concatenate(parts, axis=1)


def unpack_days(sizes, packed):
    rows = sizes.row_counts[2] // sizes.day_parts
    return jnp.concatenate(
        [
            packed[:rows, p * sizes.columns : (p + 1) * sizes.columns]
            for p in range(sizes.day_parts)
        ],
        axis=0,
    )


def fetch(sources, targets, semaphores):
    copies = [
        pltpu.make_async_copy(source, target, semaphores.at[n])
        for n, (source, target) in enumerate(zip(sources, targets))
    ]
    for copy in copies:
        copy.start()
    for copy in copies:
        copy.wait()


def pack_kernel(sizes, user_hbm, item_hbm, day_hbm, out_ref, user, item, day, semaphores):
    columns = sizes.columns
    fetch((user_hbm, item_hbm, day_hbm), (user, item, day), semaphores)
    out_ref[:columns, :] = user[...].astype(bf16)
    out_ref[columns : 2 * columns, :] = item[...].astype(bf16)
    out_ref[2 * columns :, :] = pack_days(sizes, day[...]).astype(bf16)


def exchange_order(size):
    order = list(range(1, size))
    return [1] + order[:0:-1]


def slot_kernel(sizes, me_ref, *refs):
    owners = sizes.owners
    picks, places, note_ref, status_ref = refs[5:8], refs[8:11], refs[11], refs[12]
    lists, semaphores, status_semaphore = refs[13:16], refs[16], refs[17]
    status_copy = pltpu.make_async_copy(refs[4].at[0], status_ref, status_semaphore.at[0])
    fetch(refs[:3], lists, semaphores)
    status_copy.start()
    me = me_ref[0]
    notes = [[] for _ in range(owners)]
    for t in range(3):
        count, rows, slots = sizes.list_counts[t], sizes.row_counts[t], sizes.slots[t]
        number = lists[t][...]
        owner = number // rows
        row = number % rows
        partner = lax.bitwise_xor(owner, jnp.full_like(owner, me))
        picks[t][...] = onehot(iota((owners * rows, count), 0) == partner * rows + row)
        earlier = onehot(iota((count, count), 0) < iota((count, count), 1))
        owner_hot = iota((owners, count), 0) == owner
        before = jnp.dot(onehot(owner_hot), earlier, preferred_element_type=f32)
        position = jnp.sum(jnp.where(owner_hot, before, 0.0), axis=0, keepdims=True)
        target = partner * slots + position.astype(jnp.int32)
        place = onehot(iota((owners * slots, count), 0) == target)
        places[t][...] = place
        following = (row + 1).astype(bf16)
        for s in range(owners):
            notes[s].append(dot_nt(following, place[s * slots : (s + 1) * slots]) - 1.0)
    blank = jnp.full((1, sizes.rank - sizes.slot_rows), -1.0, f32)
    note_ref[...] = jnp.concatenate(
        [jnp.concatenate(note + [blank], axis=1) for note in notes], axis=0
    )
    status_copy.wait()


def table_kernel(sizes, *refs):
    order = exchange_order(sizes.holders) + [0]
    pieces, out_ref = [refs[order.index(j)] for j in range(sizes.holders)], refs[-1]
    columns, rank, day_rows = sizes.columns, sizes.rank, sizes.row_counts[2]
    for j, ref in enumerate(pieces):
        for t in range(2):
            out_ref[t * rank + j * columns : t * rank + (j + 1) * columns, :] = ref[
                t * columns : (t + 1) * columns, :
            ]
    days = jnp.concatenate(
        [unpack_days(sizes, ref[2 * columns :, :].astype(f32)) for ref in pieces], axis=1
    ).astype(bf16)
    for chunk in range(sizes.day_chunks):
        start = 2 * rank + chunk * day_rows
        out_ref[start : start + day_rows, :] = days[:, chunk * LANES : (chunk + 1) * LANES]


def table_order(owners):
    return [0, 2] + list(range(owners - 2, 2, -2))


def pick_rows(sizes, tables, picks):
    rank, day_rows = sizes.rank, sizes.row_counts[2]
    selectors = []
    for t in range(3):
        rows = sizes.row_counts[t]
        selectors.append(
            jnp.concatenate([picks[t][n * rows : (n + 1) * rows, :] for n in tables], axis=0)
        )
    picked = []
    for t in range(2):
        table = jnp.concatenate(
            [ref[t * rank : (t + 1) * rank, :] for ref in tables.values()], axis=1
        )
        picked.append(jnp.dot(table, selectors[t], preferred_element_type=f32))
    starts = [2 * rank + chunk * day_rows for chunk in range(sizes.day_chunks)]
    day_table = jnp.concatenate(
        [
            jnp.concatenate([ref[start : start + day_rows, :] for start in starts], axis=1)
            for ref in tables.values()
        ],
        axis=0,
    )
    picked.append(
        lax.dot_general(
            selectors[2], day_table, (((0,), (0,)), ((), ())), preferred_element_type=f32
        )
    )
    return picked


def early_pick_kernel(sizes, numbers, *refs):
    tables, picks, outs = refs[: len(numbers)], refs[len(numbers) : -3], refs[-3:]
    for out, rows in zip(outs, pick_rows(sizes, dict(zip(numbers, tables)), picks)):
        out[...] = rows


def block_kernel(sizes, *refs):
    owners = sizes.owners
    table, early, refs = refs[0], refs[1:4], refs[4:]
    picks, places = refs[:3], refs[3:6]
    note_ref, status, own_ref, other_ref = refs[6:10]
    (
        users,
        users_low,
        items,
        items_half_t,
        days,
        user_gradient,
        item_gradient,
        day_gradient,
        scaled_even,
        scaled_odd,
        residual_even,
        residual_odd,
    ) = refs[10:]
    pair = 2
    pairs = status.shape[0] // pair

    last = pick_rows(sizes, {HOLD + 1: table}, picks)
    users_t, items_t, day_values = [ref[...] + rows for ref, rows in zip(early, last)]
    user_values = users_t.T
    users[...] = user_values
    users_low[...] = user_values.astype(bf16)
    items[...] = items_t.T.astype(bf16)
    items_half_t[...] = (0.5 * items_t).astype(bf16)
    days[...] = day_values
    user_gradient[...] = jnp.zeros_like(user_gradient)
    item_gradient[...] = jnp.zeros_like(item_gradient)
    count = users.shape[0]

    def residuals(first, scaled, residual):
        for j in range(pair):
            day = days[pl.ds(first + j, 1), :].astype(bf16)
            scaled[j * count : (j + 1) * count, :] = day * users_low[...]
        half_logits = jnp.dot(scaled[...], items_half_t[...], preferred_element_type=f32)
        for j in range(pair):
            rows = slice(j * count, (j + 1) * count)
            state = status[first + j]
            residual[rows, :] = (
                state.astype(f32)
                * (jnp.tanh(half_logits[rows]) + jnp.where(state == 1, -1.0, 1.0))
            ).astype(bf16)

    def gradients(first, scaled, residual):
        projected = jnp.dot(residual[...], items[...], preferred_element_type=f32)
        total = 0.0
        for j in range(pair):
            part = projected[j * count : (j + 1) * count]
            day = days[pl.ds(first + j, 1), :]
            total = total + part * day
            day_gradient[pl.ds(first + j, 1), :] = jnp.sum(
                part * users[...], axis=0, keepdims=True
            )
        user_gradient[...] += total
        item_gradient[...] += lax.dot_general(
            residual[...], scaled[...], (((0,), (0,)), ((), ())), preferred_element_type=f32
        )

    even, odd = (scaled_even, residual_even), (scaled_odd, residual_odd)
    residuals(0, *even)

    for n in range(pairs // 2 - 1):
        first = 2 * n * pair
        residuals(first + pair, *odd)
        gradients(first, *even)
        residuals(first + 2 * pair, *even)
        gradients(first + pair, *odd)

    last = (pairs - 1) * pair
    residuals(last, *odd)
    gradients(last - pair, *even)
    gradients(last, *odd)

    for t, gradient in enumerate((user_gradient, item_gradient, day_gradient)):
        start, slots = sizes.slot_starts[t], sizes.slots[t]
        values = (0.5 * loss_scale * gradient[...]).astype(bf16)
        placed = jnp.dot(places[t][...], values, preferred_element_type=f32)
        for s in range(owners):
            rows = placed[s * slots : (s + 1) * slots]
            if t == 2:
                note = iota(rows.shape, 0) == sizes.note_row
                rows = jnp.where(note, note_ref[s : s + 1, :], rows)
            out = (own_ref, other_ref)[s % 2]
            first = (s // 2) * sizes.slot_rows + start
            out[first : first + slots, :] = rows.astype(bf16)


def hold_kernel(arrived_ref, note_ref, out_ref):
    out_ref[...] = arrived_ref[...]


def merge_kernel(sizes, own_ref, crossed_ref, *outs):
    rows = sizes.slot_rows
    for n, out in enumerate(outs):
        start = (n + 1) * rows
        out[:rows, :] = own_ref[start : start + rows, :]
        out[rows:, :] = crossed_ref[start : start + rows, :]


def add_messages(sizes, totals, messages):
    day_start = sizes.slot_starts[2]
    for ref in messages:
        notes = ref[day_start : day_start + sizes.slots[2], :].astype(f32)
        rows = notes[sizes.note_row : sizes.note_row + 1, : sizes.slot_rows].astype(jnp.int32)
        for t in range(3):
            start, slots = sizes.slot_starts[t], sizes.slots[t]
            shape = (sizes.row_counts[t], sizes.slot_rows)
            slot = iota(shape, 1)
            mine = (slot >= start) & (slot < start + slots)
            selector = onehot((iota(shape, 0) == rows) & mine)
            totals[t] = totals[t] + jnp.dot(selector, ref[...], preferred_element_type=f32)
    return totals


def early_sum_kernel(sizes, own_ref, crossed_ref, arrived_ref, *outs):
    rows = sizes.slot_rows
    messages = [own_ref.at[:rows], crossed_ref.at[:rows]]
    messages += [arrived_ref.at[:rows], arrived_ref.at[rows:]]
    for out, total in zip(outs, add_messages(sizes, [0.0, 0.0, 0.0], messages)):
        out[...] = total


def sum_kernel(sizes, *refs):
    holders, columns, rows = sizes.holders, sizes.columns, sizes.slot_rows
    early, arrived, outs = refs[:3], refs[3:-holders], refs[-holders:]
    messages = [ref.at[:rows] for ref in arrived] + [ref.at[rows:] for ref in arrived]
    totals = add_messages(sizes, [ref[...] for ref in early], messages)
    for t in range(3):
        if t < 2:
            turned = totals[t].T.astype(bf16)
            for j in range(holders):
                outs[j][t * columns : (t + 1) * columns, :] = turned[
                    j * columns : (j + 1) * columns
                ]
        else:
            for j in range(holders):
                outs[j][2 * columns :, :] = pack_days(
                    sizes, totals[t][:, j * columns : (j + 1) * columns]
                ).astype(bf16)


def adam_kernel(sizes, *refs):
    holders, columns = sizes.holders, sizes.columns
    pieces = refs[:holders]
    states = refs[holders : holders + 9]
    outs = refs[holders + 9 :]
    total = pieces[0][...].astype(f32)
    for ref in pieces[1:]:
        total = total + ref[...].astype(f32)
    for t in range(3):
        if t < 2:
            gradient = total[t * columns : (t + 1) * columns]
        else:
            gradient = unpack_days(sizes, total[2 * columns :])
        factor, first, second = states[3 * t : 3 * t + 3]
        new_factor, new_first, new_second = outs[3 * t : 3 * t + 3]
        first_value = beta_one * first[...] + (1.0 - beta_one) * gradient
        second_value = beta_two * second[...] + (1.0 - beta_two) * gradient * gradient
        change = (
            learn_rate
            * (first_value / bias_one)
            / (jnp.sqrt(second_value / bias_two) + epsilon)
        )
        new_factor[...] = factor[...] - change
        new_first[...] = first_value
        new_second[...] = second_value


def swap(array, axis, size, bits):
    return lax.ppermute(array, axis, [(i, i ^ bits) for i in range(size)])


def local(
    users_list,
    items_list,
    days_list,
    status,
    user_factor,
    user_first,
    user_second,
    item_factor,
    item_first,
    item_second,
    day_factor,
    day_first,
    day_second,
):
    owners = lax.axis_size("dp")
    holders = lax.axis_size("mp")
    row_counts = (user_factor.shape[0], item_factor.shape[0], day_factor.shape[0])
    list_counts = (users_list.shape[1], items_list.shape[1], days_list.shape[1])
    sizes = Sizes(owners, holders, user_factor.shape[1], row_counts, list_counts)
    shape = jax.ShapeDtypeStruct
    small = pltpu.CompilerParams(vmem_limit_bytes=SMALL_VMEM)

    hbm = pl.BlockSpec(memory_space=pltpu.HBM)
    in_hbm = lambda a: pltpu.with_memory_space_constraint(a, pltpu.HBM)
    tables_in = (user_factor.T, item_factor.T, day_factor)
    piece = pl.pallas_call(
        functools.partial(pack_kernel, sizes),
        out_shape=shape((sizes.piece_rows, LANES), bf16),
        in_specs=[hbm] * 3,
        scratch_shapes=[pltpu.VMEM(a.shape, f32) for a in tables_in]
        + [pltpu.SemaphoreType.DMA((3,))],
        compiler_params=small,
        name="pack",
    )(*[in_hbm(a) for a in tables_in])
    distances = exchange_order(holders)
    pieces = [swap(piece, "mp", holders, bits) for bits in distances] + [piece]

    table = pl.pallas_call(
        functools.partial(table_kernel, sizes),
        out_shape=shape((sizes.table_rows, LANES), bf16),
        compiler_params=small,
        name="table",
    )(*pieces)
    arrived = {bits: swap(table, "dp", owners, bits) for bits in range(2, owners, 2)}
    own_crossed = swap(table, "dp", owners, 1)
    picks_places_notes = pl.pallas_call(
        functools.partial(slot_kernel, sizes),
        out_shape=tuple(
            [shape((owners * row_counts[t], list_counts[t]), bf16) for t in range(3)]
            + [shape((owners * sizes.slots[t], list_counts[t]), bf16) for t in range(3)]
            + [shape((owners, sizes.rank), f32), shape(status.shape[1:], jnp.int32)]
        ),
        in_specs=[pl.BlockSpec(memory_space=pltpu.SMEM)]
        + [hbm] * 3
        + [pl.BlockSpec(memory_space=pl.ANY), hbm],
        scratch_shapes=[pltpu.VMEM((1, count), jnp.int32) for count in list_counts]
        + [pltpu.SemaphoreType.DMA((3,)), pltpu.SemaphoreType.DMA((1,))],
        compiler_params=small,
        name="slots",
    )(
        lax.axis_index("dp").astype(jnp.int32).reshape(1),
        *[in_hbm(a) for a in (users_list, items_list, days_list)],
        table,
        in_hbm(status),
    )

    hold = pl.pallas_call(
        hold_kernel,
        out_shape=shape(table.shape, bf16),
        compiler_params=small,
        name="hold",
    )
    arrived = {bits: hold(a, picks_places_notes[6]) for bits, a in arrived.items()}
    tables = {0: table, 1: own_crossed}
    for bits in table_order(owners)[1:]:
        tables[bits] = arrived[bits]
        tables[bits + 1] = swap(arrived[bits], "dp", owners, 1)
    last = tables.pop(HOLD + 1)
    early = pl.pallas_call(
        functools.partial(early_pick_kernel, sizes, tuple(tables)),
        out_shape=(
            shape((sizes.rank, list_counts[0]), f32),
            shape((sizes.rank, list_counts[1]), f32),
            shape((list_counts[2], sizes.rank), f32),
        ),
        compiler_params=small,
        name="early_picks",
    )(*tables.values(), *picks_places_notes[:3])
    inputs = [last, *early, *picks_places_notes]
    users, items, days = list_counts
    half = shape((owners // 2 * sizes.slot_rows, sizes.rank), bf16)
    own, other = pl.pallas_call(
        functools.partial(block_kernel, sizes),
        out_shape=(half, half),
        in_specs=[pl.BlockSpec(memory_space=pltpu.VMEM)] * len(inputs),
        scratch_shapes=[
            pltpu.VMEM((users, sizes.rank), f32),
            pltpu.VMEM((users, sizes.rank), bf16),
            pltpu.VMEM((items, sizes.rank), bf16),
            pltpu.VMEM((sizes.rank, items), bf16),
            pltpu.VMEM((days, sizes.rank), f32),
            pltpu.VMEM((users, sizes.rank), f32),
            pltpu.VMEM((items, sizes.rank), f32),
            pltpu.VMEM((days, sizes.rank), f32),
            pltpu.VMEM((2 * users, sizes.rank), bf16),
            pltpu.VMEM((2 * users, sizes.rank), bf16),
            pltpu.VMEM((2 * users, items), bf16),
            pltpu.VMEM((2 * users, items), bf16),
        ],
        compiler_params=pltpu.CompilerParams(vmem_limit_bytes=BLOCK_VMEM),
        name="block_gradients",
    )(*inputs)
    crossed = swap(other, "dp", owners, 1)
    message = shape((2 * sizes.slot_rows, sizes.rank), bf16)
    merged = pl.pallas_call(
        functools.partial(merge_kernel, sizes),
        out_shape=tuple([message] * (owners // 2 - 1)),
        compiler_params=small,
        name="merge",
    )(own, crossed)
    returned = [own, crossed]
    returned += [
        swap(merged[bits // 2 - 1], "dp", owners, bits) for bits in range(owners - 2, 0, -2)
    ]

    early = pl.pallas_call(
        functools.partial(early_sum_kernel, sizes),
        out_shape=tuple(shape((rows, sizes.rank), f32) for rows in row_counts),
        compiler_params=small,
        name="early_sums",
    )(*returned[:3])
    totals = pl.pallas_call(
        functools.partial(sum_kernel, sizes),
        out_shape=tuple([shape(piece.shape, bf16)] * holders),
        compiler_params=small,
        name="row_sums",
    )(*early, *returned[3:])
    column_totals = [totals[0]] + [
        swap(totals[bits], "mp", holders, bits) for bits in range(holders - 1, 0, -1)
    ]

    states = (
        user_factor.T,
        user_first.T,
        user_second.T,
        item_factor.T,
        item_first.T,
        item_second.T,
        day_factor,
        day_first,
        day_second,
    )
    updated = pl.pallas_call(
        functools.partial(adam_kernel, sizes),
        out_shape=tuple(shape(a.shape, a.dtype) for a in states),
        compiler_params=small,
        name="adam",
    )(*column_totals, *states)
    return tuple(a.T for a in updated[:6]) + tuple(updated[6:])


def solution(mesh):
    block = P(("dp", "mp"), None)
    piece = P("dp", "mp")
    return jax.shard_map(
        local,
        mesh=mesh,
        in_specs=(block, block, block, P(("dp", "mp"), None, None, None)) + (piece,) * 9,
        out_specs=(piece,) * 9,
        check_vma=False,
    )
```
